128 devices in a mesh: lat: 16 (over y, x_lo, core), ch: 8 (over z, x_hi).
Axes of the slice: x: 4 (x_hi: 2, x_lo: 2; x = x_hi * 2 + x_lo), y: 4, z: 4, core: 2. Of those that a mesh axis runs over, the one named last changes fastest.
Arguments:
- inputs: float32 [384, 80, 180], P('ch', 'lat'), may hold values from -44 to 44
- cotangent: float32 [384, 80, 180], P('ch', 'lat'), may hold values from -1.5 to 1.5
- first_gain: float32 [4, 384], P(None, 'ch'), may hold values from 0.5 to 1.5
- first_shift: float32 [4, 384], P(None, 'ch'), may hold values from -3 to 3
- filter_inner: float32 [4, 2, 8, 48, 48], P(None, None, 'ch'), may hold values from -0.625 to 0.625
- filter_inner_bias: float32 [4, 2, 8, 48], P(None, None, 'ch'), may hold values from -3 to 3
- filter_outer: float32 [4, 2, 8, 48, 48], P(None, None, 'ch'), may hold values from -0.625 to 0.625
- filter_outer_bias: float32 [4, 2, 8, 48], P(None, None, 'ch'), may hold values from -3 to 3
- second_gain: float32 [4, 384], P(None, 'ch'), may hold values from 0.5 to 1.5
- second_shift: float32 [4, 384], P(None, 'ch'), may hold values from -3 to 3
- up_weight: bfloat16 [4, 384, 1536], P(None, None, 'ch'), may hold values from -0.3125 to 0.3125
- up_bias: float32 [4, 1536], P(None, 'ch'), may hold values from -3 to 3
- down_weight: bfloat16 [4, 1536, 384], P(None, 'ch'), may hold values from -0.15625 to 0.15625
- down_bias: float32 [4, 384], P(None, 'ch'), may hold values from -3 to 3
- kept_lat: int32 [60], replicated, may hold values from 0 to 79, as said below
- kept_lon: int32 [64], replicated, may hold values from 0 to 90, as said below
Outputs:
- outputs: float32 [384, 80, 180], P('ch', 'lat')
- input_grad: float32 [384, 80, 180], P('ch', 'lat')
- first_gain_grad: float32 [4, 384], P(None, 'ch')
- first_shift_grad: float32 [4, 384], P(None, 'ch')
- inner_weight_grad: float32 [4, 2, 8, 48, 48], P(None, None, 'ch')
- inner_bias_grad: float32 [4, 2, 8, 48], P(None, None, 'ch')
- outer_weight_grad: float32 [4, 2, 8, 48, 48], P(None, None, 'ch')
- outer_bias_grad: float32 [4, 2, 8, 48], P(None, None, 'ch')
- second_gain_grad: float32 [4, 384], P(None, 'ch')
- second_shift_grad: float32 [4, 384], P(None, 'ch')
- up_weight_grad: float32 [4, 384, 1536], P(None, None, 'ch')
- up_bias_grad: float32 [4, 1536], P(None, 'ch')
- down_weight_grad: float32 [4, 1536, 384], P(None, 'ch')
- down_bias_grad: float32 [4, 384], P(None, 'ch')
The draws below stay inside these ranges and needn't reach their ends.
Inputs may be any that keep to these rules, and one draw needn't show every extreme that they name: `kept_lat`: 60 distinct latitude mode numbers, among them 0 and 79. `kept_lon`: 64 distinct longitude mode numbers, among them 0 and 90.
All inputs are finite; a program needn't handle non-finite values.
Results may differ from the reference program's by a relative error of at most 0.025.
Values may be sent and summed in bfloat16 or wider, within the bound.
A program may use at most 128 MiB of HBM per device.

```python
import math
import jax
import jax.numpy as jnp
from jax import lax

D = 384
BLOCKS = 8
BLOCK = 48
FF = 1536
LON = 180
KEEP_LON = 64
LAYERS = 4
LAT = 80
KEEP_LAT = 60
N_CH = 8


def draw_inputs(key, part):
    key = jax.random.fold_in(key, 5)
    base_key, chan_key = jax.random.split(key, 2)
    base_draw = jax.random.truncated_normal(base_key, -4.0, 4.0, (D, LAT, LON), jnp.float32)
    chan_ramp = jnp.arange(D, dtype=jnp.float32) / D
    chan_scale = 0.2 * jnp.exp(chan_ramp * math.log(3.0) + jax.random.uniform(chan_key, (D,), jnp.float32) * math.log(5.0))
    lat_ramp = jnp.exp((jnp.arange(LAT, dtype=jnp.float32) / LAT - 0.5) * math.log(3.0))
    values = base_draw * chan_scale[:, None, None] * lat_ramp[None, :, None]
    return values


def pick_modes(key, mode_count, mode_limit):
    order_key, shuffle_key = jax.random.split(key)
    inner_modes = jax.random.permutation(order_key, mode_limit - 2)[:mode_count - 2].astype(jnp.int32) + 1
    chosen = jnp.concatenate([jnp.zeros((1,), jnp.int32), inner_modes, jnp.full((1,), mode_limit - 1, jnp.int32)])
    return jax.random.permutation(shuffle_key, chosen).astype(jnp.int32)


def draw_kept_lat(key, part):
    key = jax.random.fold_in(key, 11)
    return pick_modes(key, KEEP_LAT, LAT)


def draw_kept_lon(key, part):
    key = jax.random.fold_in(key, 13)
    return pick_modes(key, KEEP_LON, LON // 2 + 1)


def block_scale(stream_key, dims, cuts, low, largest):
    loudness = 1.0
    for axis_at, blocks in cuts:
        draws = jax.random.uniform(jax.random.fold_in(jax.random.fold_in(stream_key, 6), axis_at), (blocks,), jnp.float32, low / len(cuts), largest / len(cuts))
        loudness = loudness * jnp.repeat(jnp.exp(draws), dims[axis_at] // blocks).reshape((-1,) + (1,) * (len(dims) - 1 - axis_at))
    return loudness


def gaussian(stream_key, shape, deviation, limit, shards=(), kind=jnp.bfloat16):
    result = deviation * jax.random.normal(stream_key, shape, jnp.float32)
    if shards:
        result = result * block_scale(stream_key, shape, shards, -0.22, 0.18)
    return jnp.clip(result, -limit, limit).astype(kind)


def setup_inputs(seed: int = 0) -> dict:
    streams_of = jax.random.split(jax.random.key(seed), 17)
    return {
        "inputs": draw_inputs(jax.random.fold_in(streams_of[16], 71), 0),
        "cotangent": gaussian(streams_of[1], (D, LAT, LON), 0.25, 1.5, ((0, 8), (1, 16)), jnp.float32),
        "first_gain": jnp.clip(1.0 + 0.1 * jax.random.normal(streams_of[2], (LAYERS, D), jnp.float32), 0.5, 1.5),
        "first_shift": gaussian(streams_of[3], (LAYERS, D), 0.5, 3.0, ((1, 8),), jnp.float32),
        "filter_inner": gaussian(streams_of[4], (LAYERS, 2, BLOCKS, BLOCK, BLOCK), (2 * BLOCK) ** -0.5, 0.625, ((2, 8),), jnp.float32),
        "filter_inner_bias": gaussian(streams_of[5], (LAYERS, 2, BLOCKS, BLOCK), 0.5, 3.0, ((2, 8),), jnp.float32),
        "filter_outer": gaussian(streams_of[6], (LAYERS, 2, BLOCKS, BLOCK, BLOCK), (2 * BLOCK) ** -0.5, 0.625, ((2, 8),), jnp.float32),
        "filter_outer_bias": gaussian(streams_of[7], (LAYERS, 2, BLOCKS, BLOCK), 0.5, 3.0, ((2, 8),), jnp.float32),
        "second_gain": jnp.clip(1.0 + 0.1 * jax.random.normal(streams_of[8], (LAYERS, D), jnp.float32), 0.5, 1.5),
        "second_shift": gaussian(streams_of[9], (LAYERS, D), 0.5, 3.0, ((1, 8),), jnp.float32),
        "up_weight": gaussian(streams_of[10], (LAYERS, D, FF), D ** -0.5, 0.3125, ((2, 8),)),
        "up_bias": gaussian(streams_of[11], (LAYERS, FF), 0.5, 3.0, ((1, 8),), jnp.float32),
        "down_weight": gaussian(streams_of[12], (LAYERS, FF, D), FF ** -0.5, 0.15625, ((1, 8),)),
        "down_bias": gaussian(streams_of[13], (LAYERS, D), 0.5, 3.0, ((1, 8),), jnp.float32),
        "kept_lat": draw_kept_lat(jax.random.fold_in(streams_of[16], 71), 0),
        "kept_lon": draw_kept_lon(jax.random.fold_in(streams_of[16], 71), 0),
    }


shrink_level = 0.01
norm_eps = 1e-05
highest = lax.Precision.HIGHEST

def gelu_exact(values):
    return 0.5 * values * (1.0 + lax.erf(values * 0.7071067811865476))

def gelu_slope(values):
    return 0.5 * (1.0 + lax.erf(values * 0.7071067811865476)) + values * jnp.exp(-0.5 * values * values) * 0.3989422804014327

def soft_shrink(values):
    return values - shrink_level * jnp.tanh(values / shrink_level)

def complex_mix(real_part, imag_part, weight, bias_pair):
    real_out = jnp.einsum('bimk,bij->bjmk', real_part, weight[0], precision=highest) - jnp.einsum('bimk,bij->bjmk', imag_part, weight[1], precision=highest)
    imag_out = jnp.einsum('bimk,bij->bjmk', imag_part, weight[0], precision=highest) + jnp.einsum('bimk,bij->bjmk', real_part, weight[1], precision=highest)
    return (real_out + bias_pair[0][:, :, None, None], imag_out + bias_pair[1][:, :, None, None])

def block_mlp(real_part, imag_part, weight_in, bias_in, weight_out, bias_out):
    hidden_re, hidden_im = complex_mix(real_part, imag_part, weight_in, bias_in)
    out_re, out_im = complex_mix(gelu_exact(hidden_re), gelu_exact(hidden_im), weight_out, bias_out)
    return (soft_shrink(out_re), soft_shrink(out_im))

def norm_parts(values):
    mean_value = lax.optimization_barrier(jnp.mean(values, axis=0))
    spread = lax.optimization_barrier(jnp.mean(values * values, axis=0)) - mean_value * mean_value
    rstd_value = lax.rsqrt(spread + norm_eps)
    return ((values - mean_value) * rstd_value, rstd_value)

def spectral(mixed_field, weight_in, bias_in, weight_out, bias_out, kept_lat, kept_lon):
    spectrum = jnp.fft.rfft2(mixed_field, axes=(1, 2), norm='ortho')
    picked = spectrum[:, kept_lat, :][:, :, kept_lon]
    block_shape = (BLOCKS, BLOCK, KEEP_LAT, KEEP_LON)
    out_re, out_im = block_mlp(jnp.real(picked).reshape(block_shape), jnp.imag(picked).reshape(block_shape), weight_in, bias_in, weight_out, bias_out)
    values = lax.complex(out_re.reshape(D, KEEP_LAT, KEEP_LON), out_im.reshape(D, KEEP_LAT, KEEP_LON))
    placed = jnp.zeros((D, LAT, LON // 2 + 1), values.dtype).at[:, kept_lat[:, None], kept_lon[None, :]].set(values)
    return jnp.fft.irfft2(placed, s=(LAT, LON), axes=(1, 2), norm='ortho')

def grouped(left, right):
    group_width = left.shape[1] // N_CH
    running = jnp.zeros((left.shape[0], right.shape[1]), jnp.float32)
    for group_index in range(N_CH):
        lower = group_index * group_width
        part_sum = jnp.dot(left[:, lower:lower + group_width], right[lower:lower + group_width], preferred_element_type=jnp.float32)
        running = running + lax.optimization_barrier(part_sum.astype(jnp.bfloat16)).astype(jnp.float32)
    return running

def layer_parts(current, params, kept_lat, kept_lon):
    gain_one, shift_one, weight_in, bias_in, weight_out, bias_out, gain_two, shift_two, up_layer, up_shift, down_layer, down_shift = params
    normed_one, rstd_one = norm_parts(current)
    mixed_one = normed_one * gain_one[:, None, None] + shift_one[:, None, None]

    def filter_fn(mixed_field, first_w, first_b, second_w, second_b):
        return spectral(mixed_field, first_w, first_b, second_w, second_b, kept_lat, kept_lon)
    back_field, filter_vjp = jax.vjp(filter_fn, mixed_one, weight_in, bias_in, weight_out, bias_out)
    inner_field = current + mixed_one + back_field
    normed_two, rstd_two = norm_parts(inner_field)
    lifted = (normed_two * gain_two[:, None, None] + shift_two[:, None, None]).astype(jnp.bfloat16).reshape(D, LAT * LON)
    pre_act = jnp.dot(up_layer.T, lifted, preferred_element_type=jnp.float32) + up_shift[:, None]
    hidden_act = gelu_exact(pre_act).astype(jnp.bfloat16)
    summed = grouped(down_layer.T, hidden_act)
    outputs_next = inner_field + summed.reshape(D, LAT, LON) + down_shift[:, None, None]
    return (outputs_next, (normed_one, rstd_one, filter_vjp, normed_two, rstd_two, lifted, pre_act, hidden_act))

def reference(inputs, cotangent, first_gain, first_shift, filter_inner, filter_inner_bias, filter_outer, filter_outer_bias, second_gain, second_shift, up_weight, up_bias, down_weight, down_bias, kept_lat, kept_lon):
    param_list = (first_gain, first_shift, filter_inner, filter_inner_bias, filter_outer, filter_outer_bias, second_gain, second_shift, up_weight, up_bias, down_weight, down_bias)
    stored = []
    current = inputs
    for layer_index in range(LAYERS):
        params = tuple((item[layer_index] for item in param_list))
        current, layer_saved = layer_parts(current, params, kept_lat, kept_lon)
        stored.append(layer_saved)
    outputs_field = current
    grad_now = cotangent
    collected = []
    for layer_index in reversed(range(LAYERS)):
        params = tuple((item[layer_index] for item in param_list))
        gain_one = params[0]
        gain_two = params[6]
        up_layer = params[8]
        down_layer = params[10]
        normed_one, rstd_one, filter_vjp, normed_two, rstd_two, lifted, pre_act, hidden_act = stored[layer_index]
        grad_flat = grad_now.reshape(D, LAT * LON)
        cot_round = grad_flat.astype(jnp.bfloat16)
        down_shift_grad = lax.optimization_barrier(jnp.sum(grad_flat, axis=1))
        hidden_grad = jnp.dot(down_layer, cot_round, preferred_element_type=jnp.float32)
        down_grad = jnp.dot(hidden_act, cot_round.T, preferred_element_type=jnp.float32)
        pre_grad = hidden_grad * gelu_slope(pre_act)
        pre_round = pre_grad.astype(jnp.bfloat16)
        up_shift_grad = lax.optimization_barrier(jnp.sum(pre_grad, axis=1))
        up_grad = jnp.dot(lifted, pre_round.T, preferred_element_type=jnp.float32)
        lift_grad = grouped(up_layer, pre_round).reshape(D, LAT, LON)
        gain_two_grad = lax.optimization_barrier(jnp.sum(lift_grad * normed_two, axis=(1, 2)))
        shift_two_grad = lax.optimization_barrier(jnp.sum(lift_grad, axis=(1, 2)))
        scaled_two = lift_grad * gain_two[:, None, None]
        inner_grad = grad_now + rstd_two * (scaled_two - lax.optimization_barrier(jnp.mean(scaled_two, axis=0)) - normed_two * lax.optimization_barrier(jnp.mean(scaled_two * normed_two, axis=0)))
        spec_grad, first_w_grad, first_b_grad, second_w_grad, second_b_grad = filter_vjp(inner_grad)
        mixed_grad = inner_grad + spec_grad
        gain_one_grad = lax.optimization_barrier(jnp.sum(mixed_grad * normed_one, axis=(1, 2)))
        shift_one_grad = lax.optimization_barrier(jnp.sum(mixed_grad, axis=(1, 2)))
        scaled_one = mixed_grad * gain_one[:, None, None]
        grad_now = inner_grad + rstd_one * (scaled_one - lax.optimization_barrier(jnp.mean(scaled_one, axis=0)) - normed_one * lax.optimization_barrier(jnp.mean(scaled_one * normed_one, axis=0)))
        collected.append((gain_one_grad, shift_one_grad, first_w_grad, first_b_grad, second_w_grad, second_b_grad, gain_two_grad, shift_two_grad, up_grad, up_shift_grad, down_grad, down_shift_grad))
    collected = collected[::-1]
    stacked = [jnp.stack([terms[position] for terms in collected]) for position in range(12)]
    return (outputs_field, grad_now, stacked[0], stacked[1], stacked[2], stacked[3], stacked[4], stacked[5], stacked[6], stacked[7], stacked[8], stacked[9], stacked[10], stacked[11])
```

```python
import functools
import math

import jax
import jax.numpy as jnp
from jax import lax
from jax.experimental import pallas as pl
from jax.experimental.pallas import tpu as pltpu
from jax.sharding import PartitionSpec as P

shrink_level = 0.01
norm_eps = 1e-05
highest = lax.Precision.HIGHEST
MESH = pl.DeviceIdType.MESH


def gelu_exact(values):
    return 0.5 * values * (1.0 + lax.erf(values * 0.7071067811865476))


def gelu_slope(values):
    return (
        0.5 * (1.0 + lax.erf(values * 0.7071067811865476))
        + values * jnp.exp(-0.5 * values * values) * 0.3989422804014327
    )


def soft_shrink(values):
    return values - shrink_level * jnp.tanh(values / shrink_level)


def push_kernel(axis, n, scatters, *refs):
    count = len(scatters)
    sources, targets = refs[:count], refs[count : 2 * count]
    send_sem, recv_sem, own_sem = refs[2 * count :]
    me = lax.axis_index(axis)
    barrier = pltpu.get_barrier_semaphore()
    for step in range(1, n):
        pl.semaphore_signal(
            barrier, inc=1, device_id={axis: lax.rem(me + step, n)}, device_id_type=MESH
        )
    own = []
    for at, scatter in enumerate(scatters):
        block = sources[at].at[me] if scatter else sources[at]
        copy = pltpu.make_async_copy(block, targets[at].at[me], own_sem.at[at])
        copy.start()
        own.append(copy)
    pl.semaphore_wait(barrier, n - 1)
    copies = []
    for step in range(1, n):
        peer = lax.rem(me + step, n)
        for at, scatter in enumerate(scatters):
            block = sources[at].at[peer] if scatter else sources[at]
            copy = pltpu.make_async_remote_copy(
                src_ref=block,
                dst_ref=targets[at].at[me],
                send_sem=send_sem.at[at, step],
                recv_sem=recv_sem.at[at, step],
                device_id={axis: peer},
                device_id_type=MESH,
            )
            copy.start()
            copies.append(copy)
    for copy in own + copies:
        copy.wait()


def push(axis, ident, arrays, scatters):
    n = lax.axis_size(axis)
    shapes = [
        jax.ShapeDtypeStruct(a.shape if s else (n,) + a.shape, a.dtype)
        for a, s in zip(arrays, scatters)
    ]
    count = len(arrays)
    return pl.pallas_call(
        functools.partial(push_kernel, axis, n, scatters),
        out_shape=shapes,
        in_specs=[pl.BlockSpec(memory_space=pltpu.VMEM)] * count,
        out_specs=[pl.BlockSpec(memory_space=pltpu.VMEM)] * count,
        scratch_shapes=[
            pltpu.SemaphoreType.DMA((count, n)),
            pltpu.SemaphoreType.DMA((count, n)),
            pltpu.SemaphoreType.DMA((count,)),
        ],
        compiler_params=pltpu.CompilerParams(collective_id=ident, has_side_effects=True),
    )(*arrays)


def block_mlp(values, weight_in, bias_in, weight_out, bias_out):
    def mix(part, weight, bias_pair):
        re, im = part[:, 0], part[:, 1]
        out_re = jnp.einsum("kim,ij->kjm", re, weight[0], precision=highest) - jnp.einsum(
            "kim,ij->kjm", im, weight[1], precision=highest
        )
        out_im = jnp.einsum("kim,ij->kjm", im, weight[0], precision=highest) + jnp.einsum(
            "kim,ij->kjm", re, weight[1], precision=highest
        )
        return jnp.stack(
            [out_re + bias_pair[0][:, None], out_im + bias_pair[1][:, None]], axis=1
        )

    inner = gelu_exact(mix(values, weight_in, bias_in))
    return soft_shrink(mix(inner, weight_out, bias_out))


def spectral_local(spectrum, weight_in, bias_in, weight_out, bias_out, lat_matrix):
    groups, pairs, _ = spectrum.shape
    modes = lat_matrix.shape[1]
    rows = lat_matrix.shape[4]
    paired = spectrum.reshape(groups, pairs // 2, 2, -1, rows)
    mode = jnp.einsum("xmsyr,skycr->kxcm", lat_matrix, paired, precision=highest)
    out = block_mlp(mode, weight_in[:, 0], bias_in[:, 0], weight_out[:, 0], bias_out[:, 0])
    back = jnp.einsum("xmsyr,kxcm->skycr", lat_matrix, out, precision=highest)
    return back.reshape(spectrum.shape)


def lat_matrix_of(cos_lat, sin_lat, groups):
    modes, cells = cos_lat.shape
    rows = cells // groups
    both = jnp.stack(
        [jnp.stack([cos_lat, sin_lat], axis=1), jnp.stack([-sin_lat, cos_lat], axis=1)], axis=0
    )
    return jnp.transpose(both.reshape(2, modes, 2, groups, rows), (0, 1, 3, 2, 4))


def block_sums(values):
    return jnp.stack([jnp.sum(values, axis=0), jnp.sum(values * values, axis=0)])


def to_modes(values, table, groups):
    moved = jnp.einsum("crw,wp->pcr", values, table, precision=highest)
    pairs = table.shape[1] // groups
    return push("lat", 0, [moved.reshape(groups, pairs, -1)], [True])[0]


def to_rows(values, table, shape):
    moved = push("lat", 0, [values], [True])[0]
    chan_count, row_count, _ = shape
    return jnp.einsum(
        "pcr,pw->crw", moved.reshape(-1, chan_count, row_count), table, precision=highest
    )


def lat_tables(kept_lat, lat_cells):
    cell_index = jnp.arange(lat_cells, dtype=jnp.int32)
    phase_index = kept_lat[:, None] * cell_index[None, :] % lat_cells
    angles = phase_index.astype(jnp.float32) * (2.0 * math.pi / lat_cells)
    norm_scale = 1.0 / math.sqrt(lat_cells)
    return (jnp.cos(angles) * norm_scale, jnp.sin(angles) * norm_scale)


def lon_tables(kept_lon, lon_cells):
    cell_index = jnp.arange(lon_cells, dtype=jnp.int32)
    phase_index = kept_lon[:, None] * cell_index[None, :] % lon_cells
    angles = phase_index.astype(jnp.float32) * (2.0 * math.pi / lon_cells)
    norm_scale = 1.0 / math.sqrt(lon_cells)
    mode_weight = jnp.where((kept_lon == 0) | (2 * kept_lon == lon_cells), 1.0, 2.0).astype(
        jnp.float32
    )[:, None]
    forward_table = (
        jnp.stack([jnp.cos(angles), -jnp.sin(angles)], axis=1).reshape(-1, lon_cells).T * norm_scale
    )
    inverse_table = (
        jnp.stack([jnp.cos(angles) * mode_weight, -jnp.sin(angles) * mode_weight], axis=1).reshape(
            -1, lon_cells
        )
        * norm_scale
    )
    return (forward_table, inverse_table)


def body(
    inputs,
    cotangent,
    first_gain,
    first_shift,
    filter_inner,
    filter_inner_bias,
    filter_outer,
    filter_outer_bias,
    second_gain,
    second_shift,
    up_weight,
    up_bias,
    down_weight,
    down_bias,
    kept_lat,
    kept_lon,
):
    shape = inputs.shape
    chan_count, row_count, lon_cells = shape
    cells = row_count * lon_cells
    groups = lax.axis_size("lat")
    blocks = lax.axis_size("ch")
    lat_cells = row_count * groups
    channel_total = chan_count * blocks
    layer_count = first_gain.shape[0]
    lon_forward, lon_inverse = lon_tables(kept_lon, lon_cells)
    cos_lat, sin_lat = lat_tables(kept_lat, lat_cells)
    lat_matrix = lat_matrix_of(cos_lat, sin_lat, groups)
    gathered_gain = push(
        "ch", 1, [jnp.stack([second_gain, second_shift])], [False]
    )[0]
    full_gain = gathered_gain[:, 0].transpose(1, 0, 2)
    full_shift = gathered_gain[:, 1].transpose(1, 0, 2)

    current = inputs
    saved_layers = []
    for layer in range(layer_count):
        sums = push("ch", 2, [block_sums(current).reshape(2, cells)], [False])[0]
        sums = jnp.sum(sums, axis=0).reshape(2, row_count, lon_cells) / channel_total
        mean_one = sums[0]
        rstd_one = lax.rsqrt(sums[1] - mean_one * mean_one + norm_eps)
        normed_one = (current - mean_one) * rstd_one
        mixed_one = (
            normed_one * first_gain[layer][:, None, None] + first_shift[layer][:, None, None]
        )
        spectrum = to_modes(mixed_one, lon_forward, groups)
        filtered = spectral_local(
            spectrum,
            filter_inner[layer],
            filter_inner_bias[layer],
            filter_outer[layer],
            filter_outer_bias[layer],
            lat_matrix,
        )
        inner_field = current + mixed_one + to_rows(filtered, lon_inverse, shape)
        flat = inner_field.reshape(chan_count, cells)
        block_mean = jnp.mean(flat, axis=0)
        centered = flat - block_mean
        round_part = centered.astype(jnp.bfloat16)
        own_sums = jnp.stack([block_mean, jnp.sum(centered * centered, axis=0)])
        parts, sums = push("ch", 3, [round_part, own_sums], [False, False])
        means = sums[:, 0]
        mean_two = jnp.mean(means, axis=0)
        offsets = means - mean_two
        spread = jnp.mean(offsets * offsets, axis=0) + jnp.sum(sums[:, 1], axis=0) / channel_total
        rstd_two = lax.rsqrt(spread + norm_eps)
        full_normed = (parts.astype(jnp.float32) + offsets[:, None, :]) * rstd_two
        normed_two = (flat - mean_two) * rstd_two
        lifted = (
            (full_normed * full_gain[layer][:, :, None] + full_shift[layer][:, :, None])
            .astype(jnp.bfloat16)
            .reshape(channel_total, cells)
        )
        pre_act = (
            jnp.einsum("cn,cf->fn", lifted, up_weight[layer], preferred_element_type=jnp.float32)
            + up_bias[layer][:, None]
        )
        hidden_act = gelu_exact(pre_act).astype(jnp.bfloat16)
        partial = jnp.einsum(
            "fn,fc->cn", hidden_act, down_weight[layer], preferred_element_type=jnp.float32
        ).astype(jnp.bfloat16)
        pieces = push("ch", 4, [partial.reshape(blocks, chan_count, cells)], [True])[0]
        summed = jnp.sum(pieces.astype(jnp.float32), axis=0)
        current = (flat + summed + down_bias[layer][:, None]).reshape(shape)
        saved_layers.append(
            (
                normed_one,
                rstd_one,
                spectrum,
                normed_two,
                rstd_two,
                full_normed,
                lifted,
                pre_act,
                hidden_act,
            )
        )
    grad_now = cotangent
    collected = []
    for layer in reversed(range(layer_count)):
        (
            normed_one,
            rstd_one,
            spectrum,
            normed_two,
            rstd_two,
            full_normed,
            lifted,
            pre_act,
            hidden_act,
        ) = saved_layers[layer]
        flat_grad = grad_now.reshape(chan_count, cells)
        down_shift_grad = jnp.sum(flat_grad, axis=1)
        full_cot = push("ch", 5, [flat_grad.astype(jnp.bfloat16)], [False])[0]
        full_cot = full_cot.reshape(channel_total, cells)
        hidden_grad = jnp.einsum(
            "cn,fc->fn", full_cot, down_weight[layer], preferred_element_type=jnp.float32
        )
        down_grad = jnp.einsum(
            "fn,cn->fc", hidden_act, full_cot, preferred_element_type=jnp.float32
        )
        pre_grad = hidden_grad * gelu_slope(pre_act)
        pre_round = pre_grad.astype(jnp.bfloat16)
        up_shift_grad = jnp.sum(pre_grad, axis=1)
        up_grad = jnp.einsum("cn,fn->cf", lifted, pre_round, preferred_element_type=jnp.float32)
        partial = jnp.einsum(
            "fn,cf->cn", pre_round, up_weight[layer], preferred_element_type=jnp.float32
        ).reshape(blocks, chan_count, cells)
        scaled_part = partial * full_gain[layer][:, :, None]
        own_sums = jnp.stack(
            [
                jnp.sum(scaled_part, axis=(0, 1)),
                jnp.sum(scaled_part * full_normed, axis=(0, 1)),
            ]
        )
        pieces, sums = push("ch", 6, [partial.astype(jnp.bfloat16), own_sums], [True, False])
        lift_grad = jnp.sum(pieces.astype(jnp.float32), axis=0)
        gain_two_grad = jnp.sum(lift_grad * normed_two, axis=1)
        shift_two_grad = jnp.sum(lift_grad, axis=1)
        scaled_two = lift_grad * second_gain[layer][:, None]
        sums = jnp.sum(sums, axis=0) / channel_total
        inner_grad = (
            flat_grad + rstd_two * (scaled_two - sums[0] - normed_two * sums[1])
        ).reshape(shape)
        mode_grad = to_modes(inner_grad, lon_inverse.T, groups)

        def local_filter(spec_in, weight_in, bias_in, weight_out, bias_out):
            return spectral_local(spec_in, weight_in, bias_in, weight_out, bias_out, lat_matrix)

        _, filter_vjp = jax.vjp(
            local_filter,
            spectrum,
            filter_inner[layer],
            filter_inner_bias[layer],
            filter_outer[layer],
            filter_outer_bias[layer],
        )
        spectrum_grad, first_w_grad, first_b_grad, second_w_grad, second_b_grad = filter_vjp(
            mode_grad
        )
        mixed_grad = inner_grad + to_rows(spectrum_grad, lon_forward.T, shape)
        gain_one_grad = jnp.sum(mixed_grad * normed_one, axis=(1, 2))
        shift_one_grad = jnp.sum(mixed_grad, axis=(1, 2))
        scaled_one = mixed_grad * first_gain[layer][:, None, None]
        own_sums = jnp.stack([jnp.sum(scaled_one, axis=0), jnp.sum(scaled_one * normed_one, axis=0)])
        sums = push("ch", 2, [own_sums.reshape(2, cells)], [False])[0]
        sums = jnp.sum(sums, axis=0).reshape(2, row_count, lon_cells) / channel_total
        grad_now = inner_grad + rstd_one * (scaled_one - sums[0] - normed_one * sums[1])
        layer_terms = (
            gain_one_grad,
            shift_one_grad,
            first_w_grad,
            first_b_grad,
            second_w_grad,
            second_b_grad,
            gain_two_grad,
            shift_two_grad,
            lax.psum(up_grad, "lat"),
            up_shift_grad,
            lax.psum(down_grad, "lat"),
            down_shift_grad,
        )
        collected.append(layer_terms)
    collected = collected[::-1]
    stacked = [jnp.stack([terms[position] for terms in collected]) for position in range(12)]
    small = [at for at in range(12) if at not in (8, 10)]
    packed = jnp.concatenate([stacked[at].reshape(-1) for at in small])
    packed = jnp.pad(packed, (0, -packed.size % 1024)).reshape(-1, 128)
    packed = jnp.sum(push("lat", 7, [packed], [False])[0], axis=0).reshape(-1)
    begin = 0
    for at in small:
        size = stacked[at].size
        stacked[at] = packed[begin : begin + size].reshape(stacked[at].shape)
        begin += size
    return (current, grad_now) + tuple(stacked)


def solution(mesh):
    placed = (
        P("ch", "lat", None),
        P("ch", "lat", None),
        P(None, "ch"),
        P(None, "ch"),
        P(None, None, "ch", None, None),
        P(None, None, "ch", None),
        P(None, None, "ch", None, None),
        P(None, None, "ch", None),
        P(None, "ch"),
        P(None, "ch"),
        P(None, None, "ch"),
        P(None, "ch"),
        P(None, "ch", None),
        P(None, "ch"),
        P(),
        P(),
    )
    return jax.shard_map(
        body,
        mesh=mesh,
        in_specs=placed,
        out_specs=(
            P("ch", "lat", None),
            P("ch", "lat", None),
            P(None, "ch"),
            P(None, "ch"),
            P(None, None, "ch", None, None),
            P(None, None, "ch", None),
            P(None, None, "ch", None, None),
            P(None, None, "ch", None),
            P(None, "ch"),
            P(None, "ch"),
            P(None, None, "ch"),
            P(None, "ch"),
            P(None, "ch", None),
            P(None, "ch"),
        ),
        check_vma=False,
    )
```

```python
import functools
import math

import jax
import jax.numpy as jnp
from jax import lax
from jax.experimental import pallas as pl
from jax.experimental.pallas import tpu as pltpu
from jax.sharding import PartitionSpec as P

shrink_level = 0.01
norm_eps = 1e-05
highest = lax.Precision.HIGHEST
MESH = pl.DeviceIdType.MESH
F32 = jnp.float32
BF16 = jnp.bfloat16

LAYERS = 4
NCH = 8
NLAT = 16
CB = 48
CP = 64
D = NCH * CB
ROWS = 5
LON = 180
TILE = 128
FB = 192
FF = NCH * FB
CHUNK = 384
TILE_FROM = [r * LON // TILE for r in range(ROWS)]
TILE_TO = [-(-(r + 1) * LON // TILE) for r in range(ROWS)]
SPAN = max(b - a for a, b in zip(TILE_FROM, TILE_TO)) * TILE


def gelu_exact(values):
    return 0.5 * values * (1.0 + lax.erf(values * 0.7071067811865476))


def gelu_slope(values):
    return (
        0.5 * (1.0 + lax.erf(values * 0.7071067811865476))
        + values * jnp.exp(-0.5 * values * values) * 0.3989422804014327
    )


def mm(a, b, dims=((1,), (0,)), precision=highest):
    return lax.dot_general(a, b, (dims, ((), ())), precision=precision, preferred_element_type=F32)


def mb(a, b, dims=((1,), (0,))):
    return lax.dot_general(a, b, (dims, ((), ())), preferred_element_type=F32)


NT = ((1,), (1,))


def stack_kernel(
    x0, ct, prm, wsh, bdw, bdt, fb, lat_a, lat_t, lon,
    out_h, out_g, gw, gp, gf, gfb,
    h_s, g_s, xin, pbuf, pcol, bcol, mbuf, fbuf, sbuf, xbuf, zbuf, cbuf, bbuf,
    wall, wT, n1_s, n2_s, r1_s, r2_s, lifted_s, pre_s, hid_s, y_s, hh_s, t_s,
    xs, prs, gr, psend, pget, gsend, gget, prow, pin, ig_s,
    bsem_s, bsem_r, asem_s, asem_r, psem_s, psem_r, gsem_s, gsem_r, qsem_s, qsem_r,
    c_s, c_r, l_s, l_r,
):
    ch = lax.axis_index("ch")
    lat = lax.axis_index("lat")
    core = lax.rem(lat, 2)
    partner = lat + 1 - 2 * core
    flip = lat + 2 - 4 * lax.rem(lat // 2, 2)
    ch_peer = [lax.rem(ch + s, NCH) for s in range(NCH)]
    lat_peer = [lax.rem(lat + s, NLAT) for s in range(NLAT)]

    barrier = pltpu.get_barrier_semaphore()
    for s in range(1, NCH):
        pl.semaphore_signal(barrier, inc=1, device_id={"ch": ch_peer[s]}, device_id_type=MESH)
        if s % 2:
            pl.semaphore_signal(
                barrier, inc=1, device_id={"lat": flip, "ch": ch_peer[s]}, device_id_type=MESH
            )
    for s in range(1, NLAT):
        pl.semaphore_signal(barrier, inc=1, device_id={"lat": lat_peer[s]}, device_id_type=MESH)

    def remote(src, dst, send, recv, where):
        return pltpu.make_async_remote_copy(
            src_ref=src, dst_ref=dst, send_sem=send, recv_sem=recv,
            device_id=where, device_id_type=MESH,
        )

    def over_ch(src, dst, send, recv):
        copies = [
            remote(src(ch_peer[s]), dst, send.at[s], recv.at[s], {"ch": ch_peer[s]})
            for s in range(1, NCH)
        ]
        for copy in copies:
            copy.start()
        return copies

    def over_near(src, dst, send, recv):
        copies = []
        for s in range(1, NCH):
            where = {"lat": flip, "ch": ch_peer[s]} if s % 2 else {"ch": ch_peer[s]}
            copies.append(remote(src(ch_peer[s]), dst, send.at[s], recv.at[s], where))
        return copies

    def over_lat(src, dst, at):
        copies = [
            remote(
                src.at[lat_peer[s]], dst.at[lat], l_s.at[at, s], l_r.at[at, s], {"lat": lat_peer[s]}
            )
            for s in range(1, NLAT)
        ]
        for copy in copies:
            copy.start()
        return copies

    def done(copies):
        for copy in copies:
            copy.wait()

    def weights_near(layer):
        mine = wall.at[layer, core, pl.ds(pl.multiple_of(ch * FB, FB), FB)]
        return over_near(
            lambda p: wsh.at[layer, core], mine, asem_s.at[layer], asem_r.at[layer]
        )

    def weights_pair(layer):
        block = wall.at[layer, core]
        return remote(block, block, psem_s.at[layer], psem_r.at[layer], {"lat": partner})

    def weights_start(layer):
        for copy in weights_near(layer):
            copy.start()

    def weights_pass(layer):
        wall[layer, core, pl.ds(pl.multiple_of(ch * FB, FB), FB)] = wsh[layer, core]
        done(weights_near(layer))
        weights_pair(layer).start()

    def weights_done(layer):
        weights_pair(layer).wait()

    fbuf[...] = jnp.zeros(fbuf.shape, F32)
    sbuf[...] = jnp.zeros(sbuf.shape, F32)
    prow[...] = jnp.zeros(prow.shape, F32)
    gfb[...] = jnp.zeros(gfb.shape, F32)
    xin[0, ch] = x0[ch]
    xin[1, ch] = ct[ch]
    pbuf[ch] = prm[...]
    pl.semaphore_wait(barrier, 2 * (NCH - 1) + NLAT - 1 - 3)
    first = over_ch(lambda p: x0.at[p], xin.at[0, ch], bsem_s.at[0], bsem_r.at[0])
    first += over_ch(lambda p: prm, pbuf.at[ch], bsem_s.at[1], bsem_r.at[1])
    second = over_ch(lambda p: ct.at[p], xin.at[1, ch], bsem_s.at[2], bsem_r.at[2])
    weights_start(0)
    done(first)
    for j in range(NCH):
        turned = jnp.transpose(pbuf[j])
        for layer in range(LAYERS):
            part = turned[:, layer * 8 : layer * 8 + 8]
            pcol[layer, j * CB : (j + 1) * CB, 0:8] = part[:CB]
            bcol[layer, j * FB : (j + 1) * FB, 0:8] = part[:FB]
    h_s[...] = xin[0]

    low = lax.broadcasted_iota(jnp.int32, (NLAT, TILE), 1) < CP

    def swap(v):
        return pltpu.roll(v, CP, 1)

    def lon_to_modes(which):
        for r in range(ROWS):
            a, b = TILE_FROM[r], TILE_TO[r]
            field = jnp.concatenate([fbuf[t] for t in range(a, b)], axis=1)
            part = mm(lon[which, r, :, : (b - a) * TILE], field, NT)
            sbuf[:, :, r * CP : (r + 1) * CP] = part.reshape(NLAT, 8, CP)

    def gather_lat():
        for ri in range(2):
            for kt in range(2):
                even = xbuf[:, 4 * kt + ri, :]
                odd = xbuf[:, 4 * kt + 2 + ri, :]
                for r in range(ROWS):
                    cut = slice(r // 2 * TILE, (r // 2 + 1) * TILE)
                    a, b = even[:, cut], odd[:, cut]
                    tile = jnp.where(low, swap(a), b) if r % 2 else jnp.where(low, a, swap(b))
                    at = ri * ROWS * NLAT + r * NLAT
                    xs[at : at + NLAT, kt * TILE : (kt + 1) * TILE] = tile

    def scatter_lat(z):
        for ri in range(2):
            for k in range(4):
                for t in range(3):
                    at = ri * ROWS * NLAT + 2 * t * NLAT
                    lanes = slice(k // 2 * TILE, (k // 2 + 1) * TILE)
                    a = z[at : at + NLAT, lanes]
                    if t == 2:
                        b = jnp.zeros_like(a)
                    else:
                        b = z[at + NLAT : at + 2 * NLAT, lanes]
                    tile = jnp.where(low, swap(a), b) if k % 2 else jnp.where(low, a, swap(b))
                    sbuf[:, 2 * k + ri, t * TILE : (t + 1) * TILE] = tile

    def lon_to_cells(which):
        tiles = [None] * NCH
        for r in range(ROWS):
            if r % 2 == 0:
                turned = jnp.transpose(
                    zbuf[:, :, r // 2 * TILE : (r // 2 + 1) * TILE].reshape(TILE, TILE)
                )
            a, b = TILE_FROM[r], TILE_TO[r]
            rows = turned[(r % 2) * CP : (r % 2) * CP + CB]
            part = mm(rows, lon[which, r, :, : (b - a) * TILE])
            for t in range(a, b):
                piece = part[:, (t - a) * TILE : (t - a + 1) * TILE]
                tiles[t] = piece if tiles[t] is None else tiles[t] + piece
        for t in range(NCH):
            cbuf[t] = tiles[t]

    def mix(v, table, sign):
        out = []
        for t in range(2):
            q = mm(v[:, t * TILE : (t + 1) * TILE], table)
            re = q[:64, :TILE] - sign * q[64:, TILE:]
            im = q[64:, :TILE] + sign * q[:64, TILE:]
            out.append(jnp.concatenate([re, im], axis=0))
        return jnp.concatenate(out, axis=1)

    def bias_rows(layer, at):
        re = jnp.broadcast_to(fb[layer, at : at + 1, :], (64, 2 * TILE))
        im = jnp.broadcast_to(fb[layer, at + 1 : at + 2, :], (64, 2 * TILE))
        return jnp.concatenate([re, im], axis=0)

    def exchange_one(value):
        mbuf[...] = value.reshape(NCH, CB, TILE)
        copies = over_ch(lambda p: mbuf.at[p], fbuf.at[ch, pl.ds(0, CB)], c_s.at[0], c_r.at[0])
        fbuf[ch, 0:CB] = mbuf[ch]
        return copies

    def exchange_four():
        copies = over_ch(lambda p: cbuf.at[p], bbuf.at[ch], c_s.at[1], c_r.at[1])
        bbuf[ch] = cbuf[ch]
        return copies

    def exchange_lat(dst, at):
        copies = over_lat(sbuf, dst, at)
        dst[lat] = sbuf[lat]
        return copies

    def col(layer, at):
        return pcol[layer, :, at : at + 1]

    def forward(layer, carry):
        h = h_s[...].reshape(D, TILE)
        mean = jnp.sum(h, axis=0, keepdims=True) * (1.0 / D)
        spread = jnp.sum(h * h, axis=0, keepdims=True) * (1.0 / D) - mean * mean
        rstd = lax.rsqrt(spread + norm_eps)
        n1 = (h - mean) * rstd
        n1_s[layer] = n1
        r1_s[layer] = jnp.broadcast_to(rstd, (8, TILE))
        mixed = n1 * col(layer, 0) + col(layer, 1)
        copies = exchange_one(mixed)
        ig_s[...] = h + mixed

        @pl.when(layer < LAYERS - 1)
        def _():
            weights_start(layer + 1)

        done(copies)
        lon_to_modes(0)
        copies = exchange_lat(xbuf, 0)
        weights_pass(layer)
        done(copies)
        gather_lat()
        y = mm(lat_a[...], xs[...])
        y_s[layer] = y
        hh = mix(y, bdw[layer, 0], 1.0) + bias_rows(layer, 0)
        hh_s[layer] = hh
        b = mix(gelu_exact(hh), bdw[layer, 1], 1.0) + bias_rows(layer, 2)
        t = jnp.tanh(b / shrink_level)
        t_s[layer] = t
        scatter_lat(mm(lat_t[...], b - shrink_level * t))
        copies = exchange_lat(zbuf, 1)
        weights_done(layer)
        for at in range(0, FF, CHUNK):
            wT[:, at : at + CHUNK] = jnp.transpose(wall[layer, 1, at : at + CHUNK, :])
        done(copies)
        lon_to_cells(1)
        copies = exchange_four()
        done(copies)
        inner = ig_s[...] + bbuf[...].reshape(D, TILE)
        mean = jnp.sum(inner, axis=0, keepdims=True) * (1.0 / D)
        spread = jnp.sum(inner * inner, axis=0, keepdims=True) * (1.0 / D) - mean * mean
        rstd = lax.rsqrt(spread + norm_eps)
        n2 = (inner - mean) * rstd
        n2_s[layer] = n2
        r2_s[layer] = jnp.broadcast_to(rstd, (8, TILE))
        lifted = (n2 * col(layer, 2) + col(layer, 3)).astype(BF16)
        lifted_s[layer] = lifted
        total = inner + col(layer, 4)
        for at in range(0, FF, CHUNK):
            pre = mb(wall[layer, 0, at : at + CHUNK, :], lifted) + bcol[layer, at : at + CHUNK, 5:6]
            pre_s[layer, at : at + CHUNK] = pre
            hidden = gelu_exact(pre).astype(BF16)
            hid_s[layer, at : at + CHUNK] = hidden
            total = total + mb(wT[:, at : at + CHUNK], hidden)
        h_s[...] = total.reshape(NCH, CB, TILE)
        return carry

    lax.fori_loop(0, LAYERS, forward, 0)
    last_h = over_ch(lambda p: h_s.at[p], out_h.at[ch], bsem_s.at[3], bsem_r.at[3])
    out_h[ch] = h_s[ch]
    done(second)
    g_s[...] = xin[1]
    ones = jnp.ones((8, TILE), F32)

    def turn_up(layer):
        for at in range(0, FF, CHUNK):
            wT[:, at : at + CHUNK] = jnp.transpose(wall[layer, 0, at : at + CHUNK, :])

    turn_up(LAYERS - 1)

    def row_sums(layer, at, value, width):
        for j in range(NCH):
            part = mm(ones, value[j * width : (j + 1) * width], NT)
            prow[j, layer, at : at + 1, 0:width] = part[0:1]

    def grads_pair(layer):
        return remote(
            psend.at[layer], pget.at[layer], qsem_s.at[layer], qsem_r.at[layer], {"lat": partner}
        )

    def grads_near(layer):
        return over_near(
            lambda p: gsend.at[layer, p], gget.at[layer, ch], gsem_s.at[layer], gsem_r.at[layer]
        )

    def grads_done(layer):
        gget[layer, ch] = gsend[layer, ch]
        done(grads_near(layer))
        total = gget[layer, 0].astype(F32)
        for j in range(1, NCH):
            total = total + gget[layer, j].astype(F32)
        gw[layer] = total

    def backward(step, carry):
        layer = LAYERS - 1 - step
        g = g_s[...].reshape(D, TILE)
        g_round = g.astype(BF16)
        lift = jnp.zeros((D, TILE), F32)
        for at in range(0, FF, CHUNK):
            hidden_grad = mb(wall[layer, 1, at : at + CHUNK, :], g_round)
            pre_grad = hidden_grad * gelu_slope(pre_s[layer, at : at + CHUNK])
            pre_s[layer, at : at + CHUNK] = pre_grad
            pre_round = pre_grad.astype(BF16)
            prs[at : at + CHUNK] = pre_round
            lift = lift + mb(wT[:, at : at + CHUNK], pre_round)
        n2 = n2_s[layer]
        q2 = lift * col(layer, 2)
        m1 = jnp.sum(q2, axis=0, keepdims=True) * (1.0 / D)
        m2 = jnp.sum(q2 * n2, axis=0, keepdims=True) * (1.0 / D)
        inner_grad = g + r2_s[layer, 0:1, :] * (q2 - m1 - n2 * m2)
        copies = exchange_one(inner_grad)
        ig_s[...] = inner_grad
        lifted = lifted_s[layer]
        for at in range(0, FF, CHUNK):
            gr[1, at : at + CHUNK] = mb(hid_s[layer, at : at + CHUNK], g_round, NT)
            gr[0, at : at + CHUNK] = mb(prs[at : at + CHUNK], lifted, NT)
        psend[layer] = gr[1 - core].astype(BF16)
        grads_pair(layer).start()
        row_sums(layer, 4, g, CB)
        row_sums(layer, 2, lift * n2, CB)
        row_sums(layer, 3, lift, CB)
        done(copies)
        lon_to_modes(1)
        copies = exchange_lat(xbuf, 0)
        row_sums(layer, 5, pre_s[layer], FB)
        grads_pair(layer).wait()
        gsend[layer] = (
            (gr[core] + pget[layer].astype(F32)).astype(BF16).reshape(NCH, FB, D)
        )
        for copy in grads_near(layer):
            copy.start()
        done(copies)
        gather_lat()
        t = t_s[layer]
        db = mm(lat_a[...], xs[...]) * (t * t)
        hh = hh_s[layer]
        dh = mix(db, bdt[layer, 1], -1.0) * gelu_slope(hh)
        dy = mix(dh, bdt[layer, 0], -1.0)
        scatter_lat(mm(lat_t[...], dy))
        copies = exchange_lat(zbuf, 1)

        def filter_grads(at, left, right):
            turned = jnp.concatenate([right[64:], -right[:64]], axis=0)
            total = jnp.zeros((TILE, 2 * TILE), F32)
            for tt in range(2):
                lanes = slice(tt * TILE, (tt + 1) * TILE)
                pair = jnp.concatenate([right[:, lanes], turned[:, lanes]], axis=1)
                total = total + mm(jnp.transpose(left[:, lanes]), pair)
            re = total[:64, :TILE] + swap(total[64:, :TILE])
            im = total[:64, TILE:] + swap(total[64:, TILE:])
            keep = lax.broadcasted_iota(jnp.int32, (64, TILE), 1) < CP
            gf[layer, at] = jnp.where(keep, re, swap(im))
            gfb[layer, 2 * at : 2 * at + 1] = jnp.sum(right[:64], axis=0, keepdims=True)
            gfb[layer, 2 * at + 1 : 2 * at + 2] = jnp.sum(right[64:], axis=0, keepdims=True)

        filter_grads(1, gelu_exact(hh), db)
        filter_grads(0, y_s[layer], dh)

        @pl.when(layer > 0)
        def _():
            turn_up(layer - 1)

        done(copies)
        lon_to_cells(0)
        copies = exchange_four()

        @pl.when(layer < LAYERS - 1)
        def _():
            grads_done(layer + 1)

        done(copies)
        inner_grad = ig_s[...]
        mixed_grad = inner_grad + bbuf[...].reshape(D, TILE)
        n1 = n1_s[layer]
        q1 = mixed_grad * col(layer, 0)
        m1 = jnp.sum(q1, axis=0, keepdims=True) * (1.0 / D)
        m2 = jnp.sum(q1 * n1, axis=0, keepdims=True) * (1.0 / D)
        g = inner_grad + r1_s[layer, 0:1, :] * (q1 - m1 - n1 * m2)
        g_s[...] = g.reshape(NCH, CB, TILE)
        row_sums(layer, 0, mixed_grad * n1, CB)
        row_sums(layer, 1, mixed_grad, CB)
        return carry

    lax.fori_loop(0, LAYERS, backward, 0)
    final = over_ch(lambda p: g_s.at[p], out_g.at[ch], bsem_s.at[4], bsem_r.at[4])
    final += over_ch(lambda p: prow.at[p], pin.at[ch], bsem_s.at[5], bsem_r.at[5])
    out_g[ch] = g_s[ch]
    pin[ch] = prow[ch]
    grads_done(0)
    done(last_h)
    done(final)
    total = pin[0]
    for j in range(1, NCH):
        total = total + pin[j]
    gp[...] = total


def run_stack(*args):
    shapes = [
        jax.ShapeDtypeStruct((NCH, CB, TILE), F32),
        jax.ShapeDtypeStruct((NCH, CB, TILE), F32),
        jax.ShapeDtypeStruct((LAYERS, FB, D), F32),
        jax.ShapeDtypeStruct((LAYERS, 8, 256), F32),
        jax.ShapeDtypeStruct((LAYERS, 2, 64, TILE), F32),
        jax.ShapeDtypeStruct((LAYERS, 8, 256), F32),
    ]
    v = pltpu.VMEM
    dma = pltpu.SemaphoreType.DMA
    scratch = [
        v((NCH, CB, TILE), F32),
        v((NCH, CB, TILE), F32),
        v((2, NCH, CB, TILE), F32),
        v((NCH, 32, 256), F32),
        v((LAYERS, D, TILE), F32),
        v((LAYERS, FF, TILE), F32),
        v((NCH, CB, TILE), F32),
        v((NCH, CP, TILE), F32),
        v((NLAT, 8, 3 * TILE), F32),
        v((NLAT, 8, 3 * TILE), F32),
        v((NLAT, 8, 3 * TILE), F32),
        v((NCH, CB, TILE), F32),
        v((NCH, CB, TILE), F32),
        v((LAYERS, 2, FF, D), BF16),
        v((D, FF), BF16),
        v((LAYERS, D, TILE), F32),
        v((LAYERS, D, TILE), F32),
        v((LAYERS, 8, TILE), F32),
        v((LAYERS, 8, TILE), F32),
        v((LAYERS, D, TILE), BF16),
        v((LAYERS, FF, TILE), F32),
        v((LAYERS, FF, TILE), BF16),
        v((LAYERS, TILE, 256), F32),
        v((LAYERS, TILE, 256), F32),
        v((LAYERS, TILE, 256), F32),
        v((2 * ROWS * NLAT, 256), F32),
        v((FF, TILE), BF16),
        v((2, FF, D), F32),
        v((LAYERS, FF, D), BF16),
        v((LAYERS, FF, D), BF16),
        v((LAYERS, NCH, FB, D), BF16),
        v((LAYERS, NCH, FB, D), BF16),
        v((NCH, LAYERS, 8, 256), F32),
        v((NCH, LAYERS, 8, 256), F32),
        v((D, TILE), F32),
        dma((6, NCH)),
        dma((6, NCH)),
        dma((LAYERS, NCH)),
        dma((LAYERS, NCH)),
        dma((LAYERS,)),
        dma((LAYERS,)),
        dma((LAYERS, NCH)),
        dma((LAYERS, NCH)),
        dma((LAYERS,)),
        dma((LAYERS,)),
        dma((2, NCH)),
        dma((2, NCH)),
        dma((2, NLAT)),
        dma((2, NLAT)),
    ]
    return pl.pallas_call(
        stack_kernel,
        out_shape=shapes,
        in_specs=[pl.BlockSpec(memory_space=pltpu.VMEM)] * len(args),
        out_specs=[pl.BlockSpec(memory_space=pltpu.VMEM)] * len(shapes),
        scratch_shapes=scratch,
        compiler_params=pltpu.CompilerParams(
            collective_id=0, has_side_effects=True, vmem_limit_bytes=60 << 20
        ),
        name="stack",
    )(*args)


SMALL = 640
WROWS = LAYERS * FB // 8


def finish_kernel(gw, small, wout, sout, wget, sget, wsum, ssum, s1, r1, s2, r2, s3, r3, s4, r4):
    lat = lax.axis_index("lat")
    core = lax.rem(lat, 2)
    near = lat // 2
    peer = [lax.rem(lat + s, NLAT) for s in range(NLAT)]
    barrier = pltpu.get_barrier_semaphore()
    for s in range(1, NLAT):
        pl.semaphore_signal(barrier, inc=1, device_id={"lat": peer[s]}, device_id_type=MESH)

    def remote(src, dst, send, recv, where):
        copy = pltpu.make_async_remote_copy(
            src_ref=src, dst_ref=dst, send_sem=send, recv_sem=recv,
            device_id={"lat": where}, device_id_type=MESH,
        )
        copy.start()
        return copy

    pl.semaphore_wait(barrier, NLAT - 1)
    copies = [
        remote(gw.at[peer[s] // 2], wget.at[near], s1.at[s], r1.at[s], peer[s])
        for s in range(2, NLAT, 2)
    ]
    copies += [
        remote(small.at[peer[s]], sget.at[lat], s2.at[s], r2.at[s], peer[s])
        for s in range(1, NLAT)
    ]
    wget[near] = gw[near]
    sget[lat] = small[lat]
    for copy in copies:
        copy.wait()
    total = wget[0]
    for j in range(1, 8):
        total = total + wget[j]
    wsum[...] = total.astype(BF16)
    copies = [
        remote(wsum, wout.at[core, near], s3.at[s], r3.at[s], peer[s]) for s in range(1, NLAT)
    ]
    part = sget[0]
    for j in range(1, NLAT):
        part = part + sget[j]
    ssum[...] = part
    copies += [
        remote(ssum, sout.at[lat], s4.at[s], r4.at[s], peer[s]) for s in range(1, NLAT)
    ]
    wout[core, near] = wsum[...]
    sout[lat] = ssum[...]
    for copy in copies:
        copy.wait()


def run_finish(gw, small):
    v = pltpu.VMEM
    dma = pltpu.SemaphoreType.DMA
    return pl.pallas_call(
        finish_kernel,
        out_shape=[
            jax.ShapeDtypeStruct((2, 8, WROWS, D), BF16),
            jax.ShapeDtypeStruct((NLAT, SMALL // NLAT, TILE), F32),
        ],
        in_specs=[pl.BlockSpec(memory_space=pltpu.VMEM)] * 2,
        out_specs=[pl.BlockSpec(memory_space=pltpu.VMEM)] * 2,
        scratch_shapes=[
            v((8, WROWS, D), F32),
            v((NLAT, SMALL // NLAT, TILE), F32),
            v((WROWS, D), BF16),
            v((SMALL // NLAT, TILE), F32),
        ]
        + [dma((NLAT,))] * 8,
        compiler_params=pltpu.CompilerParams(
            collective_id=1, has_side_effects=True, vmem_limit_bytes=40 << 20
        ),
        name="finish",
    )(gw.reshape(8, WROWS, D), small.reshape(NLAT, SMALL // NLAT, TILE))


def lat_table(kept_lat, lat_cells):
    cell_index = jnp.arange(lat_cells, dtype=jnp.int32)
    phase_index = kept_lat[:, None] * cell_index[None, :] % lat_cells
    angles = phase_index.astype(F32) * (2.0 * math.pi / lat_cells)
    scale = 1.0 / math.sqrt(lat_cells)
    modes = kept_lat.shape[0]

    def place(table):
        table = table.reshape(modes, NLAT, ROWS).transpose(0, 2, 1).reshape(modes, lat_cells)
        return jnp.pad(table, ((0, 64 - modes), (0, 0)))

    cos, sin = place(jnp.cos(angles) * scale), place(jnp.sin(angles) * scale)
    return jnp.concatenate(
        [jnp.concatenate([cos, sin], axis=1), jnp.concatenate([-sin, cos], axis=1)], axis=0
    )


def lon_tables(kept_lon, lon_cells):
    cell_index = jnp.arange(lon_cells, dtype=jnp.int32)
    phase_index = kept_lon[:, None] * cell_index[None, :] % lon_cells
    angles = phase_index.astype(F32) * (2.0 * math.pi / lon_cells)
    scale = 1.0 / math.sqrt(lon_cells)
    weight = jnp.where((kept_lon == 0) | (2 * kept_lon == lon_cells), 1.0, 2.0).astype(F32)
    table = jnp.stack([jnp.cos(angles), -jnp.sin(angles)], axis=1) * scale
    both = jnp.stack([table, table * weight[:, None, None]]).reshape(2, -1, lon_cells)
    rows = []
    for r in range(ROWS):
        before = r * LON - TILE_FROM[r] * TILE
        rows.append(jnp.pad(both, ((0, 0), (0, 0), (before, SPAN - LON - before))))
    return jnp.stack(rows, axis=1)


def pair_table(weight):
    padded = jnp.pad(weight, ((0, 0), (0, 0), (0, CP - CB), (0, CP - CB)))
    zero = jnp.zeros_like(padded)
    top = jnp.concatenate([padded, zero], axis=3)
    bottom = jnp.concatenate([zero, padded], axis=3)
    both = jnp.concatenate([top, bottom], axis=2)
    return jnp.concatenate([both[:, 0], both[:, 1]], axis=2)


def body(
    inputs,
    cotangent,
    first_gain,
    first_shift,
    filter_inner,
    filter_inner_bias,
    filter_outer,
    filter_outer_bias,
    second_gain,
    second_shift,
    up_weight,
    up_bias,
    down_weight,
    down_bias,
    kept_lat,
    kept_lon,
):
    shape = inputs.shape
    cells = ROWS * LON

    def to_tiles(field):
        flat = jnp.pad(field.reshape(CB, cells), ((0, 0), (0, NCH * TILE - cells)))
        return flat.reshape(CB, NCH, TILE).transpose(1, 0, 2)

    def from_tiles(tiles):
        return tiles.transpose(1, 0, 2).reshape(CB, NCH * TILE)[:, :cells].reshape(shape)

    vectors = jnp.stack([first_gain, first_shift, second_gain, second_shift, down_bias], axis=1)
    prm = jnp.concatenate(
        [
            jnp.pad(vectors, ((0, 0), (0, 0), (0, 256 - CB))),
            jnp.pad(up_bias[:, None, :], ((0, 0), (0, 2), (0, 256 - FB))),
        ],
        axis=1,
    ).reshape(32, 256)
    shards = jnp.stack([up_weight.transpose(0, 2, 1), down_weight], axis=1)
    inner_w, outer_w = filter_inner[:, :, 0], filter_outer[:, :, 0]
    bdw = jnp.stack([pair_table(inner_w), pair_table(outer_w)], axis=1)
    bdt = jnp.stack(
        [pair_table(inner_w.transpose(0, 1, 3, 2)), pair_table(outer_w.transpose(0, 1, 3, 2))],
        axis=1,
    )
    biases = jnp.concatenate([filter_inner_bias[:, :, 0], filter_outer_bias[:, :, 0]], axis=1)
    biases = jnp.tile(jnp.pad(biases, ((0, 0), (0, 4), (0, CP - CB))), (1, 1, 4))
    lat_a = lat_table(kept_lat, ROWS * NLAT)
    lon = lon_tables(kept_lon, LON)
    out_h, out_g, gw, gp, gf, gfb = run_stack(
        to_tiles(inputs), to_tiles(cotangent), prm, shards, bdw, bdt, biases,
        lat_a, lat_a.T, lon,
    )
    small = jnp.concatenate(
        [gf.reshape(-1, TILE), gfb.reshape(-1, TILE), gp.reshape(-1, TILE)], axis=0
    )
    wout, sout = run_finish(gw, small)
    wout = wout.reshape(2, LAYERS, FB, D).astype(F32)
    sout = sout.reshape(SMALL, TILE)
    filters = sout[:512].reshape(LAYERS, 2, CP, 2, CP)[:, :, :CB, :, :CB].transpose(1, 0, 3, 2, 4)
    fbias = sout[512:576].reshape(LAYERS, 8, 4, CP)[:, :4, :, :CB].sum(axis=2)
    fbias = fbias.reshape(LAYERS, 2, 2, 1, CB)
    rows = sout[576:].reshape(LAYERS, 8, 256)
    return (
        from_tiles(out_h),
        from_tiles(out_g),
        rows[:, 0, :CB],
        rows[:, 1, :CB],
        filters[0][:, :, None],
        fbias[:, 0],
        filters[1][:, :, None],
        fbias[:, 1],
        rows[:, 2, :CB],
        rows[:, 3, :CB],
        wout[0].transpose(0, 2, 1),
        rows[:, 5, :FB],
        wout[1],
        rows[:, 4, :CB],
    )


def solution(mesh):
    placed = (
        P("ch", "lat", None),
        P("ch", "lat", None),
        P(None, "ch"),
        P(None, "ch"),
        P(None, None, "ch", None, None),
        P(None, None, "ch", None),
        P(None, None, "ch", None, None),
        P(None, None, "ch", None),
        P(None, "ch"),
        P(None, "ch"),
        P(None, None, "ch"),
        P(None, "ch"),
        P(None, "ch", None),
        P(None, "ch"),
        P(),
        P(),
    )
    return jax.shard_map(
        body,
        mesh=mesh,
        in_specs=placed,
        out_specs=(
            P("ch", "lat", None),
            P("ch", "lat", None),
            P(None, "ch"),
            P(None, "ch"),
            P(None, None, "ch", None, None),
            P(None, None, "ch", None),
            P(None, None, "ch", None, None),
            P(None, None, "ch", None),
            P(None, "ch"),
            P(None, "ch"),
            P(None, None, "ch"),
            P(None, "ch"),
            P(None, "ch", None),
            P(None, "ch"),
        ),
        check_vma=False,
    )
```

```python
import functools
import math

import jax
import jax.numpy as jnp
import ml_dtypes
import numpy as np
from jax import lax
from jax.experimental import pallas as pl
from jax.experimental.pallas import tpu as pltpu
from jax.sharding import PartitionSpec as P

shrink_level = 0.01
norm_eps = 1e-05
highest = lax.Precision.HIGHEST
MESH = pl.DeviceIdType.MESH
F32 = jnp.float32
BF16 = jnp.bfloat16

LAYERS = 4
NCH = 8
NLAT = 16
CB = 48
CP = 64
D = NCH * CB
ROWS = 5
LON = 180
TILE = 128
FB = 192
FF = NCH * FB
CHUNK = 384
WROWS = FB // 8
TILE_FROM = [r * LON // TILE for r in range(ROWS)]
TILE_TO = [-(-(r + 1) * LON // TILE) for r in range(ROWS)]
SPAN = max(b - a for a, b in zip(TILE_FROM, TILE_TO)) * TILE


def gelu_exact(values):
    return 0.5 * values * (1.0 + lax.erf(values * 0.7071067811865476))


def gelu_slope(values):
    return (
        0.5 * (1.0 + lax.erf(values * 0.7071067811865476))
        + values * jnp.exp(-0.5 * values * values) * 0.3989422804014327
    )


def mm(a, b, dims=((1,), (0,)), precision=highest):
    return lax.dot_general(a, b, (dims, ((), ())), precision=precision, preferred_element_type=F32)


def mb(a, b, dims=((1,), (0,))):
    return lax.dot_general(a, b, (dims, ((), ())), preferred_element_type=F32)


NT = ((1,), (1,))


def split(value):
    high = value.astype(BF16)
    return high, (value - high.astype(F32)).astype(BF16)


def rows_times(value, high, low):
    vh, vl = split(value)
    n = value.shape[0]
    both = mb(jnp.concatenate([vh, vl], axis=0), high)
    return both[:n] + both[n:] + mb(vh, low)


def table_times(high, low, value):
    vh, vl = split(value)
    n = value.shape[1]
    both = mb(high, jnp.concatenate([vh, vl], axis=1))
    return both[:, :n] + both[:, n:] + mb(low, vh)


def stack_kernel(
    x0, ct, prm, wsh, fi, fo, fb, idx, all_a, all_t, all_k, all_v,
    out_h, out_g, wout, sout, rout, eout,
    h_s, g_s, xin, pbuf, pcol, bcol, mbuf, fbuf, sbuf, sbuf2, xbuf, zbuf, cbuf, bbuf,
    wall, wT, n1_s, n2_s, r1_s, r2_s, lifted_s, pre_s, hid_s, y_s, hh_s, t_s,
    xs, prs, gr, psend, pget, gsend, gget, pc, pin, bc, brow, bin_s, ig_s, mg_s, bwf,
    bw, bt, la, lt, lk, lv,
    gw, wget, wsum, gf, fget, fsum, gpsum, gpget, late, lin, lsum, lget,
    bsem_s, bsem_r, asem_s, asem_r, psem_s, psem_r, gsem_s, gsem_r, qsem_s, qsem_r,
    c_s, c_r, l_s, l_r, w1_s, w1_r, w2_s, w2_r, f_s, f_r,
):
    ch = lax.axis_index("ch")
    lat = lax.axis_index("lat")
    core = lax.rem(lat, 2)
    partner = lat + 1 - 2 * core
    flip = lat + 2 - 4 * lax.rem(lat // 2, 2)
    ch_peer = [lax.rem(ch + s, NCH) for s in range(NCH)]
    lat_peer = [lax.rem(lat + s, NLAT) for s in range(NLAT)]

    barrier = pltpu.get_barrier_semaphore()
    for s in range(1, NCH):
        pl.semaphore_signal(barrier, inc=1, device_id={"ch": ch_peer[s]}, device_id_type=MESH)
        if s % 2:
            pl.semaphore_signal(
                barrier, inc=1, device_id={"lat": flip, "ch": ch_peer[s]}, device_id_type=MESH
            )
    for s in range(1, NLAT):
        pl.semaphore_signal(barrier, inc=1, device_id={"lat": lat_peer[s]}, device_id_type=MESH)

    def remote(src, dst, send, recv, where):
        return pltpu.make_async_remote_copy(
            src_ref=src, dst_ref=dst, send_sem=send, recv_sem=recv,
            device_id=where, device_id_type=MESH,
        )

    def over_ch(src, dst, send, recv):
        copies = [
            remote(src(ch_peer[s]), dst, send.at[s], recv.at[s], {"ch": ch_peer[s]})
            for s in range(1, NCH)
        ]
        for copy in copies:
            copy.start()
        return copies

    def over_near(src, dst, send, recv):
        copies = []
        for s in range(1, NCH):
            where = {"lat": flip, "ch": ch_peer[s]} if s % 2 else {"ch": ch_peer[s]}
            copies.append(remote(src(ch_peer[s]), dst, send.at[s], recv.at[s], where))
        return copies

    def to_lat(src, dst, send, recv):
        return [
            remote(src(lat_peer[s]), dst, send.at[s], recv.at[s], {"lat": lat_peer[s]})
            for s in range(1, NLAT)
        ]

    def start(copies):
        for copy in copies:
            copy.start()
        return copies

    def arrived(copies):
        for copy in copies:
            copy.wait_recv()

    def sent(copies):
        for copy in copies:
            copy.wait_send()

    def done(copies):
        for copy in copies:
            copy.wait()

    def weights_near(layer):
        mine = wall.at[layer, core, pl.ds(pl.multiple_of(ch * FB, FB), FB)]
        return over_near(
            lambda p: wsh.at[layer, core], mine, asem_s.at[layer], asem_r.at[layer]
        )

    def weights_pair(layer):
        block = wall.at[layer, core]
        return remote(block, block, psem_s.at[layer], psem_r.at[layer], {"lat": partner})

    def weights_start(layer):
        for copy in weights_near(layer):
            copy.start()

    def weights_pass(layer):
        wall[layer, core, pl.ds(pl.multiple_of(ch * FB, FB), FB)] = wsh[layer, core]
        done(weights_near(layer))
        weights_pair(layer).start()

    def weights_done(layer):
        weights_pair(layer).wait()

    xin[0, ch] = x0[ch]
    xin[1, ch] = ct[ch]
    pbuf[ch] = prm[...]
    pl.semaphore_wait(barrier, 2 * (NCH - 1) + NLAT - 1 - 3)
    first = over_ch(lambda p: x0.at[p], xin.at[0, ch], bsem_s.at[0], bsem_r.at[0])
    first += over_ch(lambda p: prm, pbuf.at[ch], bsem_s.at[1], bsem_r.at[1])
    weights_start(0)
    pc[...] = jnp.zeros(pc.shape, F32)
    bc[...] = jnp.zeros(bc.shape, F32)
    late[...] = jnp.zeros(late.shape, F32)
    bwf[...] = jnp.zeros(bwf.shape, F32)

    def picker(at):
        rows = lax.broadcasted_iota(jnp.int32, (2 * TILE, TILE), 0)
        return jnp.where(rows == idx[at : at + 1, :], 1.0, 0.0)

    def turn(pick):
        return jnp.concatenate([jnp.transpose(pick[:TILE]), jnp.transpose(pick[TILE:])], axis=1)

    ends = (idx[0:1, :] < 2) | (idx[0:1, :] >= 180)
    mode_weight = jnp.where(ends, 1.0, 2.0)
    pick = picker(0)
    pick_t = jnp.concatenate([turn(pick), turn(pick * mode_weight)], axis=0).astype(BF16)
    pick = pick.astype(BF16)
    for part in range(2):
        for r in range(ROWS):
            table = mb(all_k[part, r], pick)
            lk[part, 0, r] = table.astype(BF16)
            lk[part, 1, r] = (table * mode_weight).astype(BF16)
            table = mb(pick_t, all_v[part, r]).astype(BF16)
            lv[part, 0, r] = table[:TILE]
            lv[part, 1, r] = table[TILE:]
    pick = picker(1)
    pick_t = turn(pick).astype(BF16)
    pick = pick.astype(BF16)
    for part in range(2):
        la[part] = mb(pick_t, all_a[part]).astype(BF16)
        lt[part] = mb(all_t[part], pick).astype(BF16)
    done(first)
    second = over_ch(lambda p: ct.at[p], xin.at[1, ch], bsem_s.at[2], bsem_r.at[2])
    for j in range(NCH):
        turned = jnp.transpose(pbuf[j])
        for layer in range(LAYERS):
            part = turned[:, layer * 8 : layer * 8 + 8]
            pcol[layer, j * CB : (j + 1) * CB, 0:8] = part[:CB]
            bcol[layer, j * FB : (j + 1) * FB, 0:8] = part[:FB]
    h_s[...] = xin[0]

    lane = lax.broadcasted_iota(jnp.int32, (NLAT, TILE), 1)

    def filter_tables(layer):
        for at, weight in enumerate((fi, fo)):
            for part in range(2):
                for k in range(2):
                    lanes = part * TILE + k * CP
                    bwf[k * CP : k * CP + CB, lanes : lanes + CB] = weight[layer, part]
            table = bwf[...]
            bw[0, layer, at], bw[1, layer, at] = split(table)
            bt[0, layer, at], bt[1, layer, at] = split(
                jnp.concatenate(
                    [jnp.transpose(table[:, :TILE]), jnp.transpose(table[:, TILE:])], axis=1
                )
            )

    def swap(v):
        return pltpu.roll(v, CP, 1)

    def lon_to_modes(which):
        parts = []
        for r in range(ROWS):
            a, b = TILE_FROM[r], TILE_TO[r]
            field = jnp.concatenate([fbuf[t] for t in range(a, b)], axis=1)
            span = (b - a) * TILE
            parts.append(rows_times(field, lk[0, which, r, :span], lk[1, which, r, :span]))
        parts.append(jnp.zeros((2 * TILE - ROWS * CB, TILE), F32))
        both = jnp.concatenate(parts, axis=0)
        for t in range(2):
            turned = jnp.transpose(both[t * TILE : (t + 1) * TILE])
            sbuf[:, :, t * TILE : (t + 1) * TILE] = turned.reshape(NLAT, 8, TILE)

    def gather_lat():
        for ri in range(2):
            for kt in range(2):
                sides = []
                for side in range(2):
                    q = 4 * kt + 2 * side + ri
                    left, right = xbuf[:, q, :TILE], xbuf[:, q, TILE:]
                    middle = jnp.where(lane >= 2 * CB, left, right)
                    sides.append([left, left, middle, right, right])
                for r in range(ROWS):
                    a = pltpu.roll(sides[0][r], (-r * CB) % TILE, 1) if r else sides[0][r]
                    b = pltpu.roll(sides[1][r], (CP - r * CB) % TILE, 1)
                    at = ri * ROWS * NLAT + r * NLAT
                    xs[at : at + NLAT, kt * TILE : (kt + 1) * TILE] = jnp.where(lane < CP, a, b)

    def scatter_lat(z):
        for ri in range(2):
            for k in range(4):
                lanes = slice(k // 2 * TILE, (k // 2 + 1) * TILE)
                p = []
                for r in range(ROWS):
                    at = ri * ROWS * NLAT + r * NLAT
                    piece = z[at : at + NLAT, lanes]
                    move = (r * CB - k % 2 * CP) % TILE
                    p.append(pltpu.roll(piece, move, 1) if move else piece)
                left = jnp.where(lane < CB, p[0], jnp.where(lane < 2 * CB, p[1], p[2]))
                right = jnp.where(lane < 16, p[2], jnp.where(lane < 64, p[3], p[4]))
                sbuf2[:, 2 * k + ri, :TILE] = left
                sbuf2[:, 2 * k + ri, TILE:] = jnp.where(lane < 112, right, 0.0)

    def lon_to_cells(which):
        both = jnp.concatenate(
            [
                jnp.transpose(zbuf[:, :, t * TILE : (t + 1) * TILE].reshape(TILE, TILE))
                for t in range(2)
            ],
            axis=0,
        )
        tiles = [None] * NCH
        for r in range(ROWS):
            a, b = TILE_FROM[r], TILE_TO[r]
            span = (b - a) * TILE
            rows = both[r * CB : (r + 1) * CB]
            part = rows_times(rows, lv[0, which, r, :, :span], lv[1, which, r, :, :span])
            for t in range(a, b):
                piece = part[:, (t - a) * TILE : (t - a + 1) * TILE]
                tiles[t] = piece if tiles[t] is None else tiles[t] + piece
        for t in range(NCH):
            cbuf[t] = tiles[t]

    def mix(v, table, layer, at, sign):
        out = []
        for t in range(2):
            q = rows_times(v[:, t * TILE : (t + 1) * TILE], table[0, layer, at], table[1, layer, at])
            re = q[:64, :TILE] - sign * q[64:, TILE:]
            im = q[64:, :TILE] + sign * q[:64, TILE:]
            out.append(jnp.concatenate([re, im], axis=0))
        return jnp.concatenate(out, axis=1)

    def bias_rows(layer, at):
        rows = [jnp.broadcast_to(fb[layer, at + ri : at + ri + 1, :], (64, TILE)) for ri in range(2)]
        both = jnp.concatenate(rows, axis=0)
        return jnp.concatenate([both, both], axis=1)

    def exchange_one(value):
        mbuf[...] = value.reshape(NCH, CB, TILE)
        copies = over_ch(lambda p: mbuf.at[p], fbuf.at[ch], c_s.at[0], c_r.at[0])
        fbuf[ch] = mbuf[ch]
        return copies

    def exchange_four():
        copies = over_ch(lambda p: cbuf.at[p], bbuf.at[ch], c_s.at[1], c_r.at[1])
        bbuf[ch] = cbuf[ch]
        return copies

    def exchange_lat(src, dst, at):
        copies = start(to_lat(lambda p: src.at[p], dst.at[lat], l_s.at[at], l_r.at[at]))
        dst[lat] = src[lat]
        return copies

    def col(layer, at):
        return pcol[layer, :, at : at + 1]

    def forward(layer, carry):
        h = h_s[...].reshape(D, TILE)
        mean = jnp.sum(h, axis=0, keepdims=True) * (1.0 / D)
        spread = jnp.sum(h * h, axis=0, keepdims=True) * (1.0 / D) - mean * mean
        rstd = lax.rsqrt(spread + norm_eps)
        n1 = (h - mean) * rstd
        n1_s[layer] = n1
        r1_s[layer] = jnp.broadcast_to(rstd, (8, TILE))
        mixed = n1 * col(layer, 0) + col(layer, 1)
        one = exchange_one(mixed)
        ig_s[...] = h + mixed
        filter_tables(layer)
        arrived(one)
        lon_to_modes(0)
        two = exchange_lat(sbuf, xbuf, 0)
        sent(one)

        @pl.when(layer < LAYERS - 1)
        def _():
            weights_start(layer + 1)

        arrived(two)
        gather_lat()
        y = table_times(la[0], la[1], xs[...])
        y_s[layer] = y
        hh = mix(y, bw, layer, 0, 1.0) + bias_rows(layer, 0)
        hh_s[layer] = hh
        b = mix(gelu_exact(hh), bw, layer, 1, 1.0) + bias_rows(layer, 2)
        t = jnp.tanh(b / shrink_level)
        t_s[layer] = t
        scatter_lat(table_times(lt[0], lt[1], b - shrink_level * t))
        three = exchange_lat(sbuf2, zbuf, 1)
        sent(two)
        weights_pass(layer)
        arrived(three)
        lon_to_cells(1)
        four = exchange_four()
        sent(three)
        weights_done(layer)
        for at in range(0, FF, CHUNK):
            wT[:, at : at + CHUNK] = jnp.transpose(wall[layer, 1, at : at + CHUNK, :])
        arrived(four)
        inner = ig_s[...] + bbuf[...].reshape(D, TILE)
        mean = jnp.sum(inner, axis=0, keepdims=True) * (1.0 / D)
        spread = jnp.sum(inner * inner, axis=0, keepdims=True) * (1.0 / D) - mean * mean
        rstd = lax.rsqrt(spread + norm_eps)
        n2 = (inner - mean) * rstd
        n2_s[layer] = n2
        r2_s[layer] = jnp.broadcast_to(rstd, (8, TILE))
        lifted = (n2 * col(layer, 2) + col(layer, 3)).astype(BF16)
        lifted_s[layer] = lifted
        total = inner + col(layer, 4)
        for at in range(0, FF, CHUNK):
            pre = mb(wall[layer, 0, at : at + CHUNK, :], lifted) + bcol[layer, at : at + CHUNK, 5:6]
            pre_s[layer, at : at + CHUNK] = pre
            hidden = gelu_exact(pre).astype(BF16)
            hid_s[layer, at : at + CHUNK] = hidden
            total = total + mb(wT[:, at : at + CHUNK], hidden)
        h_s[...] = total.reshape(NCH, CB, TILE)
        sent(four)
        return carry

    lax.fori_loop(0, LAYERS, forward, 0)
    last_h = over_ch(lambda p: h_s.at[p], out_h.at[ch], bsem_s.at[3], bsem_r.at[3])
    out_h[ch] = h_s[ch]
    done(second)
    g_s[...] = xin[1]
    ones = jnp.ones((8, TILE), F32)

    def turn_up(layer):
        for at in range(0, FF, CHUNK):
            wT[:, at : at + CHUNK] = jnp.transpose(wall[layer, 0, at : at + CHUNK, :])

    turn_up(LAYERS - 1)

    lanes_d = lax.broadcasted_iota(jnp.int32, (D, TILE), 1)
    lanes_f = lax.broadcasted_iota(jnp.int32, (CHUNK, TILE), 1)

    def cell_sums(layer, at, value):
        total = jnp.sum(value, axis=1, keepdims=True)
        held = pc[...].reshape(D, TILE)
        held = jnp.where(lanes_d == layer * 8 + at, total, held)
        pc[...] = held.reshape(NCH, CB, TILE)

    def hidden_sums(layer):
        for at in range(0, FF, CHUNK):
            total = jnp.sum(pre_s[layer, at : at + CHUNK], axis=1, keepdims=True)
            held = bc[at : at + CHUNK]
            bc[at : at + CHUNK] = jnp.where(lanes_f == layer, total, held)

    def turn_hidden_sums():
        blank = jnp.zeros((2 * TILE - FB, TILE), F32)
        for j in range(NCH):
            tall = jnp.concatenate([bc[j * FB : (j + 1) * FB], blank], axis=0)
            for t in range(2):
                turned = jnp.transpose(tall[t * TILE : (t + 1) * TILE])
                brow[j, :, t * TILE : (t + 1) * TILE] = turned[:8]

    def grads_pair(layer):
        return remote(
            psend, pget, qsem_s.at[layer], qsem_r.at[layer], {"lat": partner}
        )

    def grads_near(layer):
        return over_near(
            lambda p: gsend.at[p], gget.at[lax.rem(layer, 2), ch], gsem_s.at[layer], gsem_r.at[layer]
        )

    def grads_done(layer):
        slot = lax.rem(layer, 2)
        gget[slot, ch] = gsend[ch]
        done(grads_near(layer))
        total = gget[slot, 0].astype(F32)
        for j in range(1, NCH):
            total = total + gget[slot, j].astype(F32)
        gw[layer] = total.reshape(8, WROWS, D)

    near = lat // 2

    def sum_share(layer):
        return [
            remote(
                gw.at[layer, lat_peer[s] // 2], wget.at[layer, near],
                w1_s.at[layer, s], w1_r.at[layer, s], {"lat": lat_peer[s]},
            )
            for s in range(2, NLAT, 2)
        ]

    def sum_give(layer):
        return to_lat(
            lambda p: wsum.at[layer], wout.at[layer, core, near], w2_s.at[layer], w2_r.at[layer]
        )

    def sum_pass(layer):
        wget[layer, near] = gw[layer, near]
        done(sum_share(layer))
        total = wget[layer, 0]
        for j in range(1, 8):
            total = total + wget[layer, j]
        wsum[layer] = total
        wout[layer, core, near] = total
        start(sum_give(layer))

    def filters_share():
        return to_lat(lambda p: gf.at[p], fget.at[lat], f_s.at[0], f_r.at[0])

    def filters_give():
        return to_lat(lambda p: fsum, sout.at[lat], f_s.at[1], f_r.at[1])

    def rows_share():
        copies = []
        for s in range(1, NCH):
            p, where = ch_peer[s], {"ch": ch_peer[s]}
            copies.append(remote(pc.at[p], pin.at[ch], bsem_s.at[5, s], bsem_r.at[5, s], where))
            copies.append(
                remote(brow.at[p], bin_s.at[ch], bsem_s.at[7, s], bsem_r.at[7, s], where)
            )
        return copies

    def rows_give():
        return to_lat(lambda p: gpsum, gpget.at[lat], f_s.at[2], f_r.at[2])

    def rows_pass():
        pin[ch] = pc[ch]
        bin_s[ch] = brow[ch]
        done(rows_share())
        total, hidden = pin[0], bin_s[0]
        for j in range(1, NCH):
            total, hidden = total + pin[j], hidden + bin_s[j]
        tall = jnp.concatenate([total, jnp.zeros((TILE - CB, TILE), F32)], axis=0)
        gpsum[:32] = jnp.transpose(tall)[:32]
        gpsum[32:40] = hidden[:, :TILE]
        gpsum[40:48] = hidden[:, TILE:]
        gpget[lat] = gpsum[...]
        start(rows_give())

    def backward(step, carry):
        layer = LAYERS - 1 - step
        g = g_s[...].reshape(D, TILE)
        g_round = g.astype(BF16)
        lift = jnp.zeros((D, TILE), F32)
        for at in range(0, FF, CHUNK):
            hidden_grad = mb(wall[layer, 1, at : at + CHUNK, :], g_round)
            pre_grad = hidden_grad * gelu_slope(pre_s[layer, at : at + CHUNK])
            pre_s[layer, at : at + CHUNK] = pre_grad
            pre_round = pre_grad.astype(BF16)
            prs[at : at + CHUNK] = pre_round
            lift = lift + mb(wT[:, at : at + CHUNK], pre_round)
        n2 = n2_s[layer]
        q2 = lift * col(layer, 2)
        m1 = jnp.sum(q2, axis=0, keepdims=True) * (1.0 / D)
        m2 = jnp.sum(q2 * n2, axis=0, keepdims=True) * (1.0 / D)
        inner_grad = g + r2_s[layer, 0:1, :] * (q2 - m1 - n2 * m2)
        one = exchange_one(inner_grad)
        ig_s[...] = inner_grad
        lifted = lifted_s[layer]
        for at in range(0, FF, CHUNK):
            gr[1, at : at + CHUNK] = mb(hid_s[layer, at : at + CHUNK], g_round, NT)
            gr[0, at : at + CHUNK] = mb(prs[at : at + CHUNK], lifted, NT)
        psend[...] = gr[1 - core].astype(BF16)
        grads_pair(layer).start()
        cell_sums(layer, 4, g)
        cell_sums(layer, 2, lift * n2)
        cell_sums(layer, 3, lift)
        arrived(one)
        lon_to_modes(1)
        two = exchange_lat(sbuf, xbuf, 0)
        sent(one)

        @pl.when(layer < LAYERS - 1)
        def _():
            grads_done(layer + 1)
            start(sum_share(layer + 1))

        grads_pair(layer).wait()
        gsend[...] = (gr[core] + pget[...].astype(F32)).astype(BF16).reshape(NCH, FB, D)
        start(grads_near(layer))
        hidden_sums(layer)
        arrived(two)
        gather_lat()
        t = t_s[layer]
        db = table_times(la[0], la[1], xs[...]) * (t * t)
        hh = hh_s[layer]
        dh = mix(db, bt, layer, 1, -1.0) * gelu_slope(hh)
        dy = mix(dh, bt, layer, 0, -1.0)
        scatter_lat(table_times(lt[0], lt[1], dy))
        three = exchange_lat(sbuf2, zbuf, 1)
        sent(two)

        def filter_grads(at, left, right):
            turned = jnp.concatenate([right[64:], -right[:64]], axis=0)
            total = jnp.zeros((TILE, 2 * TILE), F32)
            for tt in range(2):
                lanes = slice(tt * TILE, (tt + 1) * TILE)
                pair = jnp.concatenate([right[:, lanes], turned[:, lanes]], axis=1)
                total = total + mm(jnp.transpose(left[:, lanes]), pair)
            re = total[:64, :TILE] + swap(total[64:, :TILE])
            im = total[:64, TILE:] + swap(total[64:, TILE:])
            keep = lax.broadcasted_iota(jnp.int32, (64, TILE), 1) < CP
            value = jnp.where(keep, re, swap(im))
            base = (layer * 2 + at) * 2
            gf[base] = value[:32]
            gf[base + 1] = value[32:]
            sums = []
            for part in (right[:64], right[64:]):
                row = jnp.sum(part, axis=0, keepdims=True)
                row = row[:, :TILE] + row[:, TILE:]
                sums.append(row + swap(row))
            gf[base + 1, 16:17, :] = jnp.where(keep[:1], sums[0], sums[1])

        filter_grads(1, gelu_exact(hh), db)
        filter_grads(0, y_s[layer], dh)

        @pl.when(layer > 0)
        def _():
            turn_up(layer - 1)

        @pl.when(layer == 0)
        def _():
            start(filters_share())
            turn_hidden_sums()
            start(rows_share())

        arrived(three)
        lon_to_cells(0)
        four = exchange_four()
        sent(three)

        @pl.when(layer < LAYERS - 1)
        def _():
            sum_pass(layer + 1)

        @pl.when(layer == 0)
        def _():
            fget[lat] = gf[lat]
            done(filters_share())
            total = fget[0]
            for j in range(1, NLAT):
                total = total + fget[j]
            fsum[...] = total
            sout[lat] = total
            start(filters_give())
            rows_pass()
            grads_done(0)
            start(sum_share(0))

        arrived(four)
        inner_grad = ig_s[...]
        mixed_grad = inner_grad + bbuf[...].reshape(D, TILE)
        n1 = n1_s[layer]
        q1 = mixed_grad * col(layer, 0)
        m1 = jnp.sum(q1, axis=0, keepdims=True) * (1.0 / D)
        m2 = jnp.sum(q1 * n1, axis=0, keepdims=True) * (1.0 / D)
        g = inner_grad + r1_s[layer, 0:1, :] * (q1 - m1 - n1 * m2)
        g_s[...] = g.reshape(NCH, CB, TILE)
        mg_s[...] = mixed_grad

        @pl.when(layer > 0)
        def _():
            cell_sums(layer, 0, mixed_grad * n1)
            cell_sums(layer, 1, mixed_grad)

        sent(four)
        return carry

    lax.fori_loop(0, LAYERS, backward, 0)
    final = over_ch(lambda p: g_s.at[p], out_g.at[ch], bsem_s.at[4], bsem_r.at[4])
    out_g[ch] = g_s[ch]
    mixed_grad = mg_s[...]
    for at, value in enumerate((mixed_grad * n1_s[0], mixed_grad)):
        for j in range(NCH):
            part = mm(ones, value[j * CB : (j + 1) * CB], NT)
            late[j, at : at + 1, 0:CB] = part[0:1]
    late_copies = over_ch(lambda p: late.at[p], lin.at[ch], bsem_s.at[6], bsem_r.at[6])
    lin[ch] = late[ch]
    sum_pass(0)
    done(late_copies)
    total = lin[0]
    for j in range(1, NCH):
        total = total + lin[j]
    lsum[...] = total
    lget[lat] = total
    give_late = start(to_lat(lambda p: lsum, lget.at[lat], f_s.at[3], f_r.at[3]))
    done(last_h)
    done(final)
    done(filters_give())
    for layer in range(LAYERS):
        done(sum_give(layer))
    done(rows_give())
    total = gpget[0]
    for j in range(1, NLAT):
        total = total + gpget[j]
    rout[...] = total
    done(give_late)
    total = lget[0]
    for j in range(1, NLAT):
        total = total + lget[j]
    eout[...] = total


def run_stack(*args):
    shapes = [
        jax.ShapeDtypeStruct((NCH, CB, TILE), F32),
        jax.ShapeDtypeStruct((NCH, CB, TILE), F32),
        jax.ShapeDtypeStruct((LAYERS, 2, 8, WROWS, D), F32),
        jax.ShapeDtypeStruct((NLAT, 32, TILE), F32),
        jax.ShapeDtypeStruct((48, TILE), F32),
        jax.ShapeDtypeStruct((8, TILE), F32),
    ]
    v = pltpu.VMEM
    dma = pltpu.SemaphoreType.DMA
    scratch = [
        v((NCH, CB, TILE), F32),
        v((NCH, CB, TILE), F32),
        v((2, NCH, CB, TILE), F32),
        v((NCH, 32, 256), F32),
        v((LAYERS, D, TILE), F32),
        v((LAYERS, FF, TILE), F32),
        v((NCH, CB, TILE), F32),
        v((NCH, CB, TILE), F32),
        v((NLAT, 8, 2 * TILE), F32),
        v((NLAT, 8, 2 * TILE), F32),
        v((NLAT, 8, 2 * TILE), F32),
        v((NLAT, 8, 2 * TILE), F32),
        v((NCH, CB, TILE), F32),
        v((NCH, CB, TILE), F32),
        v((LAYERS, 2, FF, D), BF16),
        v((D, FF), BF16),
        v((LAYERS, D, TILE), F32),
        v((LAYERS, D, TILE), F32),
        v((LAYERS, 8, TILE), F32),
        v((LAYERS, 8, TILE), F32),
        v((LAYERS, D, TILE), BF16),
        v((LAYERS, FF, TILE), F32),
        v((LAYERS, FF, TILE), BF16),
        v((LAYERS, TILE, 256), F32),
        v((LAYERS, TILE, 256), F32),
        v((LAYERS, TILE, 256), F32),
        v((2 * ROWS * NLAT, 256), F32),
        v((FF, TILE), BF16),
        v((2, FF, D), F32),
        v((FF, D), BF16),
        v((FF, D), BF16),
        v((NCH, FB, D), BF16),
        v((2, NCH, FB, D), BF16),
        v((NCH, CB, TILE), F32),
        v((NCH, CB, TILE), F32),
        v((FF, TILE), F32),
        v((NCH, 8, 256), F32),
        v((NCH, 8, 256), F32),
        v((D, TILE), F32),
        v((D, TILE), F32),
        v((TILE, 256), F32),
        v((2, LAYERS, 2, TILE, 256), BF16),
        v((2, LAYERS, 2, TILE, 256), BF16),
        v((2, TILE, 2 * ROWS * NLAT), BF16),
        v((2, 2 * ROWS * NLAT, TILE), BF16),
        v((2, 2, ROWS, SPAN, TILE), BF16),
        v((2, 2, ROWS, TILE, SPAN), BF16),
        v((LAYERS, 8, WROWS, D), F32),
        v((LAYERS, 8, WROWS, D), F32),
        v((LAYERS, WROWS, D), F32),
        v((NLAT, 32, TILE), F32),
        v((NLAT, 32, TILE), F32),
        v((32, TILE), F32),
        v((48, TILE), F32),
        v((NLAT, 48, TILE), F32),
        v((NCH, 8, TILE), F32),
        v((NCH, 8, TILE), F32),
        v((8, TILE), F32),
        v((NLAT, 8, TILE), F32),
        dma((8, NCH)),
        dma((8, NCH)),
        dma((LAYERS, NCH)),
        dma((LAYERS, NCH)),
        dma((LAYERS,)),
        dma((LAYERS,)),
        dma((LAYERS, NCH)),
        dma((LAYERS, NCH)),
        dma((LAYERS,)),
        dma((LAYERS,)),
        dma((2, NCH)),
        dma((2, NCH)),
        dma((2, NLAT)),
        dma((2, NLAT)),
        dma((LAYERS, NLAT)),
        dma((LAYERS, NLAT)),
        dma((LAYERS, NLAT)),
        dma((LAYERS, NLAT)),
        dma((4, NLAT)),
        dma((4, NLAT)),
    ]
    return pl.pallas_call(
        stack_kernel,
        out_shape=shapes,
        in_specs=[pl.BlockSpec(memory_space=pltpu.VMEM)] * len(args),
        out_specs=[pl.BlockSpec(memory_space=pltpu.VMEM)] * len(shapes),
        scratch_shapes=scratch,
        compiler_params=pltpu.CompilerParams(
            collective_id=0, has_side_effects=True, vmem_limit_bytes=60 << 20
        ),
        name="stack",
    )(*args)


def two_parts(table):
    high = table.astype(ml_dtypes.bfloat16)
    return np.stack([high, (table - high.astype(np.float64)).astype(ml_dtypes.bfloat16)])


def lat_all():
    lat_cells = ROWS * NLAT
    phase = np.outer(np.arange(lat_cells), np.arange(lat_cells)) % lat_cells
    angles = phase * (2.0 * math.pi / lat_cells)

    def place(table):
        return table.reshape(lat_cells, NLAT, ROWS).transpose(0, 2, 1).reshape(lat_cells, -1)

    cos, sin = place(np.cos(angles)), place(np.sin(angles))
    table = np.block([[cos, sin], [-sin, cos]]) / math.sqrt(lat_cells)
    table = np.pad(table, ((0, 2 * TILE - 2 * lat_cells), (0, 0)))
    return two_parts(table), two_parts(np.ascontiguousarray(table.T))


def lon_all():
    modes = LON // 2 + 1
    phase = np.outer(np.arange(modes), np.arange(LON)) % LON
    angles = phase * (2.0 * math.pi / LON)
    table = np.stack([np.cos(angles), -np.sin(angles)], axis=1).reshape(2 * modes, LON)
    table = table / math.sqrt(LON)
    rows = []
    for r in range(ROWS):
        before = r * LON - TILE_FROM[r] * TILE
        rows.append(
            np.pad(table, ((0, 2 * TILE - 2 * modes), (before, SPAN - LON - before)))
        )
    cells = np.stack(rows)
    return two_parts(np.ascontiguousarray(cells.transpose(0, 2, 1))), two_parts(cells)


def body(
    inputs,
    cotangent,
    first_gain,
    first_shift,
    filter_inner,
    filter_inner_bias,
    filter_outer,
    filter_outer_bias,
    second_gain,
    second_shift,
    up_weight,
    up_bias,
    down_weight,
    down_bias,
    kept_lat,
    kept_lon,
):
    shape = inputs.shape
    cells = ROWS * LON

    def to_tiles(field):
        flat = jnp.pad(field.reshape(CB, cells), ((0, 0), (0, NCH * TILE - cells)))
        return flat.reshape(CB, NCH, TILE).transpose(1, 0, 2)

    def from_tiles(tiles):
        return tiles.transpose(1, 0, 2).reshape(CB, NCH * TILE)[:, :cells].reshape(shape)

    vectors = jnp.stack([first_gain, first_shift, second_gain, second_shift, down_bias], axis=1)
    prm = jnp.concatenate(
        [
            jnp.pad(vectors, ((0, 0), (0, 0), (0, 256 - CB))),
            jnp.pad(up_bias[:, None, :], ((0, 0), (0, 2), (0, 256 - FB))),
        ],
        axis=1,
    ).reshape(32, 256)
    shards = jnp.stack([up_weight.transpose(0, 2, 1), down_weight], axis=1)
    biases = jnp.concatenate([filter_inner_bias[:, :, 0], filter_outer_bias[:, :, 0]], axis=1)
    biases = jnp.tile(jnp.pad(biases, ((0, 0), (0, 4), (0, CP - CB))), (1, 1, 2))
    lon_index = (kept_lon[:, None] * 2 + jnp.arange(2, dtype=jnp.int32)).reshape(1, TILE)
    lat_index = jnp.pad(kept_lat, (0, 64 - kept_lat.shape[0]), constant_values=-4 * LON)
    lat_index = (jnp.arange(2, dtype=jnp.int32)[:, None] * (ROWS * NLAT) + lat_index).reshape(1, TILE)
    index = jnp.concatenate([lon_index, lat_index, jnp.zeros((6, TILE), jnp.int32)], axis=0)
    all_a, all_t = lat_all()
    all_k, all_v = lon_all()
    out_h, out_g, wout, sout, sums, edge = run_stack(
        to_tiles(inputs), to_tiles(cotangent), prm, shards,
        filter_inner.reshape(LAYERS, 2, CB, CB), filter_outer.reshape(LAYERS, 2, CB, CB),
        biases, index, all_a, all_t, all_k, all_v,
    )
    rows = sums[:32].reshape(LAYERS, 8, TILE)
    up_shift_grad = jnp.concatenate([sums[32:36], sums[40:44]], axis=1)[:, :FB]
    wout = wout.reshape(LAYERS, 2, FB, D)
    filters = sout.reshape(LAYERS, 2, CP, 2, CP).transpose(1, 0, 3, 2, 4)
    fbias = filters[:, :, :, CB, :CB]
    filters = filters[:, :, :, :CB, :CB]
    first_rows = jnp.concatenate([edge[None, :2, :CB], rows[1:, :2, :CB]], axis=0)
    return (
        from_tiles(out_h),
        from_tiles(out_g),
        first_rows[:, 0],
        first_rows[:, 1],
        filters[0][:, :, None],
        fbias[0][:, :, None],
        filters[1][:, :, None],
        fbias[1][:, :, None],
        rows[:, 2, :CB],
        rows[:, 3, :CB],
        wout[:, 0].transpose(0, 2, 1),
        up_shift_grad,
        wout[:, 1],
        rows[:, 4, :CB],
    )


def solution(mesh):
    placed = (
        P("ch", "lat", None),
        P("ch", "lat", None),
        P(None, "ch"),
        P(None, "ch"),
        P(None, None, "ch", None, None),
        P(None, None, "ch", None),
        P(None, None, "ch", None, None),
        P(None, None, "ch", None),
        P(None, "ch"),
        P(None, "ch"),
        P(None, None, "ch"),
        P(None, "ch"),
        P(None, "ch", None),
        P(None, "ch"),
        P(),
        P(),
    )
    return jax.shard_map(
        body,
        mesh=mesh,
        in_specs=placed,
        out_specs=(
            P("ch", "lat", None),
            P("ch", "lat", None),
            P(None, "ch"),
            P(None, "ch"),
            P(None, None, "ch", None, None),
            P(None, None, "ch", None),
            P(None, None, "ch", None, None),
            P(None, None, "ch", None),
            P(None, "ch"),
            P(None, "ch"),
            P(None, None, "ch"),
            P(None, "ch"),
            P(None, "ch", None),
            P(None, "ch"),
        ),
        check_vma=False,
    )
```

```python
import functools
import math

import jax
import jax.numpy as jnp
import ml_dtypes
import numpy as np
from jax import lax
from jax.experimental import pallas as pl
from jax.experimental.pallas import tpu as pltpu
from jax.sharding import PartitionSpec as P

shrink_level = 0.01
norm_eps = 1e-05
highest = lax.Precision.HIGHEST
MESH = pl.DeviceIdType.MESH
F32 = jnp.float32
BF16 = jnp.bfloat16

LAYERS = 4
NCH = 8
NLAT = 16
CB = 48
CP = 64
D = NCH * CB
ROWS = 5
LON = 180
TILE = 128
FB = 192
FF = NCH * FB
CHUNK = 384
WROWS = 32
SHARES = FB // WROWS
TILE_FROM = [r * LON // TILE for r in range(ROWS)]
TILE_TO = [-(-(r + 1) * LON // TILE) for r in range(ROWS)]
SPAN = max(b - a for a, b in zip(TILE_FROM, TILE_TO)) * TILE


def gelu_exact(values):
    return 0.5 * values * (1.0 + lax.erf(values * 0.7071067811865476))


def gelu_slope(values):
    return (
        0.5 * (1.0 + lax.erf(values * 0.7071067811865476))
        + values * jnp.exp(-0.5 * values * values) * 0.3989422804014327
    )


def mm(a, b, dims=((1,), (0,)), precision=highest):
    return lax.dot_general(a, b, (dims, ((), ())), precision=precision, preferred_element_type=F32)


def mb(a, b, dims=((1,), (0,))):
    return lax.dot_general(a, b, (dims, ((), ())), preferred_element_type=F32)


NT = ((1,), (1,))


def split(value):
    high = value.astype(BF16)
    return high, (value - high.astype(F32)).astype(BF16)


def rows_times(value, high, low):
    vh, vl = split(value)
    n = value.shape[0]
    both = mb(jnp.concatenate([vh, vl], axis=0), high)
    return both[:n] + both[n:] + mb(vh, low)


def table_times(high, low, value):
    vh, vl = split(value)
    n = value.shape[1]
    both = mb(high, jnp.concatenate([vh, vl], axis=1))
    return both[:, :n] + both[:, n:] + mb(low, vh)


def stack_kernel(
    x0, ct, prm, wsh, fi, fo, fb, idx, all_a, all_t, all_k, all_v,
    out_h, out_g, wout, sout, rout,
    h_s, g_s, xin, pbuf, pcol, bcol, mbuf, fbuf, sbuf, sbuf2, xbuf, zbuf, cbuf, bbuf,
    wall, wT, n1_s, n2_s, r1_s, r2_s, lifted_s, pre_s, hid_s, y_s, hh_s, t_s,
    xs, prs, gr, psend, pget, gsend, gget, pc, pin, bc, brow, bin_s, pr, ig_s, igr, mixr_s, bwf, k_s, v_s,
    bw, bt, la, lt, lk, lv,
    gw, wget, wsum, gf, fget, fsum, gpsum, gpget,
    bsem_s, bsem_r, asem_s, asem_r, psem_s, psem_r, gsem_s, gsem_r, qsem_s, qsem_r,
    c_s, c_r, l_s, l_r, t_sem, w1_s, w1_r, w2_s, w2_r, f_s, f_r,
):
    ch = lax.axis_index("ch")
    lat = lax.axis_index("lat")
    core = lax.rem(lat, 2)
    partner = lat + 1 - 2 * core


    def flipped(at):
        return at + 2 - 4 * lax.rem(at // 2, 2)

    flip = flipped(lat)
    half = lax.rem(ch, 2)
    rank = lat + half * (flip - lat)
    ch_peer = [lax.rem(ch + s, NCH) for s in range(NCH)]
    lat_peer = [lax.rem(lat + s, NLAT) for s in range(NLAT)]

    barrier = pltpu.get_barrier_semaphore()
    for s in range(1, NCH):
        pl.semaphore_signal(barrier, inc=1, device_id={"ch": ch_peer[s]}, device_id_type=MESH)
        pl.semaphore_signal(
            barrier, inc=1, device_id={"lat": flip, "ch": ch_peer[s]}, device_id_type=MESH
        )
    for s in range(1, NLAT):
        pl.semaphore_signal(barrier, inc=1, device_id={"lat": lat_peer[s]}, device_id_type=MESH)

    def remote(src, dst, send, recv, where):
        return pltpu.make_async_remote_copy(
            src_ref=src, dst_ref=dst, send_sem=send, recv_sem=recv,
            device_id=where, device_id_type=MESH,
        )

    def over_near(src, dst, send, recv):
        copies = []
        for s in range(1, NCH):
            where = {"lat": flip, "ch": ch_peer[s]} if s % 2 else {"ch": ch_peer[s]}
            copies.append(remote(src(ch_peer[s]), dst, send.at[s], recv.at[s], where))
        return copies

    def between(src, dst, at, inward):
        copies = []
        for s in range(NCH):
            there = lat + lax.rem(half + s, 2) * (flip - lat) if inward else rank
            where = {"lat": there, "ch": ch_peer[s]}
            copies.append(remote(src(ch_peer[s]), dst, bsem_s.at[at, s], bsem_r.at[at, s], where))
        return copies

    def between_start(src, dst, at, inward, keep):
        copies = between(src, dst, at, inward)
        for copy in copies[1:]:
            copy.start()

        @pl.when(half == 1)
        def _():
            copies[0].start()

        @pl.when(half == 0)
        def _():
            keep()

        return copies

    def between_done(copies):
        for copy in copies[1:]:
            copy.wait()

        @pl.when(half == 1)
        def _():
            copies[0].wait()

    def to_lat(src, dst, send, recv):
        return [
            remote(src(lat_peer[s]), dst, send.at[s], recv.at[s], {"lat": lat_peer[s]})
            for s in range(1, NLAT)
        ]

    def start(copies):
        for copy in copies:
            copy.start()
        return copies

    def arrived(copies):
        for copy in copies:
            copy.wait_recv()

    def sent(copies):
        for copy in copies:
            copy.wait_send()

    def done(copies):
        for copy in copies:
            copy.wait()

    def weights_near(layer):
        mine = wall.at[layer, core, pl.ds(pl.multiple_of(ch * FB, FB), FB)]
        return over_near(
            lambda p: wsh.at[layer, core], mine, asem_s.at[layer], asem_r.at[layer]
        )

    def weights_pair(layer):
        block = wall.at[layer, core]
        return remote(block, block, psem_s.at[layer], psem_r.at[layer], {"lat": partner})

    def own_weights(layer):
        mine = wall.at[layer, core, pl.ds(pl.multiple_of(ch * FB, FB), FB)]
        return pltpu.make_async_copy(wsh.at[layer, core], mine, t_sem.at[2 + layer])

    def weights_start(layer):
        for copy in weights_near(layer):
            copy.start()
        own_weights(layer).start()

    def weights_pass(layer):
        done(weights_near(layer))
        own_weights(layer).wait()
        weights_pair(layer).start()

    def weights_done(layer):
        weights_pair(layer).wait()

    get_k = pltpu.make_async_copy(all_k, k_s, t_sem.at[0])
    get_v = pltpu.make_async_copy(all_v, v_s, t_sem.at[1])
    get_k.start()
    get_v.start()
    pbuf[ch] = prm[...]
    pl.semaphore_wait(barrier, 2 * (NCH - 1) + NLAT - 1)

    def keep_x():
        xin[0, ch] = x0[ch]

    def keep_ct():
        xin[1, ch] = ct[ch]

    first = between_start(lambda p: x0.at[p], xin.at[0, ch], 0, True, keep_x)
    params = start(over_near(lambda p: prm, pbuf.at[ch], bsem_s.at[1], bsem_r.at[1]))
    weights_start(0)
    pc[...] = jnp.zeros(pc.shape, F32)
    bc[...] = jnp.zeros(bc.shape, F32)
    pr[...] = jnp.zeros(pr.shape, F32)
    bwf[...] = jnp.zeros(bwf.shape, F32)

    def picker(at):
        rows = lax.broadcasted_iota(jnp.int32, (2 * TILE, TILE), 0)
        return jnp.where(rows == idx[at : at + 1, :], 1.0, 0.0)

    def turn(pick):
        return jnp.concatenate([jnp.transpose(pick[:TILE]), jnp.transpose(pick[TILE:])], axis=1)

    ends = (idx[0:1, :] < 2) | (idx[0:1, :] >= 180)
    mode_weight = jnp.where(ends, 1.0, 2.0)

    def first_tables():
        get_k.wait()
        pick = picker(0).astype(BF16)
        for part in range(2):
            for r in range(ROWS):
                table = mb(k_s[part, r], pick)
                lk[part, 0, r] = table.astype(BF16)
                lk[part, 1, r] = (table * mode_weight).astype(BF16)

    def other_tables():
        get_v.wait()
        pick = picker(0)
        pick_t = jnp.concatenate([turn(pick), turn(pick * mode_weight)], axis=0).astype(BF16)
        for part in range(2):
            for r in range(ROWS):
                table = mb(pick_t, v_s[part, r]).astype(BF16)
                lv[part, 0, r] = table[:TILE]
                lv[part, 1, r] = table[TILE:]
        pick = picker(1)
        pick_t = turn(pick).astype(BF16)
        pick = pick.astype(BF16)
        for part in range(2):
            la[part] = mb(pick_t, all_a[part]).astype(BF16)
            lt[part] = mb(all_t[part], pick).astype(BF16)

    def columns(held, width, count):
        for j in range(NCH):
            turned = jnp.transpose(pbuf[j, :, :width])
            for layer in range(LAYERS):
                part = turned[:, layer * 8 : layer * 8 + 8]
                held[layer, j * count : (j + 1) * count, 0:8] = part[:count]

    first_tables()
    done(params)
    columns(pcol, TILE, CB)
    between_done(first)
    second = between_start(lambda p: ct.at[p], xin.at[1, ch], 2, True, keep_ct)
    h_s[...] = xin[0]

    lane = lax.broadcasted_iota(jnp.int32, (NLAT, TILE), 1)

    def filter_tables(layer):
        for at, weight in enumerate((fi, fo)):
            for part in range(2):
                for k in range(2):
                    lanes = part * TILE + k * CP
                    bwf[k * CP : k * CP + CB, lanes : lanes + CB] = weight[layer, part]
            table = bwf[...]
            bw[0, layer, at], bw[1, layer, at] = split(table)
            bt[0, layer, at], bt[1, layer, at] = split(
                jnp.concatenate(
                    [jnp.transpose(table[:, :TILE]), jnp.transpose(table[:, TILE:])], axis=1
                )
            )

    def swap(v):
        return pltpu.roll(v, CP, 1)

    def lon_to_modes(which):
        parts = []
        for r in range(ROWS):
            a, b = TILE_FROM[r], TILE_TO[r]
            field = jnp.concatenate([fbuf[t] for t in range(a, b)], axis=1)
            span = (b - a) * TILE
            parts.append(rows_times(field, lk[0, which, r, :span], lk[1, which, r, :span]))
        parts.append(jnp.zeros((2 * TILE - ROWS * CB, TILE), F32))
        both = jnp.concatenate(parts, axis=0)
        for t in range(2):
            turned = jnp.transpose(both[t * TILE : (t + 1) * TILE])
            sbuf[:, :, t * TILE : (t + 1) * TILE] = turned.reshape(NLAT, 8, TILE)

    def gather_lat():
        for ri in range(2):
            for kt in range(2):
                sides = []
                for side in range(2):
                    q = 4 * kt + 2 * side + ri
                    left, right = xbuf[:, q, :TILE], xbuf[:, q, TILE:]
                    middle = jnp.where(lane >= 2 * CB, left, right)
                    sides.append([left, left, middle, right, right])
                for r in range(ROWS):
                    a = pltpu.roll(sides[0][r], (-r * CB) % TILE, 1) if r else sides[0][r]
                    b = pltpu.roll(sides[1][r], (CP - r * CB) % TILE, 1)
                    at = ri * ROWS * NLAT + r * NLAT
                    xs[at : at + NLAT, kt * TILE : (kt + 1) * TILE] = jnp.where(lane < CP, a, b)

    def scatter_lat(z):
        for ri in range(2):
            for k in range(4):
                lanes = slice(k // 2 * TILE, (k // 2 + 1) * TILE)
                p = []
                for r in range(ROWS):
                    at = ri * ROWS * NLAT + r * NLAT
                    piece = z[at : at + NLAT, lanes]
                    move = (r * CB - k % 2 * CP) % TILE
                    p.append(pltpu.roll(piece, move, 1) if move else piece)
                left = jnp.where(lane < CB, p[0], jnp.where(lane < 2 * CB, p[1], p[2]))
                right = jnp.where(lane < 16, p[2], jnp.where(lane < 64, p[3], p[4]))
                sbuf2[:, 2 * k + ri, :TILE] = left
                sbuf2[:, 2 * k + ri, TILE:] = jnp.where(lane < 112, right, 0.0)

    def lon_to_cells(which):
        both = jnp.concatenate(
            [
                jnp.transpose(zbuf[:, :, t * TILE : (t + 1) * TILE].reshape(TILE, TILE))
                for t in range(2)
            ],
            axis=0,
        )
        tiles = [None] * NCH
        for r in range(ROWS):
            a, b = TILE_FROM[r], TILE_TO[r]
            span = (b - a) * TILE
            rows = both[r * CB : (r + 1) * CB]
            part = rows_times(rows, lv[0, which, r, :, :span], lv[1, which, r, :, :span])
            for t in range(a, b):
                piece = part[:, (t - a) * TILE : (t - a + 1) * TILE]
                tiles[t] = piece if tiles[t] is None else tiles[t] + piece
        for t in range(NCH):
            cbuf[t] = tiles[t]

    def mix(v, table, layer, at, sign):
        out = []
        for t in range(2):
            q = rows_times(v[:, t * TILE : (t + 1) * TILE], table[0, layer, at], table[1, layer, at])
            re = q[:64, :TILE] - sign * q[64:, TILE:]
            im = q[64:, :TILE] + sign * q[:64, TILE:]
            out.append(jnp.concatenate([re, im], axis=0))
        return jnp.concatenate(out, axis=1)

    def bias_rows(layer, at):
        rows = [jnp.broadcast_to(fb[layer, at + ri : at + ri + 1, :], (64, TILE)) for ri in range(2)]
        both = jnp.concatenate(rows, axis=0)
        return jnp.concatenate([both, both], axis=1)

    def exchange_one(value):
        mbuf[...] = value.reshape(NCH, CB, TILE)
        copies = start(over_near(lambda p: mbuf.at[p], fbuf.at[ch], c_s.at[0], c_r.at[0]))
        fbuf[ch] = mbuf[ch]
        return copies

    def exchange_four():
        copies = start(over_near(lambda p: cbuf.at[p], bbuf.at[ch], c_s.at[1], c_r.at[1]))
        bbuf[ch] = cbuf[ch]
        return copies

    def exchange_lat(src, dst, at):
        copies = []
        for s in range(1, NLAT):
            peer = lax.rem(rank + s, NLAT)
            there = peer + half * (flipped(peer) - peer)
            copies.append(
                remote(src.at[peer], dst.at[rank], l_s.at[at, s], l_r.at[at, s], {"lat": there})
            )
        start(copies)
        dst[rank] = src[rank]
        return copies

    def col(layer, at):
        return pcol[layer, :, at : at + 1]

    def forward(layer, carry):
        h = h_s[...].reshape(D, TILE)
        mean = jnp.sum(h, axis=0, keepdims=True) * (1.0 / D)
        spread = jnp.sum(h * h, axis=0, keepdims=True) * (1.0 / D) - mean * mean
        rstd = lax.rsqrt(spread + norm_eps)
        n1 = (h - mean) * rstd
        n1_s[layer] = n1
        r1_s[layer] = jnp.broadcast_to(rstd, (8, TILE))
        mixed = n1 * col(layer, 0) + col(layer, 1)
        one = exchange_one(mixed)
        ig_s[...] = h + mixed

        @pl.when(layer == 0)
        def _():
            other_tables()

        filter_tables(layer)
        arrived(one)
        lon_to_modes(0)
        two = exchange_lat(sbuf, xbuf, 0)
        sent(one)
        mixr_s[layer] = fbuf[...]

        @pl.when(layer == 0)
        def _():
            columns(bcol, 256, FB)

        @pl.when(layer < LAYERS - 1)
        def _():
            weights_start(layer + 1)

        arrived(two)
        gather_lat()
        y = table_times(la[0], la[1], xs[...])
        y_s[layer] = y
        hh = mix(y, bw, layer, 0, 1.0) + bias_rows(layer, 0)
        hh_s[layer] = hh
        b = mix(gelu_exact(hh), bw, layer, 1, 1.0) + bias_rows(layer, 2)
        t = jnp.tanh(b / shrink_level)
        t_s[layer] = t
        scatter_lat(table_times(lt[0], lt[1], b - shrink_level * t))
        three = exchange_lat(sbuf2, zbuf, 1)
        sent(two)
        weights_pass(layer)
        arrived(three)
        lon_to_cells(1)
        four = exchange_four()
        sent(three)
        weights_done(layer)
        for at in range(0, FF, CHUNK):
            wT[:, at : at + CHUNK] = jnp.transpose(wall[layer, 1, at : at + CHUNK, :])
        arrived(four)
        inner = ig_s[...] + bbuf[...].reshape(D, TILE)
        mean = jnp.sum(inner, axis=0, keepdims=True) * (1.0 / D)
        spread = jnp.sum(inner * inner, axis=0, keepdims=True) * (1.0 / D) - mean * mean
        rstd = lax.rsqrt(spread + norm_eps)
        n2 = (inner - mean) * rstd
        n2_s[layer] = n2
        r2_s[layer] = jnp.broadcast_to(rstd, (8, TILE))
        lifted = (n2 * col(layer, 2) + col(layer, 3)).astype(BF16)
        lifted_s[layer] = lifted
        total = inner + col(layer, 4)
        for at in range(0, FF, CHUNK):
            pre = mb(wall[layer, 0, at : at + CHUNK, :], lifted) + bcol[layer, at : at + CHUNK, 5:6]
            pre_s[layer, at : at + CHUNK] = pre
            hidden = gelu_exact(pre).astype(BF16)
            hid_s[layer, at : at + CHUNK] = hidden
            total = total + mb(wT[:, at : at + CHUNK], hidden)
        h_s[...] = total.reshape(NCH, CB, TILE)
        sent(four)
        return carry

    lax.fori_loop(0, LAYERS, forward, 0)

    def keep_h():
        out_h[ch] = h_s[ch]

    def keep_g():
        out_g[ch] = g_s[ch]

    last_h = between_start(lambda p: h_s.at[p], out_h.at[ch], 3, False, keep_h)
    between_done(second)
    g_s[...] = xin[1]
    ones = jnp.ones((8, TILE), F32)

    def turn_up(layer):
        for at in range(0, FF, CHUNK):
            wT[:, at : at + CHUNK] = jnp.transpose(wall[layer, 0, at : at + CHUNK, :])

    turn_up(LAYERS - 1)

    lanes_d = lax.broadcasted_iota(jnp.int32, (D, TILE), 1)
    lanes_f = lax.broadcasted_iota(jnp.int32, (CHUNK, TILE), 1)

    def cell_sums(layer, at, value):
        total = jnp.sum(value, axis=1, keepdims=True)
        held = pc[...].reshape(D, TILE)
        held = jnp.where(lanes_d == layer * 8 + at, total, held)
        pc[...] = held.reshape(NCH, CB, TILE)

    def hidden_sums(layer):
        for at in range(0, FF, CHUNK):
            total = jnp.sum(pre_s[layer, at : at + CHUNK], axis=1, keepdims=True)
            held = bc[at : at + CHUNK]
            bc[at : at + CHUNK] = jnp.where(lanes_f == layer, total, held)

    def turn_hidden_sums():
        blank = jnp.zeros((2 * TILE - FB, TILE), F32)
        for j in range(NCH):
            tall = jnp.concatenate([bc[j * FB : (j + 1) * FB], blank], axis=0)
            for t in range(2):
                turned = jnp.transpose(tall[t * TILE : (t + 1) * TILE])
                brow[j, :, t * TILE : (t + 1) * TILE] = turned[:8]

    def grads_pair(layer):
        return remote(
            psend, pget, qsem_s.at[layer], qsem_r.at[layer], {"lat": partner}
        )

    def grads_near(layer):
        return over_near(
            lambda p: gsend.at[p], gget.at[lax.rem(layer, 2), ch], gsem_s.at[layer], gsem_r.at[layer]
        )

    def grads_done(layer):
        slot = lax.rem(layer, 2)
        gget[slot, ch] = gsend[ch]
        done(grads_near(layer))
        total = gget[slot, 0].astype(F32)
        for j in range(1, NCH):
            total = total + gget[slot, j].astype(F32)
        gw[layer] = total.astype(BF16).reshape(SHARES, WROWS, D)

    near = lat // 2
    evens = range(2, NLAT, 2)

    def sum_share(layer):
        for s in evens:
            there = lat_peer[s] // 2

            @pl.when(there < SHARES)
            def _():
                share_copy(layer, s).start()

    def share_copy(layer, s):
        return remote(
            gw.at[layer, lat_peer[s] // 2], wget.at[layer, near],
            w1_s.at[layer, s], w1_r.at[layer, s], {"lat": lat_peer[s]},
        )

    def arriving(layer, s):
        return remote(
            wget.at[layer, near], wget.at[layer, near],
            w1_s.at[layer, s], w1_r.at[layer, s], {"lat": lat_peer[s]},
        )

    def give_copy(layer, s):
        return remote(
            wsum.at[layer], wout.at[core, layer, near],
            w2_s.at[layer, s], w2_r.at[layer, s], {"lat": lat_peer[s]},
        )

    def given(layer, s):
        return remote(
            wsum.at[layer], wsum.at[layer],
            w2_s.at[layer, s], w2_r.at[layer, s], {"lat": lat_peer[s]},
        )

    def sum_pass(layer):
        for s in evens:

            @pl.when(lat_peer[s] // 2 < SHARES)
            def _():
                share_copy(layer, s).wait_send()

        @pl.when(near < SHARES)
        def _():
            wget[layer, near] = gw[layer, near]
            for s in evens:
                arriving(layer, s).wait_recv()
            total = wget[layer, 0].astype(F32)
            for j in range(1, 8):
                total = total + wget[layer, j].astype(F32)
            wsum[layer] = total.astype(BF16)
            for s in evens:
                give_copy(layer, s).start()
            wout[core, layer, near] = wsum[layer]

    def hand_copy(layer):
        whole = wout.at[core, layer]
        return remote(whole, whole, w2_s.at[layer, 0], w2_r.at[layer, 0], {"lat": partner})

    def sum_hand(layer):
        @pl.when(near < SHARES)
        def _():
            for s in evens:
                give_copy(layer, s).wait_send()

        for s in evens:

            @pl.when(lax.rem(near + 8 - s // 2, 8) < SHARES)
            def _():
                given(layer, s).wait_recv()

        hand_copy(layer).start()

    def filters_share():
        return to_lat(lambda p: gf.at[p], fget.at[lat], f_s.at[0], f_r.at[0])

    def filters_give():
        return to_lat(lambda p: fsum, sout.at[lat], f_s.at[1], f_r.at[1])

    def rows_share():
        copies = []
        for s in range(1, NCH):
            p = ch_peer[s]
            where = {"lat": flip, "ch": p} if s % 2 else {"ch": p}
            copies.append(remote(pc.at[p], pin.at[ch], bsem_s.at[5, s], bsem_r.at[5, s], where))
            copies.append(
                remote(brow.at[p], bin_s.at[ch], bsem_s.at[7, s], bsem_r.at[7, s], where)
            )
        return copies

    def rows_give():
        return to_lat(lambda p: gpsum, gpget.at[lat], f_s.at[2], f_r.at[2])

    def rows_pass():
        pin[ch] = pc[ch]
        bin_s[ch] = brow[ch]
        done(rows_share())
        total, hidden = pin[0] + pr[...], bin_s[0]
        for j in range(1, NCH):
            total, hidden = total + pin[j], hidden + bin_s[j]
        tall = jnp.concatenate([total, jnp.zeros((TILE - CB, TILE), F32)], axis=0)
        gpsum[:32] = jnp.transpose(tall)[:32]
        gpsum[32:40] = hidden[:, :TILE]
        gpsum[40:48] = hidden[:, TILE:]
        gpget[lat] = gpsum[...]
        start(rows_give())

    def backward(step, carry):
        layer = LAYERS - 1 - step
        g = g_s[...].reshape(D, TILE)
        g_round = g.astype(BF16)
        lift = jnp.zeros((D, TILE), F32)
        for at in range(0, FF, CHUNK):
            hidden_grad = mb(wall[layer, 1, at : at + CHUNK, :], g_round)
            pre_grad = hidden_grad * gelu_slope(pre_s[layer, at : at + CHUNK])
            pre_s[layer, at : at + CHUNK] = pre_grad
            pre_round = pre_grad.astype(BF16)
            prs[at : at + CHUNK] = pre_round
            lift = lift + mb(wT[:, at : at + CHUNK], pre_round)
        n2 = n2_s[layer]
        q2 = lift * col(layer, 2)
        m1 = jnp.sum(q2, axis=0, keepdims=True) * (1.0 / D)
        m2 = jnp.sum(q2 * n2, axis=0, keepdims=True) * (1.0 / D)
        inner_grad = g + r2_s[layer, 0:1, :] * (q2 - m1 - n2 * m2)
        one = exchange_one(inner_grad)
        ig_s[...] = inner_grad
        lifted = lifted_s[layer]
        for at in range(0, FF, CHUNK):
            gr[1, at : at + CHUNK] = mb(hid_s[layer, at : at + CHUNK], g_round, NT)
            gr[0, at : at + CHUNK] = mb(prs[at : at + CHUNK], lifted, NT)
        psend[...] = gr[1 - core].astype(BF16)
        grads_pair(layer).start()
        cell_sums(layer, 4, g)
        cell_sums(layer, 2, lift * n2)
        cell_sums(layer, 3, lift)
        arrived(one)
        lon_to_modes(1)
        two = exchange_lat(sbuf, xbuf, 0)
        sent(one)
        igr[...] = fbuf[...]

        @pl.when(layer < LAYERS - 1)
        def _():
            grads_done(layer + 1)
            sum_share(layer + 1)

        @pl.when(layer < LAYERS - 2)
        def _():
            sum_hand(layer + 2)

        grads_pair(layer).wait()
        gsend[...] = (gr[core] + pget[...].astype(F32)).astype(BF16).reshape(NCH, FB, D)
        start(grads_near(layer))
        hidden_sums(layer)
        arrived(two)
        gather_lat()
        t = t_s[layer]
        db = table_times(la[0], la[1], xs[...]) * (t * t)
        hh = hh_s[layer]
        dh = mix(db, bt, layer, 1, -1.0) * gelu_slope(hh)
        dy = mix(dh, bt, layer, 0, -1.0)
        scatter_lat(table_times(lt[0], lt[1], dy))
        three = exchange_lat(sbuf2, zbuf, 1)
        sent(two)

        def filter_grads(at, left, right):
            turned = jnp.concatenate([right[64:], -right[:64]], axis=0)
            total = jnp.zeros((TILE, 2 * TILE), F32)
            for tt in range(2):
                lanes = slice(tt * TILE, (tt + 1) * TILE)
                pair = jnp.concatenate([right[:, lanes], turned[:, lanes]], axis=1)
                total = total + mm(jnp.transpose(left[:, lanes]), pair)
            re = total[:64, :TILE] + swap(total[64:, :TILE])
            im = total[:64, TILE:] + swap(total[64:, TILE:])
            keep = lax.broadcasted_iota(jnp.int32, (64, TILE), 1) < CP
            value = jnp.where(keep, re, swap(im))
            base = (layer * 2 + at) * 2
            gf[base] = value[:32]
            gf[base + 1] = value[32:]
            sums = []
            for part in (right[:64], right[64:]):
                row = jnp.sum(part, axis=0, keepdims=True)
                row = row[:, :TILE] + row[:, TILE:]
                sums.append(row + swap(row))
            gf[base + 1, 16:17, :] = jnp.where(keep[:1], sums[0], sums[1])

        filter_grads(1, gelu_exact(hh), db)
        filter_grads(0, y_s[layer], dh)

        @pl.when(layer > 0)
        def _():
            turn_up(layer - 1)

        @pl.when(layer == 0)
        def _():
            start(filters_share())
            turn_hidden_sums()
            start(rows_share())

        arrived(three)
        lon_to_cells(0)
        four = exchange_four()
        sent(three)
        both = igr[...] + cbuf[...]
        plain = jnp.sum(jnp.sum(both, axis=0), axis=1, keepdims=True)
        cross = jnp.sum(jnp.sum(both * mixr_s[layer], axis=0), axis=1, keepdims=True)
        lanes_c = lax.broadcasted_iota(jnp.int32, (CB, TILE), 1) - layer * 8
        pr[...] = jnp.where(lanes_c == 0, plain, jnp.where(lanes_c == 1, cross, pr[...]))

        @pl.when(layer < LAYERS - 1)
        def _():
            sum_pass(layer + 1)

        @pl.when(layer == 0)
        def _():
            fget[lat] = gf[lat]
            done(filters_share())
            total = fget[0]
            for j in range(1, NLAT):
                total = total + fget[j]
            fsum[...] = total
            sout[lat] = total
            start(filters_give())
            rows_pass()
            grads_done(0)
            sum_share(0)

        arrived(four)
        inner_grad = ig_s[...]
        mixed_grad = inner_grad + bbuf[...].reshape(D, TILE)
        n1 = n1_s[layer]
        q1 = mixed_grad * col(layer, 0)
        m1 = jnp.sum(q1, axis=0, keepdims=True) * (1.0 / D)
        m2 = jnp.sum(q1 * n1, axis=0, keepdims=True) * (1.0 / D)
        g = inner_grad + r1_s[layer, 0:1, :] * (q1 - m1 - n1 * m2)
        g_s[...] = g.reshape(NCH, CB, TILE)
        sent(four)
        return carry

    lax.fori_loop(0, LAYERS, backward, 0)
    final = between_start(lambda p: g_s.at[p], out_g.at[ch], 4, False, keep_g)
    sum_hand(1)
    sum_pass(0)
    sum_hand(0)
    between_done(last_h)
    between_done(final)
    done(filters_give())
    for layer in range(LAYERS):
        hand_copy(layer).wait()
    done(rows_give())
    total = gpget[0]
    for j in range(1, NLAT):
        total = total + gpget[j]
    rout[...] = total


def run_stack(*args):
    shapes = [
        jax.ShapeDtypeStruct((NCH, CB, TILE), F32),
        jax.ShapeDtypeStruct((NCH, CB, TILE), F32),
        jax.ShapeDtypeStruct((2, LAYERS, SHARES, WROWS, D), BF16),
        jax.ShapeDtypeStruct((NLAT, 32, TILE), F32),
        jax.ShapeDtypeStruct((48, TILE), F32),
    ]
    v = pltpu.VMEM
    dma = pltpu.SemaphoreType.DMA
    scratch = [
        v((NCH, CB, TILE), F32),
        v((NCH, CB, TILE), F32),
        v((2, NCH, CB, TILE), F32),
        v((NCH, 32, 256), F32),
        v((LAYERS, D, TILE), F32),
        v((LAYERS, FF, TILE), F32),
        v((NCH, CB, TILE), F32),
        v((NCH, CB, TILE), F32),
        v((NLAT, 8, 2 * TILE), F32),
        v((NLAT, 8, 2 * TILE), F32),
        v((NLAT, 8, 2 * TILE), F32),
        v((NLAT, 8, 2 * TILE), F32),
        v((NCH, CB, TILE), F32),
        v((NCH, CB, TILE), F32),
        v((LAYERS, 2, FF, D), BF16),
        v((D, FF), BF16),
        v((LAYERS, D, TILE), F32),
        v((LAYERS, D, TILE), F32),
        v((LAYERS, 8, TILE), F32),
        v((LAYERS, 8, TILE), F32),
        v((LAYERS, D, TILE), BF16),
        v((LAYERS, FF, TILE), F32),
        v((LAYERS, FF, TILE), BF16),
        v((LAYERS, TILE, 256), F32),
        v((LAYERS, TILE, 256), F32),
        v((LAYERS, TILE, 256), F32),
        v((2 * ROWS * NLAT, 256), F32),
        v((FF, TILE), BF16),
        v((2, FF, D), F32),
        v((FF, D), BF16),
        v((FF, D), BF16),
        v((NCH, FB, D), BF16),
        v((2, NCH, FB, D), BF16),
        v((NCH, CB, TILE), F32),
        v((NCH, CB, TILE), F32),
        v((FF, TILE), F32),
        v((NCH, 8, 256), F32),
        v((NCH, 8, 256), F32),
        v((CB, TILE), F32),
        v((D, TILE), F32),
        v((NCH, CB, TILE), F32),
        v((LAYERS, NCH, CB, TILE), F32),
        v((TILE, 256), F32),
        v((2, ROWS, SPAN, 256), BF16),
        v((2, ROWS, 256, SPAN), BF16),
        v((2, LAYERS, 2, TILE, 256), BF16),
        v((2, LAYERS, 2, TILE, 256), BF16),
        v((2, TILE, 2 * ROWS * NLAT), BF16),
        v((2, 2 * ROWS * NLAT, TILE), BF16),
        v((2, 2, ROWS, SPAN, TILE), BF16),
        v((2, 2, ROWS, TILE, SPAN), BF16),
        v((LAYERS, SHARES, WROWS, D), BF16),
        v((LAYERS, 8, WROWS, D), BF16),
        v((LAYERS, WROWS, D), BF16),
        v((NLAT, 32, TILE), F32),
        v((NLAT, 32, TILE), F32),
        v((32, TILE), F32),
        v((48, TILE), F32),
        v((NLAT, 48, TILE), F32),
        dma((8, NCH)),
        dma((8, NCH)),
        dma((LAYERS, NCH)),
        dma((LAYERS, NCH)),
        dma((LAYERS,)),
        dma((LAYERS,)),
        dma((LAYERS, NCH)),
        dma((LAYERS, NCH)),
        dma((LAYERS,)),
        dma((LAYERS,)),
        dma((2, NCH)),
        dma((2, NCH)),
        dma((2, NLAT)),
        dma((2, NLAT)),
        dma((2 + LAYERS,)),
        dma((LAYERS, NLAT)),
        dma((LAYERS, NLAT)),
        dma((LAYERS, NLAT)),
        dma((LAYERS, NLAT)),
        dma((4, NLAT)),
        dma((4, NLAT)),
    ]
    return pl.pallas_call(
        stack_kernel,
        out_shape=shapes,
        in_specs=[
            pl.BlockSpec(memory_space=pl.ANY if at in (3, 10, 11) else pltpu.VMEM)
            for at in range(len(args))
        ],
        out_specs=[pl.BlockSpec(memory_space=pltpu.VMEM)] * len(shapes),
        scratch_shapes=scratch,
        compiler_params=pltpu.CompilerParams(
            collective_id=0, has_side_effects=True, vmem_limit_bytes=60 << 20
        ),
        name="stack",
    )(*args)


def two_parts(table):
    high = table.astype(ml_dtypes.bfloat16)
    return np.stack([high, (table - high.astype(np.float64)).astype(ml_dtypes.bfloat16)])


def lat_all():
    lat_cells = ROWS * NLAT
    phase = np.outer(np.arange(lat_cells), np.arange(lat_cells)) % lat_cells
    angles = phase * (2.0 * math.pi / lat_cells)

    def place(table):
        return table.reshape(lat_cells, NLAT, ROWS).transpose(0, 2, 1).reshape(lat_cells, -1)

    cos, sin = place(np.cos(angles)), place(np.sin(angles))
    table = np.block([[cos, sin], [-sin, cos]]) / math.sqrt(lat_cells)
    table = np.pad(table, ((0, 2 * TILE - 2 * lat_cells), (0, 0)))
    return two_parts(table), two_parts(np.ascontiguousarray(table.T))


def lon_all():
    modes = LON // 2 + 1
    phase = np.outer(np.arange(modes), np.arange(LON)) % LON
    angles = phase * (2.0 * math.pi / LON)
    table = np.stack([np.cos(angles), -np.sin(angles)], axis=1).reshape(2 * modes, LON)
    table = table / math.sqrt(LON)
    rows = []
    for r in range(ROWS):
        before = r * LON - TILE_FROM[r] * TILE
        rows.append(
            np.pad(table, ((0, 2 * TILE - 2 * modes), (before, SPAN - LON - before)))
        )
    cells = np.stack(rows)
    return two_parts(np.ascontiguousarray(cells.transpose(0, 2, 1))), two_parts(cells)


def body(
    inputs,
    cotangent,
    first_gain,
    first_shift,
    filter_inner,
    filter_inner_bias,
    filter_outer,
    filter_outer_bias,
    second_gain,
    second_shift,
    up_weight,
    up_bias,
    down_weight,
    down_bias,
    kept_lat,
    kept_lon,
):
    shape = inputs.shape
    cells = ROWS * LON

    def to_tiles(field):
        flat = jnp.pad(field.reshape(CB, cells), ((0, 0), (0, NCH * TILE - cells)))
        return flat.reshape(CB, NCH, TILE).transpose(1, 0, 2)

    def from_tiles(tiles):
        return tiles.transpose(1, 0, 2).reshape(CB, NCH * TILE)[:, :cells].reshape(shape)

    vectors = jnp.stack([first_gain, first_shift, second_gain, second_shift, down_bias], axis=1)
    prm = jnp.concatenate(
        [
            jnp.pad(vectors, ((0, 0), (0, 0), (0, 256 - CB))),
            jnp.pad(up_bias[:, None, :], ((0, 0), (0, 2), (0, 256 - FB))),
        ],
        axis=1,
    ).reshape(32, 256)
    shards = jnp.stack([up_weight.transpose(0, 2, 1), down_weight], axis=1)
    biases = jnp.concatenate([filter_inner_bias[:, :, 0], filter_outer_bias[:, :, 0]], axis=1)
    biases = jnp.tile(jnp.pad(biases, ((0, 0), (0, 4), (0, CP - CB))), (1, 1, 2))
    lon_index = (kept_lon[:, None] * 2 + jnp.arange(2, dtype=jnp.int32)).reshape(1, TILE)
    lat_index = jnp.pad(kept_lat, (0, 64 - kept_lat.shape[0]), constant_values=-4 * LON)
    lat_index = (jnp.arange(2, dtype=jnp.int32)[:, None] * (ROWS * NLAT) + lat_index).reshape(1, TILE)
    index = jnp.concatenate([lon_index, lat_index, jnp.zeros((6, TILE), jnp.int32)], axis=0)
    all_a, all_t = lat_all()
    all_k, all_v = lon_all()
    out_h, out_g, wout, sout, sums = run_stack(
        to_tiles(inputs), to_tiles(cotangent), prm, shards,
        filter_inner.reshape(LAYERS, 2, CB, CB), filter_outer.reshape(LAYERS, 2, CB, CB),
        biases, index, all_a, all_t, all_k, all_v,
    )
    rows = sums[:32].reshape(LAYERS, 8, TILE)
    up_shift_grad = jnp.concatenate([sums[32:36], sums[40:44]], axis=1)[:, :FB]
    wout = wout.reshape(2, LAYERS, FB, D)
    filters = sout.reshape(LAYERS, 2, CP, 2, CP).transpose(1, 0, 3, 2, 4)
    fbias = filters[:, :, :, CB, :CB]
    filters = filters[:, :, :, :CB, :CB]
    plain, cross = rows[:, 0, :CB], rows[:, 1, :CB]
    return (
        from_tiles(out_h),
        from_tiles(out_g),
        (cross - first_shift * plain) / first_gain,
        plain,
        filters[0][:, :, None],
        fbias[0][:, :, None],
        filters[1][:, :, None],
        fbias[1][:, :, None],
        rows[:, 2, :CB],
        rows[:, 3, :CB],
        wout[0].transpose(0, 2, 1).astype(F32),
        up_shift_grad,
        wout[1].astype(F32),
        rows[:, 4, :CB],
    )


def solution(mesh):
    placed = (
        P("ch", "lat", None),
        P("ch", "lat", None),
        P(None, "ch"),
        P(None, "ch"),
        P(None, None, "ch", None, None),
        P(None, None, "ch", None),
        P(None, None, "ch", None, None),
        P(None, None, "ch", None),
        P(None, "ch"),
        P(None, "ch"),
        P(None, None, "ch"),
        P(None, "ch"),
        P(None, "ch", None),
        P(None, "ch"),
        P(),
        P(),
    )
    return jax.shard_map(
        body,
        mesh=mesh,
        in_specs=placed,
        out_specs=(
            P("ch", "lat", None),
            P("ch", "lat", None),
            P(None, "ch"),
            P(None, "ch"),
            P(None, None, "ch", None, None),
            P(None, None, "ch", None),
            P(None, None, "ch", None, None),
            P(None, None, "ch", None),
            P(None, "ch"),
            P(None, "ch"),
            P(None, None, "ch"),
            P(None, "ch"),
            P(None, "ch", None),
            P(None, "ch"),
        ),
        check_vma=False,
    )
```

```python
import functools
import math

import jax
import jax.numpy as jnp
import ml_dtypes
import numpy as np
from jax import lax
from jax.experimental import pallas as pl
from jax.experimental.pallas import tpu as pltpu
from jax.sharding import PartitionSpec as P

shrink_level = 0.01
norm_eps = 1e-05
highest = lax.Precision.HIGHEST
MESH = pl.DeviceIdType.MESH
F32 = jnp.float32
BF16 = jnp.bfloat16

LAYERS = 4
NCH = 8
NLAT = 16
CB = 48
CP = 64
D = NCH * CB
ROWS = 5
LON = 180
TILE = 128
FB = 192
FF = NCH * FB
CHUNK = 384
QB = FB // 4
WROWS = 32
SHARES = FB // WROWS
TILE_FROM = [r * LON // TILE for r in range(ROWS)]
TILE_TO = [-(-(r + 1) * LON // TILE) for r in range(ROWS)]
SPAN = max(b - a for a, b in zip(TILE_FROM, TILE_TO)) * TILE


def gelu_exact(values):
    return 0.5 * values * (1.0 + lax.erf(values * 0.7071067811865476))


def gelu_slope(values):
    return (
        0.5 * (1.0 + lax.erf(values * 0.7071067811865476))
        + values * jnp.exp(-0.5 * values * values) * 0.3989422804014327
    )


def mm(a, b, dims=((1,), (0,)), precision=highest):
    return lax.dot_general(a, b, (dims, ((), ())), precision=precision, preferred_element_type=F32)


def mb(a, b, dims=((1,), (0,))):
    return lax.dot_general(a, b, (dims, ((), ())), preferred_element_type=F32)


NT = ((1,), (1,))


def split(value):
    high = value.astype(BF16)
    return high, (value - high.astype(F32)).astype(BF16)


def rows_times(value, high, low):
    vh, vl = split(value)
    n = value.shape[0]
    both = mb(jnp.concatenate([vh, vl], axis=0), high)
    return both[:n] + both[n:] + mb(vh, low)


def table_times(high, low, value):
    vh, vl = split(value)
    n = value.shape[1]
    both = mb(high, jnp.concatenate([vh, vl], axis=1))
    return both[:, :n] + both[:, n:] + mb(low, vh)


def stack_kernel(
    x0, ct, prm, wsh, fi, fo, fb, idx, all_a, all_t, all_k, all_v,
    out_h, out_g, wout, sout, rout,
    h_s, g_s, xin, pbuf, pcol, bcol, mbuf, fbuf, sbuf, sbuf2, xbuf, zbuf, cbuf, bbuf,
    wall, wT, n1_s, n2_s, r1_s, r2_s, lifted_s, pre_s, hid_s, y_s, hh_s, t_s,
    xs, prs, gr, psend, pget, gsend, gget, pc, pin, bc, brow, bin_s, pr, ig_s, igr, mixr_s, bwf, k_s, v_s,
    bw, bt, la, lt, lk, lv,
    gw, wget, wsum, gf, fget, fsum, gpsum, gpget,
    bsem_s, bsem_r, asem_s, asem_r, psem_s, psem_r, gsem_s, gsem_r, qsem_s, qsem_r,
    c_s, c_r, l_s, l_r, t_sem, ysem_s, ysem_r, w1_s, w1_r, w2_s, w2_r, f_s, f_r,
):
    ch = lax.axis_index("ch")
    lat = lax.axis_index("lat")
    core = lax.rem(lat, 2)
    partner = lat + 1 - 2 * core


    def flipped(at):
        return at + 2 - 4 * lax.rem(at // 2, 2)

    flip = flipped(lat)
    half = lax.rem(ch, 2)
    rank = lat + half * (flip - lat)
    ch_peer = [lax.rem(ch + s, NCH) for s in range(NCH)]
    lat_peer = [lax.rem(lat + s, NLAT) for s in range(NLAT)]

    barrier = pltpu.get_barrier_semaphore()
    for s in range(1, NCH):
        pl.semaphore_signal(barrier, inc=1, device_id={"ch": ch_peer[s]}, device_id_type=MESH)
        pl.semaphore_signal(
            barrier, inc=1, device_id={"lat": flip, "ch": ch_peer[s]}, device_id_type=MESH
        )
    for s in range(1, NLAT):
        pl.semaphore_signal(barrier, inc=1, device_id={"lat": lat_peer[s]}, device_id_type=MESH)

    def remote(src, dst, send, recv, where):
        return pltpu.make_async_remote_copy(
            src_ref=src, dst_ref=dst, send_sem=send, recv_sem=recv,
            device_id=where, device_id_type=MESH,
        )

    def over_near(src, dst, send, recv):
        copies = []
        for s in range(1, NCH):
            where = {"lat": flip, "ch": ch_peer[s]} if s % 2 else {"ch": ch_peer[s]}
            copies.append(remote(src(ch_peer[s]), dst, send.at[s], recv.at[s], where))
        return copies

    def between(src, dst, at, inward):
        copies = []
        for s in range(NCH):
            there = lat + lax.rem(half + s, 2) * (flip - lat) if inward else rank
            where = {"lat": there, "ch": ch_peer[s]}
            copies.append(remote(src(ch_peer[s]), dst, bsem_s.at[at, s], bsem_r.at[at, s], where))
        return copies

    def between_start(src, dst, at, inward, keep):
        copies = between(src, dst, at, inward)
        for copy in copies[1:]:
            copy.start()

        @pl.when(half == 1)
        def _():
            copies[0].start()

        @pl.when(half == 0)
        def _():
            keep()

        return copies

    def between_done(copies):
        for copy in copies[1:]:
            copy.wait()

        @pl.when(half == 1)
        def _():
            copies[0].wait()

    def to_lat(src, dst, send, recv):
        return [
            remote(src(lat_peer[s]), dst, send.at[s], recv.at[s], {"lat": lat_peer[s]})
            for s in range(1, NLAT)
        ]

    def start(copies):
        for copy in copies:
            copy.start()
        return copies

    def arrived(copies):
        for copy in copies:
            copy.wait_recv()

    def sent(copies):
        for copy in copies:
            copy.wait_send()

    def done(copies):
        for copy in copies:
            copy.wait()

    quarter = lat // 4

    def weights_near(layer):
        source = wsh.at[layer, core, pl.ds(pl.multiple_of(quarter * QB, QB), QB)]
        mine = wall.at[layer, core, quarter, pl.ds(pl.multiple_of(ch * QB, QB), QB)]
        return over_near(lambda p: source, mine, asem_s.at[layer], asem_r.at[layer])

    def own_weights(layer):
        source = wsh.at[layer, core, pl.ds(pl.multiple_of(quarter * QB, QB), QB)]
        mine = wall.at[layer, core, quarter, pl.ds(pl.multiple_of(ch * QB, QB), QB)]
        return pltpu.make_async_copy(source, mine, t_sem.at[2 + layer])

    def weights_along(layer):
        block = wall.at[layer, core, quarter]
        return [
            remote(block, block, ysem_s.at[layer, s], ysem_r.at[layer, s], {"lat": lat_peer[4 * s]})
            for s in range(1, 4)
        ]

    def weights_pair(layer):
        block = wall.at[layer, core]
        return remote(block, block, psem_s.at[layer], psem_r.at[layer], {"lat": partner})

    def weights_start(layer):
        start(weights_near(layer))
        own_weights(layer).start()

    def weights_spread(layer):
        done(weights_near(layer))
        own_weights(layer).wait()
        start(weights_along(layer))

    def weights_pass(layer):
        done(weights_along(layer))
        weights_pair(layer).start()

    def weights_done(layer):
        weights_pair(layer).wait()

    get_k = pltpu.make_async_copy(all_k, k_s, t_sem.at[0])
    get_v = pltpu.make_async_copy(all_v, v_s, t_sem.at[1])
    get_k.start()
    get_v.start()
    pbuf[ch] = prm[...]
    pl.semaphore_wait(barrier, 2 * (NCH - 1) + NLAT - 1)

    def keep_x():
        xin[0, ch] = x0[ch]

    def keep_ct():
        xin[1, ch] = ct[ch]

    first = between_start(lambda p: x0.at[p], xin.at[0, ch], 0, True, keep_x)
    params = start(over_near(lambda p: prm, pbuf.at[ch], bsem_s.at[1], bsem_r.at[1]))
    weights_start(0)
    pc[...] = jnp.zeros(pc.shape, F32)
    bc[...] = jnp.zeros(bc.shape, F32)
    pr[...] = jnp.zeros(pr.shape, F32)
    bwf[...] = jnp.zeros(bwf.shape, F32)

    def picker(at):
        rows = lax.broadcasted_iota(jnp.int32, (2 * TILE, TILE), 0)
        return jnp.where(rows == idx[at : at + 1, :], 1.0, 0.0)

    def turn(pick):
        return jnp.concatenate([jnp.transpose(pick[:TILE]), jnp.transpose(pick[TILE:])], axis=1)

    ends = (idx[0:1, :] < 2) | (idx[0:1, :] >= 180)
    mode_weight = jnp.where(ends, 1.0, 2.0)

    def first_tables():
        get_k.wait()
        pick = picker(0).astype(BF16)
        for part in range(2):
            for r in range(ROWS):
                table = mb(k_s[part, r], pick)
                lk[part, 0, r] = table.astype(BF16)
                lk[part, 1, r] = (table * mode_weight).astype(BF16)

    def other_tables():
        get_v.wait()
        pick = picker(0)
        pick_t = jnp.concatenate([turn(pick), turn(pick * mode_weight)], axis=0).astype(BF16)
        for part in range(2):
            for r in range(ROWS):
                table = mb(pick_t, v_s[part, r]).astype(BF16)
                lv[part, 0, r] = table[:TILE]
                lv[part, 1, r] = table[TILE:]
        pick = picker(1)
        pick_t = turn(pick).astype(BF16)
        pick = pick.astype(BF16)
        for part in range(2):
            la[part] = mb(pick_t, all_a[part]).astype(BF16)
            lt[part] = mb(all_t[part], pick).astype(BF16)

    def columns(held, width, count):
        for j in range(NCH):
            turned = jnp.transpose(pbuf[j, :, :width])
            for layer in range(LAYERS):
                part = turned[:, layer * 8 : layer * 8 + 8]
                if count == CB:
                    held[layer, j * CB : (j + 1) * CB, 0:8] = part[:CB]
                else:
                    for y in range(4):
                        at = y * CHUNK + j * QB
                        held[layer, at : at + QB, 0:8] = part[y * QB : (y + 1) * QB]

    first_tables()
    done(params)
    columns(pcol, TILE, CB)
    between_done(first)
    second = between_start(lambda p: ct.at[p], xin.at[1, ch], 2, True, keep_ct)
    h_s[...] = xin[0]

    lane = lax.broadcasted_iota(jnp.int32, (NLAT, TILE), 1)

    def filter_tables(layer):
        for at, weight in enumerate((fi, fo)):
            for part in range(2):
                for k in range(2):
                    lanes = part * TILE + k * CP
                    bwf[k * CP : k * CP + CB, lanes : lanes + CB] = weight[layer, part]
            table = bwf[...]
            bw[0, layer, at], bw[1, layer, at] = split(table)
            bt[0, layer, at], bt[1, layer, at] = split(
                jnp.concatenate(
                    [jnp.transpose(table[:, :TILE]), jnp.transpose(table[:, TILE:])], axis=1
                )
            )

    def swap(v):
        return pltpu.roll(v, CP, 1)

    def lon_to_modes(which):
        parts = []
        for r in range(ROWS):
            a, b = TILE_FROM[r], TILE_TO[r]
            field = jnp.concatenate([fbuf[t] for t in range(a, b)], axis=1)
            span = (b - a) * TILE
            parts.append(rows_times(field, lk[0, which, r, :span], lk[1, which, r, :span]))
        parts.append(jnp.zeros((2 * TILE - ROWS * CB, TILE), F32))
        both = jnp.concatenate(parts, axis=0)
        for t in range(2):
            turned = jnp.transpose(both[t * TILE : (t + 1) * TILE])
            sbuf[:, :, t * TILE : (t + 1) * TILE] = turned.reshape(NLAT, 8, TILE)

    def gather_lat():
        for ri in range(2):
            for kt in range(2):
                sides = []
                for side in range(2):
                    q = 4 * kt + 2 * side + ri
                    left, right = xbuf[:, q, :TILE], xbuf[:, q, TILE:]
                    middle = jnp.where(lane >= 2 * CB, left, right)
                    sides.append([left, left, middle, right, right])
                for r in range(ROWS):
                    a = pltpu.roll(sides[0][r], (-r * CB) % TILE, 1) if r else sides[0][r]
                    b = pltpu.roll(sides[1][r], (CP - r * CB) % TILE, 1)
                    at = ri * ROWS * NLAT + r * NLAT
                    xs[at : at + NLAT, kt * TILE : (kt + 1) * TILE] = jnp.where(lane < CP, a, b)

    def scatter_lat(z):
        for ri in range(2):
            for k in range(4):
                lanes = slice(k // 2 * TILE, (k // 2 + 1) * TILE)
                p = []
                for r in range(ROWS):
                    at = ri * ROWS * NLAT + r * NLAT
                    piece = z[at : at + NLAT, lanes]
                    move = (r * CB - k % 2 * CP) % TILE
                    p.append(pltpu.roll(piece, move, 1) if move else piece)
                left = jnp.where(lane < CB, p[0], jnp.where(lane < 2 * CB, p[1], p[2]))
                right = jnp.where(lane < 16, p[2], jnp.where(lane < 64, p[3], p[4]))
                sbuf2[:, 2 * k + ri, :TILE] = left
                sbuf2[:, 2 * k + ri, TILE:] = jnp.where(lane < 112, right, 0.0)

    def lon_to_cells(which):
        both = jnp.concatenate(
            [
                jnp.transpose(zbuf[:, :, t * TILE : (t + 1) * TILE].reshape(TILE, TILE))
                for t in range(2)
            ],
            axis=0,
        )
        tiles = [None] * NCH
        for r in range(ROWS):
            a, b = TILE_FROM[r], TILE_TO[r]
            span = (b - a) * TILE
            rows = both[r * CB : (r + 1) * CB]
            part = rows_times(rows, lv[0, which, r, :, :span], lv[1, which, r, :, :span])
            for t in range(a, b):
                piece = part[:, (t - a) * TILE : (t - a + 1) * TILE]
                tiles[t] = piece if tiles[t] is None else tiles[t] + piece
        for t in range(NCH):
            cbuf[t] = tiles[t]

    def mix(v, table, layer, at, sign):
        out = []
        for t in range(2):
            q = rows_times(v[:, t * TILE : (t + 1) * TILE], table[0, layer, at], table[1, layer, at])
            re = q[:64, :TILE] - sign * q[64:, TILE:]
            im = q[64:, :TILE] + sign * q[:64, TILE:]
            out.append(jnp.concatenate([re, im], axis=0))
        return jnp.concatenate(out, axis=1)

    def bias_rows(layer, at):
        rows = [jnp.broadcast_to(fb[layer, at + ri : at + ri + 1, :], (64, TILE)) for ri in range(2)]
        both = jnp.concatenate(rows, axis=0)
        return jnp.concatenate([both, both], axis=1)

    def exchange_one(value):
        mbuf[...] = value.reshape(NCH, CB, TILE)
        copies = start(over_near(lambda p: mbuf.at[p], fbuf.at[ch], c_s.at[0], c_r.at[0]))
        fbuf[ch] = mbuf[ch]
        return copies

    def exchange_four():
        copies = start(over_near(lambda p: cbuf.at[p], bbuf.at[ch], c_s.at[1], c_r.at[1]))
        bbuf[ch] = cbuf[ch]
        return copies

    def exchange_lat(src, dst, at):
        copies = []
        for s in range(1, NLAT):
            peer = lax.rem(rank + s, NLAT)
            there = peer + half * (flipped(peer) - peer)
            copies.append(
                remote(src.at[peer], dst.at[rank], l_s.at[at, s], l_r.at[at, s], {"lat": there})
            )
        start(copies)
        dst[rank] = src[rank]
        return copies

    def col(layer, at):
        return pcol[layer, :, at : at + 1]

    def forward(layer, carry):
        h = h_s[...].reshape(D, TILE)
        mean = jnp.sum(h, axis=0, keepdims=True) * (1.0 / D)
        spread = jnp.sum(h * h, axis=0, keepdims=True) * (1.0 / D) - mean * mean
        rstd = lax.rsqrt(spread + norm_eps)
        n1 = (h - mean) * rstd
        n1_s[layer] = n1
        r1_s[layer] = jnp.broadcast_to(rstd, (8, TILE))
        mixed = n1 * col(layer, 0) + col(layer, 1)
        one = exchange_one(mixed)
        ig_s[...] = h + mixed

        @pl.when(layer == 0)
        def _():
            weights_spread(0)
            other_tables()

        filter_tables(layer)
        arrived(one)
        lon_to_modes(0)
        two = exchange_lat(sbuf, xbuf, 0)
        weights_pass(layer)
        sent(one)
        mixr_s[layer] = fbuf[...]

        @pl.when(layer == 0)
        def _():
            columns(bcol, 256, FB)

        @pl.when(layer < LAYERS - 1)
        def _():
            weights_start(layer + 1)

        arrived(two)
        gather_lat()
        y = table_times(la[0], la[1], xs[...])
        y_s[layer] = y
        hh = mix(y, bw, layer, 0, 1.0) + bias_rows(layer, 0)
        hh_s[layer] = hh
        b = mix(gelu_exact(hh), bw, layer, 1, 1.0) + bias_rows(layer, 2)
        t = jnp.tanh(b / shrink_level)
        t_s[layer] = t
        scatter_lat(table_times(lt[0], lt[1], b - shrink_level * t))
        three = exchange_lat(sbuf2, zbuf, 1)
        sent(two)
        arrived(three)
        lon_to_cells(1)
        four = exchange_four()
        sent(three)

        @pl.when(layer < LAYERS - 1)
        def _():
            weights_spread(layer + 1)

        weights_done(layer)
        for at in range(0, FF, CHUNK):
            wT[:, at : at + CHUNK] = jnp.transpose(wall[layer, 1, at // CHUNK])
        arrived(four)
        inner = ig_s[...] + bbuf[...].reshape(D, TILE)
        mean = jnp.sum(inner, axis=0, keepdims=True) * (1.0 / D)
        spread = jnp.sum(inner * inner, axis=0, keepdims=True) * (1.0 / D) - mean * mean
        rstd = lax.rsqrt(spread + norm_eps)
        n2 = (inner - mean) * rstd
        n2_s[layer] = n2
        r2_s[layer] = jnp.broadcast_to(rstd, (8, TILE))
        lifted = (n2 * col(layer, 2) + col(layer, 3)).astype(BF16)
        lifted_s[layer] = lifted
        total = inner + col(layer, 4)
        for at in range(0, FF, CHUNK):
            pre = mb(wall[layer, 0, at // CHUNK], lifted) + bcol[layer, at : at + CHUNK, 5:6]
            pre_s[layer, at : at + CHUNK] = pre
            hidden = gelu_exact(pre).astype(BF16)
            hid_s[layer, at : at + CHUNK] = hidden
            total = total + mb(wT[:, at : at + CHUNK], hidden)
        h_s[...] = total.reshape(NCH, CB, TILE)
        sent(four)
        return carry

    lax.fori_loop(0, LAYERS, forward, 0)

    def keep_h():
        out_h[ch] = h_s[ch]

    def keep_g():
        out_g[ch] = g_s[ch]

    last_h = between_start(lambda p: h_s.at[p], out_h.at[ch], 3, False, keep_h)
    between_done(second)
    g_s[...] = xin[1]
    ones = jnp.ones((8, TILE), F32)

    def turn_up(layer):
        for at in range(0, FF, CHUNK):
            wT[:, at : at + CHUNK] = jnp.transpose(wall[layer, 0, at // CHUNK])

    turn_up(LAYERS - 1)

    lanes_d = lax.broadcasted_iota(jnp.int32, (D, TILE), 1)
    lanes_f = lax.broadcasted_iota(jnp.int32, (CHUNK, TILE), 1)

    def cell_sums(layer, at, value):
        total = jnp.sum(value, axis=1, keepdims=True)
        held = pc[...].reshape(D, TILE)
        held = jnp.where(lanes_d == layer * 8 + at, total, held)
        pc[...] = held.reshape(NCH, CB, TILE)

    def hidden_sums(layer):
        for at in range(0, FF, CHUNK):
            total = jnp.sum(pre_s[layer, at : at + CHUNK], axis=1, keepdims=True)
            held = bc[at : at + CHUNK]
            bc[at : at + CHUNK] = jnp.where(lanes_f == layer, total, held)

    def turn_hidden_sums():
        blank = jnp.zeros((2 * TILE - FB, TILE), F32)
        for j in range(NCH):
            pieces = [bc[y * CHUNK + j * QB : y * CHUNK + (j + 1) * QB] for y in range(4)]
            tall = jnp.concatenate(pieces + [blank], axis=0)
            for t in range(2):
                turned = jnp.transpose(tall[t * TILE : (t + 1) * TILE])
                brow[j, :, t * TILE : (t + 1) * TILE] = turned[:8]

    def grads_pair(layer):
        return remote(
            psend, pget, qsem_s.at[layer], qsem_r.at[layer], {"lat": partner}
        )

    def grads_near(layer):
        return over_near(
            lambda p: gsend.at[p], gget.at[lax.rem(layer, 2), ch], gsem_s.at[layer], gsem_r.at[layer]
        )

    def grads_done(layer):
        slot = lax.rem(layer, 2)
        gget[slot, ch] = gsend[ch]
        done(grads_near(layer))
        total = gget[slot, 0].astype(F32)
        for j in range(1, NCH):
            total = total + gget[slot, j].astype(F32)
        gw[layer] = total.astype(BF16).reshape(SHARES, WROWS, D)

    near = lat // 2
    evens = range(2, NLAT, 2)

    def sum_share(layer):
        for s in evens:
            there = lat_peer[s] // 2

            @pl.when(there < SHARES)
            def _():
                share_copy(layer, s).start()

    def share_copy(layer, s):
        return remote(
            gw.at[layer, lat_peer[s] // 2], wget.at[layer, near],
            w1_s.at[layer, s], w1_r.at[layer, s], {"lat": lat_peer[s]},
        )

    def arriving(layer, s):
        return remote(
            wget.at[layer, near], wget.at[layer, near],
            w1_s.at[layer, s], w1_r.at[layer, s], {"lat": lat_peer[s]},
        )

    def give_copy(layer, s):
        return remote(
            wsum.at[layer], wout.at[core, layer, near],
            w2_s.at[layer, s], w2_r.at[layer, s], {"lat": lat_peer[s]},
        )

    def given(layer, s):
        return remote(
            wsum.at[layer], wsum.at[layer],
            w2_s.at[layer, s], w2_r.at[layer, s], {"lat": lat_peer[s]},
        )

    def sum_pass(layer):
        for s in evens:

            @pl.when(lat_peer[s] // 2 < SHARES)
            def _():
                share_copy(layer, s).wait_send()

        @pl.when(near < SHARES)
        def _():
            wget[layer, near] = gw[layer, near]
            for s in evens:
                arriving(layer, s).wait_recv()
            total = wget[layer, 0].astype(F32)
            for j in range(1, 8):
                total = total + wget[layer, j].astype(F32)
            wsum[layer] = total.astype(BF16)
            for s in evens:
                give_copy(layer, s).start()
            wout[core, layer, near] = wsum[layer]

    def hand_copy(layer):
        whole = wout.at[core, layer]
        return remote(whole, whole, w2_s.at[layer, 0], w2_r.at[layer, 0], {"lat": partner})

    def sum_hand(layer):
        @pl.when(near < SHARES)
        def _():
            for s in evens:
                give_copy(layer, s).wait_send()

        for s in evens:

            @pl.when(lax.rem(near + 8 - s // 2, 8) < SHARES)
            def _():
                given(layer, s).wait_recv()

        hand_copy(layer).start()

    def filters_share():
        return to_lat(lambda p: gf.at[p], fget.at[lat], f_s.at[0], f_r.at[0])

    def filters_give():
        return to_lat(lambda p: fsum, sout.at[lat], f_s.at[1], f_r.at[1])

    def rows_share():
        copies = []
        for s in range(1, NCH):
            p = ch_peer[s]
            where = {"lat": flip, "ch": p} if s % 2 else {"ch": p}
            copies.append(remote(pc.at[p], pin.at[ch], bsem_s.at[5, s], bsem_r.at[5, s], where))
            copies.append(
                remote(brow.at[p], bin_s.at[ch], bsem_s.at[7, s], bsem_r.at[7, s], where)
            )
        return copies

    def rows_give():
        return to_lat(lambda p: gpsum, gpget.at[lat], f_s.at[2], f_r.at[2])

    def rows_pass():
        pin[ch] = pc[ch]
        bin_s[ch] = brow[ch]
        done(rows_share())
        total, hidden = pin[0] + pr[...], bin_s[0]
        for j in range(1, NCH):
            total, hidden = total + pin[j], hidden + bin_s[j]
        tall = jnp.concatenate([total, jnp.zeros((TILE - CB, TILE), F32)], axis=0)
        gpsum[:32] = jnp.transpose(tall)[:32]
        gpsum[32:40] = hidden[:, :TILE]
        gpsum[40:48] = hidden[:, TILE:]
        gpget[lat] = gpsum[...]
        start(rows_give())

    def backward(step, carry):
        layer = LAYERS - 1 - step
        g = g_s[...].reshape(D, TILE)
        g_round = g.astype(BF16)
        lift = jnp.zeros((D, TILE), F32)
        for at in range(0, FF, CHUNK):
            hidden_grad = mb(wall[layer, 1, at // CHUNK], g_round)
            pre_grad = hidden_grad * gelu_slope(pre_s[layer, at : at + CHUNK])
            pre_s[layer, at : at + CHUNK] = pre_grad
            pre_round = pre_grad.astype(BF16)
            prs[at : at + CHUNK] = pre_round
            lift = lift + mb(wT[:, at : at + CHUNK], pre_round)
        n2 = n2_s[layer]
        q2 = lift * col(layer, 2)
        m1 = jnp.sum(q2, axis=0, keepdims=True) * (1.0 / D)
        m2 = jnp.sum(q2 * n2, axis=0, keepdims=True) * (1.0 / D)
        inner_grad = g + r2_s[layer, 0:1, :] * (q2 - m1 - n2 * m2)
        one = exchange_one(inner_grad)
        ig_s[...] = inner_grad
        lifted = lifted_s[layer]
        for at in range(0, FF, CHUNK):
            gr[1, at : at + CHUNK] = mb(hid_s[layer, at : at + CHUNK], g_round, NT)
            gr[0, at : at + CHUNK] = mb(prs[at : at + CHUNK], lifted, NT)
        psend[...] = gr[1 - core].astype(BF16)
        grads_pair(layer).start()
        cell_sums(layer, 4, g)
        cell_sums(layer, 2, lift * n2)
        cell_sums(layer, 3, lift)
        arrived(one)
        lon_to_modes(1)
        two = exchange_lat(sbuf, xbuf, 0)
        sent(one)
        igr[...] = fbuf[...]

        @pl.when(layer < LAYERS - 1)
        def _():
            grads_done(layer + 1)
            sum_share(layer + 1)

        @pl.when(layer < LAYERS - 2)
        def _():
            sum_hand(layer + 2)

        grads_pair(layer).wait()
        for y in range(4):
            cut = slice(y * CHUNK, (y + 1) * CHUNK)
            part = (gr[core, cut] + pget[cut].astype(F32)).astype(BF16)
            for j in range(NCH):
                gsend[j, y * QB : (y + 1) * QB] = part[j * QB : (j + 1) * QB]
        start(grads_near(layer))
        hidden_sums(layer)
        arrived(two)
        gather_lat()
        t = t_s[layer]
        db = table_times(la[0], la[1], xs[...]) * (t * t)
        hh = hh_s[layer]
        dh = mix(db, bt, layer, 1, -1.0) * gelu_slope(hh)
        dy = mix(dh, bt, layer, 0, -1.0)
        scatter_lat(table_times(lt[0], lt[1], dy))
        three = exchange_lat(sbuf2, zbuf, 1)
        sent(two)

        def filter_grads(at, left, right):
            turned = jnp.concatenate([right[64:], -right[:64]], axis=0)
            total = jnp.zeros((TILE, 2 * TILE), F32)
            for tt in range(2):
                lanes = slice(tt * TILE, (tt + 1) * TILE)
                pair = jnp.concatenate([right[:, lanes], turned[:, lanes]], axis=1)
                total = total + mm(jnp.transpose(left[:, lanes]), pair)
            re = total[:64, :TILE] + swap(total[64:, :TILE])
            im = total[:64, TILE:] + swap(total[64:, TILE:])
            keep = lax.broadcasted_iota(jnp.int32, (64, TILE), 1) < CP
            value = jnp.where(keep, re, swap(im))
            base = (layer * 2 + at) * 2
            gf[base] = value[:32]
            gf[base + 1] = value[32:]
            sums = []
            for part in (right[:64], right[64:]):
                row = jnp.sum(part, axis=0, keepdims=True)
                row = row[:, :TILE] + row[:, TILE:]
                sums.append(row + swap(row))
            gf[base + 1, 16:17, :] = jnp.where(keep[:1], sums[0], sums[1])

        filter_grads(1, gelu_exact(hh), db)
        filter_grads(0, y_s[layer], dh)

        @pl.when(layer > 0)
        def _():
            turn_up(layer - 1)

        @pl.when(layer == 0)
        def _():
            start(filters_share())
            turn_hidden_sums()
            start(rows_share())

        arrived(three)
        lon_to_cells(0)
        four = exchange_four()
        sent(three)
        both = igr[...] + cbuf[...]
        plain = jnp.sum(jnp.sum(both, axis=0), axis=1, keepdims=True)
        cross = jnp.sum(jnp.sum(both * mixr_s[layer], axis=0), axis=1, keepdims=True)
        lanes_c = lax.broadcasted_iota(jnp.int32, (CB, TILE), 1) - layer * 8
        pr[...] = jnp.where(lanes_c == 0, plain, jnp.where(lanes_c == 1, cross, pr[...]))

        @pl.when(layer < LAYERS - 1)
        def _():
            sum_pass(layer + 1)

        @pl.when(layer == 0)
        def _():
            fget[lat] = gf[lat]
            done(filters_share())
            total = fget[0]
            for j in range(1, NLAT):
                total = total + fget[j]
            fsum[...] = total
            sout[lat] = total
            start(filters_give())
            rows_pass()
            grads_done(0)
            sum_share(0)

        arrived(four)
        inner_grad = ig_s[...]
        mixed_grad = inner_grad + bbuf[...].reshape(D, TILE)
        n1 = n1_s[layer]
        q1 = mixed_grad * col(layer, 0)
        m1 = jnp.sum(q1, axis=0, keepdims=True) * (1.0 / D)
        m2 = jnp.sum(q1 * n1, axis=0, keepdims=True) * (1.0 / D)
        g = inner_grad + r1_s[layer, 0:1, :] * (q1 - m1 - n1 * m2)
        g_s[...] = g.reshape(NCH, CB, TILE)
        sent(four)
        return carry

    lax.fori_loop(0, LAYERS, backward, 0)
    final = between_start(lambda p: g_s.at[p], out_g.at[ch], 4, False, keep_g)
    sum_hand(1)
    sum_pass(0)
    sum_hand(0)
    between_done(last_h)
    between_done(final)
    done(filters_give())
    for layer in range(LAYERS):
        hand_copy(layer).wait()
    done(rows_give())
    total = gpget[0]
    for j in range(1, NLAT):
        total = total + gpget[j]
    rout[...] = total


def run_stack(*args):
    shapes = [
        jax.ShapeDtypeStruct((NCH, CB, TILE), F32),
        jax.ShapeDtypeStruct((NCH, CB, TILE), F32),
        jax.ShapeDtypeStruct((2, LAYERS, SHARES, WROWS, D), BF16),
        jax.ShapeDtypeStruct((NLAT, 32, TILE), F32),
        jax.ShapeDtypeStruct((48, TILE), F32),
    ]
    v = pltpu.VMEM
    dma = pltpu.SemaphoreType.DMA
    scratch = [
        v((NCH, CB, TILE), F32),
        v((NCH, CB, TILE), F32),
        v((2, NCH, CB, TILE), F32),
        v((NCH, 32, 256), F32),
        v((LAYERS, D, TILE), F32),
        v((LAYERS, FF, TILE), F32),
        v((NCH, CB, TILE), F32),
        v((NCH, CB, TILE), F32),
        v((NLAT, 8, 2 * TILE), F32),
        v((NLAT, 8, 2 * TILE), F32),
        v((NLAT, 8, 2 * TILE), F32),
        v((NLAT, 8, 2 * TILE), F32),
        v((NCH, CB, TILE), F32),
        v((NCH, CB, TILE), F32),
        v((LAYERS, 2, 4, CHUNK, D), BF16),
        v((D, FF), BF16),
        v((LAYERS, D, TILE), F32),
        v((LAYERS, D, TILE), F32),
        v((LAYERS, 8, TILE), F32),
        v((LAYERS, 8, TILE), F32),
        v((LAYERS, D, TILE), BF16),
        v((LAYERS, FF, TILE), F32),
        v((LAYERS, FF, TILE), BF16),
        v((LAYERS, TILE, 256), F32),
        v((LAYERS, TILE, 256), F32),
        v((LAYERS, TILE, 256), F32),
        v((2 * ROWS * NLAT, 256), F32),
        v((FF, TILE), BF16),
        v((2, FF, D), F32),
        v((FF, D), BF16),
        v((FF, D), BF16),
        v((NCH, FB, D), BF16),
        v((2, NCH, FB, D), BF16),
        v((NCH, CB, TILE), F32),
        v((NCH, CB, TILE), F32),
        v((FF, TILE), F32),
        v((NCH, 8, 256), F32),
        v((NCH, 8, 256), F32),
        v((CB, TILE), F32),
        v((D, TILE), F32),
        v((NCH, CB, TILE), F32),
        v((LAYERS, NCH, CB, TILE), F32),
        v((TILE, 256), F32),
        v((2, ROWS, SPAN, 256), BF16),
        v((2, ROWS, 256, SPAN), BF16),
        v((2, LAYERS, 2, TILE, 256), BF16),
        v((2, LAYERS, 2, TILE, 256), BF16),
        v((2, TILE, 2 * ROWS * NLAT), BF16),
        v((2, 2 * ROWS * NLAT, TILE), BF16),
        v((2, 2, ROWS, SPAN, TILE), BF16),
        v((2, 2, ROWS, TILE, SPAN), BF16),
        v((LAYERS, SHARES, WROWS, D), BF16),
        v((LAYERS, 8, WROWS, D), BF16),
        v((LAYERS, WROWS, D), BF16),
        v((NLAT, 32, TILE), F32),
        v((NLAT, 32, TILE), F32),
        v((32, TILE), F32),
        v((48, TILE), F32),
        v((NLAT, 48, TILE), F32),
        dma((8, NCH)),
        dma((8, NCH)),
        dma((LAYERS, NCH)),
        dma((LAYERS, NCH)),
        dma((LAYERS,)),
        dma((LAYERS,)),
        dma((LAYERS, NCH)),
        dma((LAYERS, NCH)),
        dma((LAYERS,)),
        dma((LAYERS,)),
        dma((2, NCH)),
        dma((2, NCH)),
        dma((2, NLAT)),
        dma((2, NLAT)),
        dma((2 + LAYERS,)),
        dma((LAYERS, 4)),
        dma((LAYERS, 4)),
        dma((LAYERS, NLAT)),
        dma((LAYERS, NLAT)),
        dma((LAYERS, NLAT)),
        dma((LAYERS, NLAT)),
        dma((4, NLAT)),
        dma((4, NLAT)),
    ]
    return pl.pallas_call(
        stack_kernel,
        out_shape=shapes,
        in_specs=[
            pl.BlockSpec(memory_space=pl.ANY if at in (3, 10, 11) else pltpu.VMEM)
            for at in range(len(args))
        ],
        out_specs=[pl.BlockSpec(memory_space=pltpu.VMEM)] * len(shapes),
        scratch_shapes=scratch,
        compiler_params=pltpu.CompilerParams(
            collective_id=0, has_side_effects=True, vmem_limit_bytes=60 << 20
        ),
        name="stack",
    )(*args)


def two_parts(table):
    high = table.astype(ml_dtypes.bfloat16)
    return np.stack([high, (table - high.astype(np.float64)).astype(ml_dtypes.bfloat16)])


def lat_all():
    lat_cells = ROWS * NLAT
    phase = np.outer(np.arange(lat_cells), np.arange(lat_cells)) % lat_cells
    angles = phase * (2.0 * math.pi / lat_cells)

    def place(table):
        return table.reshape(lat_cells, NLAT, ROWS).transpose(0, 2, 1).reshape(lat_cells, -1)

    cos, sin = place(np.cos(angles)), place(np.sin(angles))
    table = np.block([[cos, sin], [-sin, cos]]) / math.sqrt(lat_cells)
    table = np.pad(table, ((0, 2 * TILE - 2 * lat_cells), (0, 0)))
    return two_parts(table), two_parts(np.ascontiguousarray(table.T))


def lon_all():
    modes = LON // 2 + 1
    phase = np.outer(np.arange(modes), np.arange(LON)) % LON
    angles = phase * (2.0 * math.pi / LON)
    table = np.stack([np.cos(angles), -np.sin(angles)], axis=1).reshape(2 * modes, LON)
    table = table / math.sqrt(LON)
    rows = []
    for r in range(ROWS):
        before = r * LON - TILE_FROM[r] * TILE
        rows.append(
            np.pad(table, ((0, 2 * TILE - 2 * modes), (before, SPAN - LON - before)))
        )
    cells = np.stack(rows)
    return two_parts(np.ascontiguousarray(cells.transpose(0, 2, 1))), two_parts(cells)


def body(
    inputs,
    cotangent,
    first_gain,
    first_shift,
    filter_inner,
    filter_inner_bias,
    filter_outer,
    filter_outer_bias,
    second_gain,
    second_shift,
    up_weight,
    up_bias,
    down_weight,
    down_bias,
    kept_lat,
    kept_lon,
):
    shape = inputs.shape
    cells = ROWS * LON

    def to_tiles(field):
        flat = jnp.pad(field.reshape(CB, cells), ((0, 0), (0, NCH * TILE - cells)))
        return flat.reshape(CB, NCH, TILE).transpose(1, 0, 2)

    def from_tiles(tiles):
        return tiles.transpose(1, 0, 2).reshape(CB, NCH * TILE)[:, :cells].reshape(shape)

    vectors = jnp.stack([first_gain, first_shift, second_gain, second_shift, down_bias], axis=1)
    prm = jnp.concatenate(
        [
            jnp.pad(vectors, ((0, 0), (0, 0), (0, 256 - CB))),
            jnp.pad(up_bias[:, None, :], ((0, 0), (0, 2), (0, 256 - FB))),
        ],
        axis=1,
    ).reshape(32, 256)
    shards = jnp.stack([up_weight.transpose(0, 2, 1), down_weight], axis=1)
    biases = jnp.concatenate([filter_inner_bias[:, :, 0], filter_outer_bias[:, :, 0]], axis=1)
    biases = jnp.tile(jnp.pad(biases, ((0, 0), (0, 4), (0, CP - CB))), (1, 1, 2))
    lon_index = (kept_lon[:, None] * 2 + jnp.arange(2, dtype=jnp.int32)).reshape(1, TILE)
    lat_index = jnp.pad(kept_lat, (0, 64 - kept_lat.shape[0]), constant_values=-4 * LON)
    lat_index = (jnp.arange(2, dtype=jnp.int32)[:, None] * (ROWS * NLAT) + lat_index).reshape(1, TILE)
    index = jnp.concatenate([lon_index, lat_index, jnp.zeros((6, TILE), jnp.int32)], axis=0)
    all_a, all_t = lat_all()
    all_k, all_v = lon_all()
    out_h, out_g, wout, sout, sums = run_stack(
        to_tiles(inputs), to_tiles(cotangent), prm, shards,
        filter_inner.reshape(LAYERS, 2, CB, CB), filter_outer.reshape(LAYERS, 2, CB, CB),
        biases, index, all_a, all_t, all_k, all_v,
    )
    rows = sums[:32].reshape(LAYERS, 8, TILE)
    up_shift_grad = jnp.concatenate([sums[32:36], sums[40:44]], axis=1)[:, :FB]
    wout = wout.reshape(2, LAYERS, FB, D)
    sout = sout.reshape(LAYERS, 2, CP, TILE)
    both = jnp.stack([sout[..., :CB], sout[..., CP : CP + CB]], axis=1)
    filters = [both[:, :, at, :CB] for at in range(2)]
    fbias = [both[:, :, at, CB] for at in range(2)]
    plain, cross = rows[:, 0, :CB], rows[:, 1, :CB]
    return (
        from_tiles(out_h),
        from_tiles(out_g),
        (cross - first_shift * plain) / first_gain,
        plain,
        filters[0][:, :, None],
        fbias[0][:, :, None],
        filters[1][:, :, None],
        fbias[1][:, :, None],
        rows[:, 2, :CB],
        rows[:, 3, :CB],
        wout[0].transpose(0, 2, 1).astype(F32),
        up_shift_grad,
        wout[1].astype(F32),
        rows[:, 4, :CB],
    )


def solution(mesh):
    placed = (
        P("ch", "lat", None),
        P("ch", "lat", None),
        P(None, "ch"),
        P(None, "ch"),
        P(None, None, "ch", None, None),
        P(None, None, "ch", None),
        P(None, None, "ch", None, None),
        P(None, None, "ch", None),
        P(None, "ch"),
        P(None, "ch"),
        P(None, None, "ch"),
        P(None, "ch"),
        P(None, "ch", None),
        P(None, "ch"),
        P(),
        P(),
    )
    return jax.shard_map(
        body,
        mesh=mesh,
        in_specs=placed,
        out_specs=(
            P("ch", "lat", None),
            P("ch", "lat", None),
            P(None, "ch"),
            P(None, "ch"),
            P(None, None, "ch", None, None),
            P(None, None, "ch", None),
            P(None, None, "ch", None, None),
            P(None, None, "ch", None),
            P(None, "ch"),
            P(None, "ch"),
            P(None, None, "ch"),
            P(None, "ch"),
            P(None, "ch", None),
            P(None, "ch"),
        ),
        check_vma=False,
    )
```

```python
import functools
import math

import jax
import jax.numpy as jnp
import ml_dtypes
import numpy as np
from jax import lax
from jax.experimental import pallas as pl
from jax.experimental.pallas import tpu as pltpu
from jax.sharding import PartitionSpec as P

shrink_level = 0.01
norm_eps = 1e-05
highest = lax.Precision.HIGHEST
MESH = pl.DeviceIdType.MESH
F32 = jnp.float32
BF16 = jnp.bfloat16

LAYERS = 4
NCH = 8
NLAT = 16
CB = 48
CP = 64
D = NCH * CB
ROWS = 5
LON = 180
TILE = 128
FB = 192
FF = NCH * FB
CHUNK = 384
QB = FB // 4
WROWS = 32
SHARES = FB // WROWS
TILE_FROM = [r * LON // TILE for r in range(ROWS)]
TILE_TO = [-(-(r + 1) * LON // TILE) for r in range(ROWS)]
SPAN = max(b - a for a, b in zip(TILE_FROM, TILE_TO)) * TILE


def gelu_exact(values):
    return 0.5 * values * (1.0 + lax.erf(values * 0.7071067811865476))


def gelu_slope(values):
    return (
        0.5 * (1.0 + lax.erf(values * 0.7071067811865476))
        + values * jnp.exp(-0.5 * values * values) * 0.3989422804014327
    )


def mm(a, b, dims=((1,), (0,)), precision=highest):
    return lax.dot_general(a, b, (dims, ((), ())), precision=precision, preferred_element_type=F32)


def mb(a, b, dims=((1,), (0,))):
    return lax.dot_general(a, b, (dims, ((), ())), preferred_element_type=F32)


NT = ((1,), (1,))


def split(value):
    high = value.astype(BF16)
    return high, (value - high.astype(F32)).astype(BF16)


def rows_times(value, high, low):
    vh, vl = split(value)
    n = value.shape[0]
    both = mb(jnp.concatenate([vh, vl], axis=0), high)
    return both[:n] + both[n:] + mb(vh, low)


def table_times(high, low, value):
    vh, vl = split(value)
    n = value.shape[1]
    both = mb(high, jnp.concatenate([vh, vl], axis=1))
    return both[:, :n] + both[:, n:] + mb(low, vh)


def stack_kernel(
    x0, ct, prm, wsh, fi, fo, fb, idx, all_a, all_t, all_k, all_v,
    out_h, out_g, wout, sout, rout,
    h_s, g_s, xin, pbuf, pcol, bcol, mbuf, fbuf, sbuf, sbuf2, xbuf, zbuf, cbuf, bbuf,
    wall, wT, n1_s, n2_s, r1_s, r2_s, lifted_s, pre_s, hid_s, y_s, hh_s, t_s,
    xs, prs, gr, psend, pget, gsend, gget, pc, pin, bc, brow, bin_s, pr, ig_s, igr, mixr_s, bwf, k_s, v_s,
    bw, bt, la, lt, lk, lv,
    gw, wget, wsum, gf, fget, fsum, gpsum, gpget,
    bsem_s, bsem_r, asem_s, asem_r, psem_s, psem_r, gsem_s, gsem_r, qsem_s, qsem_r,
    c_s, c_r, l_s, l_r, t_sem, ysem_s, ysem_r, w1_s, w1_r, w2_s, w2_r, f_s, f_r,
):
    ch = lax.axis_index("ch")
    lat = lax.axis_index("lat")
    core = lax.rem(lat, 2)
    partner = lat + 1 - 2 * core


    def flipped(at):
        return at + 2 - 4 * lax.rem(at // 2, 2)

    flip = flipped(lat)
    half = lax.rem(ch, 2)
    rank = lat + half * (flip - lat)
    ch_peer = [lax.rem(ch + s, NCH) for s in range(NCH)]
    lat_peer = [lax.rem(lat + s, NLAT) for s in range(NLAT)]

    barrier = pltpu.get_barrier_semaphore()
    for s in range(1, NCH):
        pl.semaphore_signal(barrier, inc=1, device_id={"ch": ch_peer[s]}, device_id_type=MESH)
        pl.semaphore_signal(
            barrier, inc=1, device_id={"lat": flip, "ch": ch_peer[s]}, device_id_type=MESH
        )
    for s in range(1, NLAT):
        pl.semaphore_signal(barrier, inc=1, device_id={"lat": lat_peer[s]}, device_id_type=MESH)

    def remote(src, dst, send, recv, where):
        return pltpu.make_async_remote_copy(
            src_ref=src, dst_ref=dst, send_sem=send, recv_sem=recv,
            device_id=where, device_id_type=MESH,
        )

    def over_near(src, dst, send, recv):
        copies = []
        for s in range(1, NCH):
            where = {"lat": flip, "ch": ch_peer[s]} if s % 2 else {"ch": ch_peer[s]}
            copies.append(remote(src(ch_peer[s]), dst, send.at[s], recv.at[s], where))
        return copies

    def between(src, dst, at, inward):
        copies = []
        for s in range(NCH):
            there = lat + lax.rem(half + s, 2) * (flip - lat) if inward else rank
            where = {"lat": there, "ch": ch_peer[s]}
            copies.append(remote(src(ch_peer[s]), dst, bsem_s.at[at, s], bsem_r.at[at, s], where))
        return copies

    def between_start(src, dst, at, inward, keep):
        copies = between(src, dst, at, inward)
        for copy in copies[1:]:
            copy.start()

        @pl.when(half == 1)
        def _():
            copies[0].start()

        @pl.when(half == 0)
        def _():
            keep()

        return copies

    def between_done(copies):
        for copy in copies[1:]:
            copy.wait()

        @pl.when(half == 1)
        def _():
            copies[0].wait()

    def to_lat(src, dst, send, recv):
        return [
            remote(src(lat_peer[s]), dst, send.at[s], recv.at[s], {"lat": lat_peer[s]})
            for s in range(1, NLAT)
        ]

    def start(copies):
        for copy in copies:
            copy.start()
        return copies

    def arrived(copies):
        for copy in copies:
            copy.wait_recv()

    def sent(copies):
        for copy in copies:
            copy.wait_send()

    def done(copies):
        for copy in copies:
            copy.wait()

    quarter = lat // 4

    def weights_near(layer):
        source = wsh.at[layer, core, pl.ds(pl.multiple_of(quarter * QB, QB), QB)]
        mine = wall.at[layer, core, quarter, pl.ds(pl.multiple_of(ch * QB, QB), QB)]
        return over_near(lambda p: source, mine, asem_s.at[layer], asem_r.at[layer])

    def own_weights(layer):
        source = wsh.at[layer, core, pl.ds(pl.multiple_of(quarter * QB, QB), QB)]
        mine = wall.at[layer, core, quarter, pl.ds(pl.multiple_of(ch * QB, QB), QB)]
        return pltpu.make_async_copy(source, mine, t_sem.at[2 + layer])

    def weights_along(layer):
        block = wall.at[layer, core, quarter]
        return [
            remote(block, block, ysem_s.at[layer, s], ysem_r.at[layer, s], {"lat": lat_peer[4 * s]})
            for s in range(1, 4)
        ]

    def weights_pair(layer):
        block = wall.at[layer, core]
        return remote(block, block, psem_s.at[layer], psem_r.at[layer], {"lat": partner})

    def weights_start(layer):
        start(weights_near(layer))
        own_weights(layer).start()

    def weights_spread(layer):
        done(weights_near(layer))
        own_weights(layer).wait()
        start(weights_along(layer))

    def weights_pass(layer):
        done(weights_along(layer))
        weights_pair(layer).start()

    def weights_done(layer):
        weights_pair(layer).wait()

    get_k = pltpu.make_async_copy(all_k, k_s, t_sem.at[0])
    get_v = pltpu.make_async_copy(all_v, v_s, t_sem.at[1])
    get_k.start()
    get_v.start()
    pbuf[ch] = prm[...]
    pl.semaphore_wait(barrier, 2 * (NCH - 1) + NLAT - 1)

    def keep_x():
        xin[0, ch] = x0[ch]

    def keep_ct():
        xin[1, ch] = ct[ch]

    first = between_start(lambda p: x0.at[p], xin.at[0, ch], 0, True, keep_x)
    params = start(over_near(lambda p: prm, pbuf.at[ch], bsem_s.at[1], bsem_r.at[1]))
    weights_start(0)
    pc[...] = jnp.zeros(pc.shape, F32)
    bc[...] = jnp.zeros(bc.shape, F32)
    pr[...] = jnp.zeros(pr.shape, F32)
    bwf[...] = jnp.zeros(bwf.shape, F32)

    def picker(at):
        rows = lax.broadcasted_iota(jnp.int32, (2 * TILE, TILE), 0)
        return jnp.where(rows == idx[at : at + 1, :], 1.0, 0.0)

    def turn(pick):
        return jnp.concatenate([jnp.transpose(pick[:TILE]), jnp.transpose(pick[TILE:])], axis=1)

    ends = (idx[0:1, :] < 2) | (idx[0:1, :] >= 180)
    mode_weight = jnp.where(ends, 1.0, 2.0)

    def first_tables():
        get_k.wait()
        pick = picker(0).astype(BF16)
        for part in range(2):
            for r in range(ROWS):
                table = mb(k_s[part, r], pick)
                lk[part, 0, r] = table.astype(BF16)
                lk[part, 1, r] = (table * mode_weight).astype(BF16)

    def other_tables():
        get_v.wait()
        pick = picker(0)
        pick_t = jnp.concatenate([turn(pick), turn(pick * mode_weight)], axis=0).astype(BF16)
        for part in range(2):
            for r in range(ROWS):
                table = mb(pick_t, v_s[part, r]).astype(BF16)
                lv[part, 0, r] = table[:TILE]
                lv[part, 1, r] = table[TILE:]
        pick = picker(1)
        pick_t = turn(pick).astype(BF16)
        pick = pick.astype(BF16)
        for part in range(2):
            la[part] = mb(pick_t, all_a[part]).astype(BF16)
            lt[part] = mb(all_t[part], pick).astype(BF16)

    def columns(held, width, count):
        for j in range(NCH):
            turned = jnp.transpose(pbuf[j, :, :width])
            for layer in range(LAYERS):
                part = turned[:, layer * 8 : layer * 8 + 8]
                if count == CB:
                    held[layer, j * CB : (j + 1) * CB, 0:8] = part[:CB]
                else:
                    for y in range(4):
                        at = y * CHUNK + j * QB
                        held[layer, at : at + QB, 0:8] = part[y * QB : (y + 1) * QB]

    first_tables()
    done(params)
    columns(pcol, TILE, CB)
    between_done(first)
    h_s[...] = xin[0]

    lane = lax.broadcasted_iota(jnp.int32, (NLAT, TILE), 1)

    def filter_tables(layer):
        for at, weight in enumerate((fi, fo)):
            for part in range(2):
                for k in range(2):
                    lanes = part * TILE + k * CP
                    bwf[k * CP : k * CP + CB, lanes : lanes + CB] = weight[layer, part]
            table = bwf[...]
            bw[0, layer, at], bw[1, layer, at] = split(table)
            bt[0, layer, at], bt[1, layer, at] = split(
                jnp.concatenate(
                    [jnp.transpose(table[:, :TILE]), jnp.transpose(table[:, TILE:])], axis=1
                )
            )

    def swap(v):
        return pltpu.roll(v, CP, 1)

    def lon_to_modes(which):
        parts = []
        for r in range(ROWS):
            a, b = TILE_FROM[r], TILE_TO[r]
            field = jnp.concatenate([fbuf[t] for t in range(a, b)], axis=1)
            span = (b - a) * TILE
            parts.append(rows_times(field, lk[0, which, r, :span], lk[1, which, r, :span]))
        parts.append(jnp.zeros((2 * TILE - ROWS * CB, TILE), F32))
        both = jnp.concatenate(parts, axis=0)
        for t in range(2):
            turned = jnp.transpose(both[t * TILE : (t + 1) * TILE])
            sbuf[:, :, t * TILE : (t + 1) * TILE] = turned.reshape(NLAT, 8, TILE)

    def gather_lat():
        for ri in range(2):
            for kt in range(2):
                sides = []
                for side in range(2):
                    q = 4 * kt + 2 * side + ri
                    left, right = xbuf[:, q, :TILE], xbuf[:, q, TILE:]
                    middle = jnp.where(lane >= 2 * CB, left, right)
                    sides.append([left, left, middle, right, right])
                for r in range(ROWS):
                    a = pltpu.roll(sides[0][r], (-r * CB) % TILE, 1) if r else sides[0][r]
                    b = pltpu.roll(sides[1][r], (CP - r * CB) % TILE, 1)
                    at = ri * ROWS * NLAT + r * NLAT
                    xs[at : at + NLAT, kt * TILE : (kt + 1) * TILE] = jnp.where(lane < CP, a, b)

    def scatter_lat(z):
        for ri in range(2):
            for k in range(4):
                lanes = slice(k // 2 * TILE, (k // 2 + 1) * TILE)
                p = []
                for r in range(ROWS):
                    at = ri * ROWS * NLAT + r * NLAT
                    piece = z[at : at + NLAT, lanes]
                    move = (r * CB - k % 2 * CP) % TILE
                    p.append(pltpu.roll(piece, move, 1) if move else piece)
                left = jnp.where(lane < CB, p[0], jnp.where(lane < 2 * CB, p[1], p[2]))
                right = jnp.where(lane < 16, p[2], jnp.where(lane < 64, p[3], p[4]))
                sbuf2[:, 2 * k + ri, :TILE] = left
                sbuf2[:, 2 * k + ri, TILE:] = jnp.where(lane < 112, right, 0.0)

    def lon_to_cells(which):
        both = jnp.concatenate(
            [
                jnp.transpose(zbuf[:, :, t * TILE : (t + 1) * TILE].reshape(TILE, TILE))
                for t in range(2)
            ],
            axis=0,
        )
        tiles = [None] * NCH
        for r in range(ROWS):
            a, b = TILE_FROM[r], TILE_TO[r]
            span = (b - a) * TILE
            rows = both[r * CB : (r + 1) * CB]
            part = rows_times(rows, lv[0, which, r, :, :span], lv[1, which, r, :, :span])
            for t in range(a, b):
                piece = part[:, (t - a) * TILE : (t - a + 1) * TILE]
                tiles[t] = piece if tiles[t] is None else tiles[t] + piece
        for t in range(NCH):
            cbuf[t] = tiles[t]

    def mix(v, table, layer, at, sign):
        out = []
        for t in range(2):
            q = rows_times(v[:, t * TILE : (t + 1) * TILE], table[0, layer, at], table[1, layer, at])
            re = q[:64, :TILE] - sign * q[64:, TILE:]
            im = q[64:, :TILE] + sign * q[:64, TILE:]
            out.append(jnp.concatenate([re, im], axis=0))
        return jnp.concatenate(out, axis=1)

    def bias_rows(layer, at):
        rows = [jnp.broadcast_to(fb[layer, at + ri : at + ri + 1, :], (64, TILE)) for ri in range(2)]
        both = jnp.concatenate(rows, axis=0)
        return jnp.concatenate([both, both], axis=1)

    def exchange_one(value):
        mbuf[...] = value.reshape(NCH, CB, TILE)
        copies = start(over_near(lambda p: mbuf.at[p], fbuf.at[ch], c_s.at[0], c_r.at[0]))
        fbuf[ch] = mbuf[ch]
        return copies

    def exchange_four():
        copies = start(over_near(lambda p: cbuf.at[p], bbuf.at[ch], c_s.at[1], c_r.at[1]))
        bbuf[ch] = cbuf[ch]
        return copies

    def exchange_lat(src, dst, at):
        copies = []
        for s in range(1, NLAT):
            peer = lax.rem(rank + s, NLAT)
            there = peer + half * (flipped(peer) - peer)
            copies.append(
                remote(src.at[peer], dst.at[rank], l_s.at[at, s], l_r.at[at, s], {"lat": there})
            )
        start(copies)
        dst[rank] = src[rank]
        return copies

    def col(layer, at):
        return pcol[layer, :, at : at + 1]

    def forward(layer, carry):
        h = h_s[...].reshape(D, TILE)
        mean = jnp.sum(h, axis=0, keepdims=True) * (1.0 / D)
        spread = jnp.sum(h * h, axis=0, keepdims=True) * (1.0 / D) - mean * mean
        rstd = lax.rsqrt(spread + norm_eps)
        n1 = (h - mean) * rstd
        n1_s[layer] = n1
        r1_s[layer] = jnp.broadcast_to(rstd, (8, TILE))
        mixed = n1 * col(layer, 0) + col(layer, 1)
        one = exchange_one(mixed)
        ig_s[...] = h + mixed

        @pl.when(layer == 0)
        def _():
            weights_spread(0)
            other_tables()

        filter_tables(layer)
        arrived(one)

        @pl.when(layer < LAYERS - 1)
        def _():
            weights_start(layer + 1)

        lon_to_modes(0)
        two = exchange_lat(sbuf, xbuf, 0)
        weights_pass(layer)
        sent(one)
        mixr_s[layer] = fbuf[...]

        @pl.when(layer == 0)
        def _():
            columns(bcol, 256, FB)

        arrived(two)
        gather_lat()
        y = table_times(la[0], la[1], xs[...])
        y_s[layer] = y
        hh = mix(y, bw, layer, 0, 1.0) + bias_rows(layer, 0)
        hh_s[layer] = hh
        b = mix(gelu_exact(hh), bw, layer, 1, 1.0) + bias_rows(layer, 2)
        t = jnp.tanh(b / shrink_level)
        t_s[layer] = t
        scatter_lat(table_times(lt[0], lt[1], b - shrink_level * t))
        three = exchange_lat(sbuf2, zbuf, 1)
        sent(two)

        @pl.when(layer == 1)
        def _():
            between_start(lambda p: ct.at[p], xin.at[1, ch], 2, True, keep_ct)

        arrived(three)
        lon_to_cells(1)
        four = exchange_four()
        sent(three)

        @pl.when(layer < LAYERS - 1)
        def _():
            weights_spread(layer + 1)

        weights_done(layer)
        for at in range(0, FF, CHUNK):
            wT[:, at : at + CHUNK] = jnp.transpose(wall[layer, 1, at // CHUNK])
        arrived(four)
        inner = ig_s[...] + bbuf[...].reshape(D, TILE)
        mean = jnp.sum(inner, axis=0, keepdims=True) * (1.0 / D)
        spread = jnp.sum(inner * inner, axis=0, keepdims=True) * (1.0 / D) - mean * mean
        rstd = lax.rsqrt(spread + norm_eps)
        n2 = (inner - mean) * rstd
        n2_s[layer] = n2
        r2_s[layer] = jnp.broadcast_to(rstd, (8, TILE))
        lifted = (n2 * col(layer, 2) + col(layer, 3)).astype(BF16)
        lifted_s[layer] = lifted
        total = inner + col(layer, 4)
        for at in range(0, FF, CHUNK):
            pre = mb(wall[layer, 0, at // CHUNK], lifted) + bcol[layer, at : at + CHUNK, 5:6]
            pre_s[layer, at : at + CHUNK] = pre
            hidden = gelu_exact(pre).astype(BF16)
            hid_s[layer, at : at + CHUNK] = hidden
            total = total + mb(wT[:, at : at + CHUNK], hidden)
        h_s[...] = total.reshape(NCH, CB, TILE)
        sent(four)
        return carry

    lax.fori_loop(0, LAYERS, forward, 0)

    def keep_h():
        out_h[ch] = h_s[ch]

    def keep_g():
        out_g[ch] = g_s[ch]

    last_h = between_start(lambda p: h_s.at[p], out_h.at[ch], 3, False, keep_h)
    between_done(between(lambda p: ct.at[p], xin.at[1, ch], 2, True))
    g_s[...] = xin[1]
    ones = jnp.ones((8, TILE), F32)

    def turn_up(layer):
        for at in range(0, FF, CHUNK):
            wT[:, at : at + CHUNK] = jnp.transpose(wall[layer, 0, at // CHUNK])

    turn_up(LAYERS - 1)

    lanes_d = lax.broadcasted_iota(jnp.int32, (D, TILE), 1)
    lanes_f = lax.broadcasted_iota(jnp.int32, (CHUNK, TILE), 1)

    def cell_sums(layer, at, value):
        total = jnp.sum(value, axis=1, keepdims=True)
        held = pc[...].reshape(D, TILE)
        held = jnp.where(lanes_d == layer * 8 + at, total, held)
        pc[...] = held.reshape(NCH, CB, TILE)

    def hidden_sums(layer):
        for at in range(0, FF, CHUNK):
            total = jnp.sum(pre_s[layer, at : at + CHUNK], axis=1, keepdims=True)
            held = bc[at : at + CHUNK]
            bc[at : at + CHUNK] = jnp.where(lanes_f == layer, total, held)

    def turn_hidden_sums():
        blank = jnp.zeros((2 * TILE - FB, TILE), F32)
        for j in range(NCH):
            pieces = [bc[y * CHUNK + j * QB : y * CHUNK + (j + 1) * QB] for y in range(4)]
            tall = jnp.concatenate(pieces + [blank], axis=0)
            for t in range(2):
                turned = jnp.transpose(tall[t * TILE : (t + 1) * TILE])
                brow[j, :, t * TILE : (t + 1) * TILE] = turned[:8]

    def grads_pair(layer):
        return remote(
            psend, pget, qsem_s.at[layer], qsem_r.at[layer], {"lat": partner}
        )

    def grads_near(layer):
        return over_near(
            lambda p: gsend.at[p], gget.at[lax.rem(layer, 2), ch], gsem_s.at[layer], gsem_r.at[layer]
        )

    def grads_done(layer):
        slot = lax.rem(layer, 2)
        gget[slot, ch] = gsend[ch]
        done(grads_near(layer))
        total = gget[slot, 0].astype(F32)
        for j in range(1, NCH):
            total = total + gget[slot, j].astype(F32)
        gw[layer] = total.astype(BF16).reshape(SHARES, WROWS, D)

    near = lat // 2
    evens = range(2, NLAT, 2)

    def sum_share(layer):
        for s in evens:
            there = lat_peer[s] // 2

            @pl.when(there < SHARES)
            def _():
                share_copy(layer, s).start()

    def share_copy(layer, s):
        return remote(
            gw.at[layer, lat_peer[s] // 2], wget.at[layer, near],
            w1_s.at[layer, s], w1_r.at[layer, s], {"lat": lat_peer[s]},
        )

    def arriving(layer, s):
        return remote(
            wget.at[layer, near], wget.at[layer, near],
            w1_s.at[layer, s], w1_r.at[layer, s], {"lat": lat_peer[s]},
        )

    def give_copy(layer, s):
        return remote(
            wsum.at[layer], wout.at[core, layer, near],
            w2_s.at[layer, s], w2_r.at[layer, s], {"lat": lat_peer[s]},
        )

    def given(layer, s):
        return remote(
            wsum.at[layer], wsum.at[layer],
            w2_s.at[layer, s], w2_r.at[layer, s], {"lat": lat_peer[s]},
        )

    def sum_pass(layer):
        for s in evens:

            @pl.when(lat_peer[s] // 2 < SHARES)
            def _():
                share_copy(layer, s).wait_send()

        @pl.when(near < SHARES)
        def _():
            wget[layer, near] = gw[layer, near]
            for s in evens:
                arriving(layer, s).wait_recv()
            total = wget[layer, 0].astype(F32)
            for j in range(1, 8):
                total = total + wget[layer, j].astype(F32)
            wsum[layer] = total.astype(BF16)
            for s in evens:
                give_copy(layer, s).start()
            wout[core, layer, near] = wsum[layer]

    def hand_copy(layer):
        whole = wout.at[core, layer]
        return remote(whole, whole, w2_s.at[layer, 0], w2_r.at[layer, 0], {"lat": partner})

    def sum_hand(layer):
        @pl.when(near < SHARES)
        def _():
            for s in evens:
                give_copy(layer, s).wait_send()

        for s in evens:

            @pl.when(lax.rem(near + 8 - s // 2, 8) < SHARES)
            def _():
                given(layer, s).wait_recv()

        hand_copy(layer).start()

    def filters_share():
        return to_lat(lambda p: gf.at[p], fget.at[lat], f_s.at[0], f_r.at[0])

    def filters_give():
        return to_lat(lambda p: fsum, sout.at[lat], f_s.at[1], f_r.at[1])

    def rows_share():
        copies = []
        for s in range(1, NCH):
            p = ch_peer[s]
            where = {"lat": flip, "ch": p} if s % 2 else {"ch": p}
            copies.append(remote(pc.at[p], pin.at[ch], bsem_s.at[5, s], bsem_r.at[5, s], where))
            copies.append(
                remote(brow.at[p], bin_s.at[ch], bsem_s.at[7, s], bsem_r.at[7, s], where)
            )
        return copies

    def rows_give():
        return to_lat(lambda p: gpsum, gpget.at[lat], f_s.at[2], f_r.at[2])

    def rows_pass():
        pin[ch] = pc[ch]
        bin_s[ch] = brow[ch]
        done(rows_share())
        total, hidden = pin[0] + pr[...], bin_s[0]
        for j in range(1, NCH):
            total, hidden = total + pin[j], hidden + bin_s[j]
        tall = jnp.concatenate([total, jnp.zeros((TILE - CB, TILE), F32)], axis=0)
        gpsum[:32] = jnp.transpose(tall)[:32]
        gpsum[32:40] = hidden[:, :TILE]
        gpsum[40:48] = hidden[:, TILE:]
        gpget[lat] = gpsum[...]
        start(rows_give())

    def backward(step, carry):
        layer = LAYERS - 1 - step
        g = g_s[...].reshape(D, TILE)
        g_round = g.astype(BF16)
        lift = jnp.zeros((D, TILE), F32)
        for at in range(0, FF, CHUNK):
            hidden_grad = mb(wall[layer, 1, at // CHUNK], g_round)
            pre_grad = hidden_grad * gelu_slope(pre_s[layer, at : at + CHUNK])
            pre_s[layer, at : at + CHUNK] = pre_grad
            pre_round = pre_grad.astype(BF16)
            prs[at : at + CHUNK] = pre_round
            lift = lift + mb(wT[:, at : at + CHUNK], pre_round)
        n2 = n2_s[layer]
        q2 = lift * col(layer, 2)
        m1 = jnp.sum(q2, axis=0, keepdims=True) * (1.0 / D)
        m2 = jnp.sum(q2 * n2, axis=0, keepdims=True) * (1.0 / D)
        inner_grad = g + r2_s[layer, 0:1, :] * (q2 - m1 - n2 * m2)
        one = exchange_one(inner_grad)
        ig_s[...] = inner_grad
        lifted = lifted_s[layer]
        for at in range(0, FF, CHUNK):
            gr[1, at : at + CHUNK] = mb(hid_s[layer, at : at + CHUNK], g_round, NT)
            gr[0, at : at + CHUNK] = mb(prs[at : at + CHUNK], lifted, NT)
        psend[...] = gr[1 - core].astype(BF16)
        grads_pair(layer).start()
        cell_sums(layer, 4, g)
        cell_sums(layer, 2, lift * n2)
        cell_sums(layer, 3, lift)
        arrived(one)
        lon_to_modes(1)
        two = exchange_lat(sbuf, xbuf, 0)
        sent(one)
        igr[...] = fbuf[...]

        @pl.when(layer < LAYERS - 1)
        def _():
            grads_done(layer + 1)
            sum_share(layer + 1)

        @pl.when(layer < LAYERS - 2)
        def _():
            sum_hand(layer + 2)

        grads_pair(layer).wait()
        for y in range(4):
            cut = slice(y * CHUNK, (y + 1) * CHUNK)
            part = (gr[core, cut] + pget[cut].astype(F32)).astype(BF16)
            for j in range(NCH):
                gsend[j, y * QB : (y + 1) * QB] = part[j * QB : (j + 1) * QB]
        start(grads_near(layer))
        hidden_sums(layer)
        arrived(two)
        gather_lat()
        t = t_s[layer]
        db = table_times(la[0], la[1], xs[...]) * (t * t)
        hh = hh_s[layer]
        dh = mix(db, bt, layer, 1, -1.0) * gelu_slope(hh)
        dy = mix(dh, bt, layer, 0, -1.0)
        scatter_lat(table_times(lt[0], lt[1], dy))
        three = exchange_lat(sbuf2, zbuf, 1)
        sent(two)

        def filter_grads(at, left, right):
            turned = jnp.concatenate([right[64:], -right[:64]], axis=0)
            total = jnp.zeros((TILE, 2 * TILE), F32)
            for tt in range(2):
                lanes = slice(tt * TILE, (tt + 1) * TILE)
                pair = jnp.concatenate([right[:, lanes], turned[:, lanes]], axis=1)
                total = total + mm(jnp.transpose(left[:, lanes]), pair)
            re = total[:64, :TILE] + swap(total[64:, :TILE])
            im = total[:64, TILE:] + swap(total[64:, TILE:])
            keep = lax.broadcasted_iota(jnp.int32, (64, TILE), 1) < CP
            value = jnp.where(keep, re, swap(im))
            base = (layer * 2 + at) * 2
            gf[base] = value[:32]
            gf[base + 1] = value[32:]
            sums = []
            for part in (right[:64], right[64:]):
                row = jnp.sum(part, axis=0, keepdims=True)
                row = row[:, :TILE] + row[:, TILE:]
                sums.append(row + swap(row))
            gf[base + 1, 16:17, :] = jnp.where(keep[:1], sums[0], sums[1])

        filter_grads(1, gelu_exact(hh), db)
        filter_grads(0, y_s[layer], dh)

        @pl.when(layer > 0)
        def _():
            turn_up(layer - 1)

        @pl.when(layer == 0)
        def _():
            start(filters_share())
            turn_hidden_sums()
            start(rows_share())

        arrived(three)
        lon_to_cells(0)
        four = exchange_four()
        sent(three)
        both = igr[...] + cbuf[...]
        plain = jnp.sum(jnp.sum(both, axis=0), axis=1, keepdims=True)
        cross = jnp.sum(jnp.sum(both * mixr_s[layer], axis=0), axis=1, keepdims=True)
        lanes_c = lax.broadcasted_iota(jnp.int32, (CB, TILE), 1) - layer * 8
        pr[...] = jnp.where(lanes_c == 0, plain, jnp.where(lanes_c == 1, cross, pr[...]))

        @pl.when(layer < LAYERS - 1)
        def _():
            sum_pass(layer + 1)

        @pl.when(layer == 0)
        def _():
            fget[lat] = gf[lat]
            done(filters_share())
            total = fget[0]
            for j in range(1, NLAT):
                total = total + fget[j]
            fsum[...] = total
            sout[lat] = total
            start(filters_give())
            rows_pass()
            grads_done(0)
            sum_share(0)

        arrived(four)
        inner_grad = ig_s[...]
        mixed_grad = inner_grad + bbuf[...].reshape(D, TILE)
        n1 = n1_s[layer]
        q1 = mixed_grad * col(layer, 0)
        m1 = jnp.sum(q1, axis=0, keepdims=True) * (1.0 / D)
        m2 = jnp.sum(q1 * n1, axis=0, keepdims=True) * (1.0 / D)
        g = inner_grad + r1_s[layer, 0:1, :] * (q1 - m1 - n1 * m2)
        g_s[...] = g.reshape(NCH, CB, TILE)
        sent(four)
        return carry

    lax.fori_loop(0, LAYERS, backward, 0)
    final = between_start(lambda p: g_s.at[p], out_g.at[ch], 4, False, keep_g)
    sum_hand(1)
    sum_pass(0)
    sum_hand(0)
    between_done(last_h)
    between_done(final)
    done(filters_give())
    for layer in range(LAYERS):
        hand_copy(layer).wait()
    done(rows_give())
    total = gpget[0]
    for j in range(1, NLAT):
        total = total + gpget[j]
    rout[...] = total


def run_stack(*args):
    shapes = [
        jax.ShapeDtypeStruct((NCH, CB, TILE), F32),
        jax.ShapeDtypeStruct((NCH, CB, TILE), F32),
        jax.ShapeDtypeStruct((2, LAYERS, SHARES, WROWS, D), BF16),
        jax.ShapeDtypeStruct((NLAT, 32, TILE), F32),
        jax.ShapeDtypeStruct((48, TILE), F32),
    ]
    v = pltpu.VMEM
    dma = pltpu.SemaphoreType.DMA
    scratch = [
        v((NCH, CB, TILE), F32),
        v((NCH, CB, TILE), F32),
        v((2, NCH, CB, TILE), F32),
        v((NCH, 32, 256), F32),
        v((LAYERS, D, TILE), F32),
        v((LAYERS, FF, TILE), F32),
        v((NCH, CB, TILE), F32),
        v((NCH, CB, TILE), F32),
        v((NLAT, 8, 2 * TILE), F32),
        v((NLAT, 8, 2 * TILE), F32),
        v((NLAT, 8, 2 * TILE), F32),
        v((NLAT, 8, 2 * TILE), F32),
        v((NCH, CB, TILE), F32),
        v((NCH, CB, TILE), F32),
        v((LAYERS, 2, 4, CHUNK, D), BF16),
        v((D, FF), BF16),
        v((LAYERS, D, TILE), F32),
        v((LAYERS, D, TILE), F32),
        v((LAYERS, 8, TILE), F32),
        v((LAYERS, 8, TILE), F32),
        v((LAYERS, D, TILE), BF16),
        v((LAYERS, FF, TILE), F32),
        v((LAYERS, FF, TILE), BF16),
        v((LAYERS, TILE, 256), F32),
        v((LAYERS, TILE, 256), F32),
        v((LAYERS, TILE, 256), F32),
        v((2 * ROWS * NLAT, 256), F32),
        v((FF, TILE), BF16),
        v((2, FF, D), F32),
        v((FF, D), BF16),
        v((FF, D), BF16),
        v((NCH, FB, D), BF16),
        v((2, NCH, FB, D), BF16),
        v((NCH, CB, TILE), F32),
        v((NCH, CB, TILE), F32),
        v((FF, TILE), F32),
        v((NCH, 8, 256), F32),
        v((NCH, 8, 256), F32),
        v((CB, TILE), F32),
        v((D, TILE), F32),
        v((NCH, CB, TILE), F32),
        v((LAYERS, NCH, CB, TILE), F32),
        v((TILE, 256), F32),
        v((2, ROWS, SPAN, 256), BF16),
        v((2, ROWS, 256, SPAN), BF16),
        v((2, LAYERS, 2, TILE, 256), BF16),
        v((2, LAYERS, 2, TILE, 256), BF16),
        v((2, TILE, 2 * ROWS * NLAT), BF16),
        v((2, 2 * ROWS * NLAT, TILE), BF16),
        v((2, 2, ROWS, SPAN, TILE), BF16),
        v((2, 2, ROWS, TILE, SPAN), BF16),
        v((LAYERS, SHARES, WROWS, D), BF16),
        v((LAYERS, 8, WROWS, D), BF16),
        v((LAYERS, WROWS, D), BF16),
        v((NLAT, 32, TILE), F32),
        v((NLAT, 32, TILE), F32),
        v((32, TILE), F32),
        v((48, TILE), F32),
        v((NLAT, 48, TILE), F32),
        dma((8, NCH)),
        dma((8, NCH)),
        dma((LAYERS, NCH)),
        dma((LAYERS, NCH)),
        dma((LAYERS,)),
        dma((LAYERS,)),
        dma((LAYERS, NCH)),
        dma((LAYERS, NCH)),
        dma((LAYERS,)),
        dma((LAYERS,)),
        dma((2, NCH)),
        dma((2, NCH)),
        dma((2, NLAT)),
        dma((2, NLAT)),
        dma((2 + LAYERS,)),
        dma((LAYERS, 4)),
        dma((LAYERS, 4)),
        dma((LAYERS, NLAT)),
        dma((LAYERS, NLAT)),
        dma((LAYERS, NLAT)),
        dma((LAYERS, NLAT)),
        dma((4, NLAT)),
        dma((4, NLAT)),
    ]
    return pl.pallas_call(
        stack_kernel,
        out_shape=shapes,
        in_specs=[
            pl.BlockSpec(memory_space=pl.ANY if at in (3, 10, 11) else pltpu.VMEM)
            for at in range(len(args))
        ],
        out_specs=[pl.BlockSpec(memory_space=pltpu.VMEM)] * len(shapes),
        scratch_shapes=scratch,
        compiler_params=pltpu.CompilerParams(
            collective_id=0, has_side_effects=True, vmem_limit_bytes=60 << 20
        ),
        name="stack",
    )(*args)


def two_parts(table):
    high = table.astype(ml_dtypes.bfloat16)
    return np.stack([high, (table - high.astype(np.float64)).astype(ml_dtypes.bfloat16)])


def lat_all():
    lat_cells = ROWS * NLAT
    phase = np.outer(np.arange(lat_cells), np.arange(lat_cells)) % lat_cells
    angles = phase * (2.0 * math.pi / lat_cells)

    def place(table):
        return table.reshape(lat_cells, NLAT, ROWS).transpose(0, 2, 1).reshape(lat_cells, -1)

    cos, sin = place(np.cos(angles)), place(np.sin(angles))
    table = np.block([[cos, sin], [-sin, cos]]) / math.sqrt(lat_cells)
    table = np.pad(table, ((0, 2 * TILE - 2 * lat_cells), (0, 0)))
    return two_parts(table), two_parts(np.ascontiguousarray(table.T))


def lon_all():
    modes = LON // 2 + 1
    phase = np.outer(np.arange(modes), np.arange(LON)) % LON
    angles = phase * (2.0 * math.pi / LON)
    table = np.stack([np.cos(angles), -np.sin(angles)], axis=1).reshape(2 * modes, LON)
    table = table / math.sqrt(LON)
    rows = []
    for r in range(ROWS):
        before = r * LON - TILE_FROM[r] * TILE
        rows.append(
            np.pad(table, ((0, 2 * TILE - 2 * modes), (before, SPAN - LON - before)))
        )
    cells = np.stack(rows)
    return two_parts(np.ascontiguousarray(cells.transpose(0, 2, 1))), two_parts(cells)


def body(
    inputs,
    cotangent,
    first_gain,
    first_shift,
    filter_inner,
    filter_inner_bias,
    filter_outer,
    filter_outer_bias,
    second_gain,
    second_shift,
    up_weight,
    up_bias,
    down_weight,
    down_bias,
    kept_lat,
    kept_lon,
):
    shape = inputs.shape
    cells = ROWS * LON

    def to_tiles(field):
        flat = jnp.pad(field.reshape(CB, cells), ((0, 0), (0, NCH * TILE - cells)))
        return flat.reshape(CB, NCH, TILE).transpose(1, 0, 2)

    def from_tiles(tiles):
        return tiles.transpose(1, 0, 2).reshape(CB, NCH * TILE)[:, :cells].reshape(shape)

    vectors = jnp.stack([first_gain, first_shift, second_gain, second_shift, down_bias], axis=1)
    prm = jnp.concatenate(
        [
            jnp.pad(vectors, ((0, 0), (0, 0), (0, 256 - CB))),
            jnp.pad(up_bias[:, None, :], ((0, 0), (0, 2), (0, 256 - FB))),
        ],
        axis=1,
    ).reshape(32, 256)
    shards = jnp.stack([up_weight.transpose(0, 2, 1), down_weight], axis=1)
    biases = jnp.concatenate([filter_inner_bias[:, :, 0], filter_outer_bias[:, :, 0]], axis=1)
    biases = jnp.tile(jnp.pad(biases, ((0, 0), (0, 4), (0, CP - CB))), (1, 1, 2))
    lon_index = (kept_lon[:, None] * 2 + jnp.arange(2, dtype=jnp.int32)).reshape(1, TILE)
    lat_index = jnp.pad(kept_lat, (0, 64 - kept_lat.shape[0]), constant_values=-4 * LON)
    lat_index = (jnp.arange(2, dtype=jnp.int32)[:, None] * (ROWS * NLAT) + lat_index).reshape(1, TILE)
    index = jnp.concatenate([lon_index, lat_index, jnp.zeros((6, TILE), jnp.int32)], axis=0)
    all_a, all_t = lat_all()
    all_k, all_v = lon_all()
    out_h, out_g, wout, sout, sums = run_stack(
        to_tiles(inputs), to_tiles(cotangent), prm, shards,
        filter_inner.reshape(LAYERS, 2, CB, CB), filter_outer.reshape(LAYERS, 2, CB, CB),
        biases, index, all_a, all_t, all_k, all_v,
    )
    rows = sums[:32].reshape(LAYERS, 8, TILE)
    up_shift_grad = jnp.concatenate([sums[32:36], sums[40:44]], axis=1)[:, :FB]
    wout = wout.reshape(2, LAYERS, FB, D)
    sout = sout.reshape(LAYERS, 2, CP, TILE)
    both = jnp.stack([sout[..., :CB], sout[..., CP : CP + CB]], axis=1)
    filters = [both[:, :, at, :CB] for at in range(2)]
    fbias = [both[:, :, at, CB] for at in range(2)]
    plain, cross = rows[:, 0, :CB], rows[:, 1, :CB]
    return (
        from_tiles(out_h),
        from_tiles(out_g),
        (cross - first_shift * plain) / first_gain,
        plain,
        filters[0][:, :, None],
        fbias[0][:, :, None],
        filters[1][:, :, None],
        fbias[1][:, :, None],
        rows[:, 2, :CB],
        rows[:, 3, :CB],
        wout[0].transpose(0, 2, 1).astype(F32),
        up_shift_grad,
        wout[1].astype(F32),
        rows[:, 4, :CB],
    )


def solution(mesh):
    placed = (
        P("ch", "lat", None),
        P("ch", "lat", None),
        P(None, "ch"),
        P(None, "ch"),
        P(None, None, "ch", None, None),
        P(None, None, "ch", None),
        P(None, None, "ch", None, None),
        P(None, None, "ch", None),
        P(None, "ch"),
        P(None, "ch"),
        P(None, None, "ch"),
        P(None, "ch"),
        P(None, "ch", None),
        P(None, "ch"),
        P(),
        P(),
    )
    return jax.shard_map(
        body,
        mesh=mesh,
        in_specs=placed,
        out_specs=(
            P("ch", "lat", None),
            P("ch", "lat", None),
            P(None, "ch"),
            P(None, "ch"),
            P(None, None, "ch", None, None),
            P(None, None, "ch", None),
            P(None, None, "ch", None, None),
            P(None, None, "ch", None),
            P(None, "ch"),
            P(None, "ch"),
            P(None, None, "ch"),
            P(None, "ch"),
            P(None, "ch", None),
            P(None, "ch"),
        ),
        check_vma=False,
    )
```
